32 devices in a mesh: dp: 16 (over z, x, core), mem: 2 (over y).
Axes of the slice: x: 2, y: 2, z: 4, core: 2. Of those that a mesh axis runs over, the one named last changes fastest.
Arguments:
- target_in: bfloat16 [16384, 1024], P(('dp', 'mem')), may hold values from -6 to 6
- memory_in: bfloat16 [16, 2, 2, 2, 384, 1024], P('dp', None, 'mem'), may hold values from -6 to 6
- bucket_ids: int32 [16, 2], P('dp'), may hold values from 0 to 1, as said below
- target_lengths: int32 [16, 2, 2], P('dp', 'mem'), may hold values from 0 to 512, as said below
- memory_mask: int32 [16, 2, 2, 2, 384], P('dp', None, 'mem'), may hold values from 0 to 1, as said below
- self_qkv: float32 [1024, 3072], P(('dp', 'mem')), may hold values from -0.1875 to 0.1875
- self_out: float32 [1024, 1024], P(('dp', 'mem')), may hold values from -4 to 4
- cross_q: float32 [1024, 1024], P(('dp', 'mem')), may hold values from -0.1875 to 0.1875
- cross_kv: float32 [1024, 2048], P(('dp', 'mem')), may hold values from -0.1875 to 0.1875
- cross_out: float32 [1024, 1024], P(('dp', 'mem')), may hold values from -4 to 4
- ffn_in: float32 [1024, 4096], P(('dp', 'mem')), may hold values from -0.1875 to 0.1875
- ffn_out: float32 [4096, 1024], P(('dp', 'mem')), may hold values from -0.5 to 0.5
- norm_gains: float32 [1024, 3], P(('dp', 'mem')), may hold values from 0.5 to 1.5
- norm_biases: float32 [1024, 3], P(('dp', 'mem')), may hold values from -1.8 to 1.8
- grad_out: bfloat16 [16384, 1024], P(('dp', 'mem')), may hold values from -6 to 6
Outputs:
- layer_out: bfloat16 [16384, 1024], P(('dp', 'mem'))
- target_grad: bfloat16 [16384, 1024], P(('dp', 'mem'))
- memory_grad: bfloat16 [16, 2, 2, 2, 384, 1024], P('dp', None, 'mem')
- self_qkv_grad: float32 [1024, 3072], P(('dp', 'mem'))
- self_out_grad: float32 [1024, 1024], P(('dp', 'mem'))
- cross_q_grad: float32 [1024, 1024], P(('dp', 'mem'))
- cross_kv_grad: float32 [1024, 2048], P(('dp', 'mem'))
- cross_out_grad: float32 [1024, 1024], P(('dp', 'mem'))
- ffn_in_grad: float32 [1024, 4096], P(('dp', 'mem'))
- ffn_out_grad: float32 [4096, 1024], P(('dp', 'mem'))
- norm_gains_grad: float32 [1024, 3], P(('dp', 'mem'))
- norm_biases_grad: float32 [1024, 3], P(('dp', 'mem'))
The draws below stay inside these ranges and needn't reach their ends.
Inputs may be any that keep to these rules, and one draw needn't show every extreme that they name: `bucket_ids`: slots of a device hold 512 / 2^bucket rows each, and 2^bucket slots are used; the first device has bucket 0. `target_lengths`: A used slot's length lies above half its slot length and at most at it; slot 0 of every device is full; entries past the device's used slots are 0. `memory_mask`: for a used slot, 1 on a prefix of the sequence's 768 memory positions (position = piece * 384 + row) that reaches into its last piece, 0 after it; 0 everywhere in unused slots.
All inputs are finite; a program needn't handle non-finite values.
Results may differ from the reference program's by a relative error of at most 0.03.
Values may be sent and summed in bfloat16 or wider, within the bound.
No kernel may reach another device: no remote copies, remote signals or barrier semaphores. Data moves between devices by JAX's collectives and lax.ppermute only.
A program may use at most 320 MiB of HBM per device.

```python
from functools import partial
import jax
import jax.numpy as jnp
from jax import lax

D = 1024
H = 16
HD = 64
FF = 4096
TOK_DEV = 512
MEM_LEN = 768
BUCKETS = 2
SLOTS = 2
MEM_PIECE = 384
MEM_ROWS = 1536
TOKENS = 16384
N_DP = 16
N_MEM = 2


def bucket_table(key):
    drawn = jax.random.randint(key, (N_DP, N_MEM), 0, BUCKETS, dtype=jnp.int32)
    return drawn.at[0, 0].set(0)


def draw_bucket_ids(key, part):
    return bucket_table(key)


def draw_target_lengths(key, part):
    buckets = bucket_table(key)
    key = jax.random.fold_in(key, 7)
    slot_len = jnp.right_shift(jnp.int32(TOK_DEV), buckets)[:, :, None]
    slot_ids = jnp.arange(SLOTS, dtype=jnp.int32)[None, None, :]
    noise_bits = jax.random.randint(key, (N_DP, N_MEM, SLOTS), 0, 1 << 20, dtype=jnp.int32)
    bottom = slot_len // 2 + 1
    length = bottom + noise_bits % (slot_len - bottom + 1)
    length = jnp.where(slot_ids == 0, slot_len, length)
    return jnp.where(slot_ids * slot_len < TOK_DEV, length, 0).astype(jnp.int32)


def draw_memory_mask(key, part):
    buckets = bucket_table(key)
    key = jax.random.fold_in(key, 9)
    slot_len = jnp.right_shift(jnp.int32(TOK_DEV), buckets)[:, :, None]
    slot_ids = jnp.arange(SLOTS, dtype=jnp.int32)[None, None, :]
    noise_bits = jax.random.randint(key, (N_DP, N_MEM, SLOTS), 0, 1 << 20, dtype=jnp.int32)
    live_len = MEM_LEN - MEM_PIECE + 1 + noise_bits % MEM_PIECE
    live_len = jnp.where(slot_ids * slot_len < TOK_DEV, live_len, 0)
    piece_ids = jnp.arange(N_MEM, dtype=jnp.int32)[None, None, :, None, None]
    row_ids = jnp.arange(MEM_PIECE, dtype=jnp.int32)[None, None, None, None, :]
    position = piece_ids * MEM_PIECE + row_ids
    limit_rows = live_len[:, :, None, :, None]
    return (position < limit_rows).astype(jnp.int32)


def level_of(rng, extent, pieces, low, high):
    factor_of = 1.0
    for axis_at, parts in pieces:
        steps = jax.random.uniform(jax.random.fold_in(jax.random.fold_in(rng, 6), axis_at), (parts,), jnp.float32, low / len(pieces), high / len(pieces))
        factor_of = factor_of * jnp.repeat(jnp.exp(steps), extent[axis_at] // parts).reshape((-1,) + (1,) * (len(extent) - 1 - axis_at))
    return factor_of


def noise(rng, dims, width, reach, cuts=(), kind=jnp.bfloat16):
    values = jax.random.normal(rng, dims, jnp.float32) * width
    if len(cuts) > 0:
        values = level_of(rng, dims, cuts, -0.22, 0.18) * values
    return jnp.clip(values, min=-reach, max=reach).astype(kind)


def setup_inputs(seed: int = 0) -> dict:
    splits = jax.random.split(jax.random.key(seed), 16)
    return {
        "target_in": noise(splits[0], (TOKENS, D), 1.0, 6.0, ((0, 32),)),
        "memory_in": noise(splits[1], (N_DP, N_MEM, N_MEM, SLOTS, MEM_PIECE, D), 1.0, 6.0, ((0, 16), (2, 2))),
        "bucket_ids": draw_bucket_ids(jax.random.fold_in(splits[15], 71), 0),
        "target_lengths": draw_target_lengths(jax.random.fold_in(splits[15], 71), 0),
        "memory_mask": draw_memory_mask(jax.random.fold_in(splits[15], 71), 0),
        "self_qkv": noise(splits[5], (D, 3 * D), D ** -0.5, 0.1875, ((0, 32),), jnp.float32),
        "self_out": noise(splits[6], (D, D), 2 ** -0.5, 4.0, ((0, 32),), jnp.float32),
        "cross_q": noise(splits[7], (D, D), D ** -0.5, 0.1875, ((0, 32),), jnp.float32),
        "cross_kv": noise(splits[8], (D, 2 * D), D ** -0.5, 0.1875, ((0, 32),), jnp.float32),
        "cross_out": noise(splits[9], (D, D), 2 ** -0.5, 4.0, ((0, 32),), jnp.float32),
        "ffn_in": noise(splits[10], (D, FF), D ** -0.5, 0.1875, ((0, 32),), jnp.float32),
        "ffn_out": noise(splits[11], (FF, D), (FF // 32) ** -0.5, 0.5, ((0, 32),), jnp.float32),
        "norm_gains": jnp.clip(1.0 + 0.1 * jax.random.normal(splits[12], (D, 3), jnp.float32), 0.5, 1.5),
        "norm_biases": noise(splits[13], (D, 3), 0.3, 1.8, ((0, 32),), jnp.float32),
        "grad_out": noise(splits[14], (TOKENS, D), 1.0, 6.0, ((0, 32),)),
    }


@jax.custom_vjp
def low(v):
    return lax.optimization_barrier(v.astype(jnp.bfloat16)).astype(jnp.float32)

@jax.custom_vjp
def low_back(v):
    return v

def low_keep(v):
    return (low(v), None)

def low_pass(kept, grad):
    return (grad,)

def back_keep(v):
    return (v, None)

def back_low(kept, grad):
    return (low(grad),)
low.defvjp(low_keep, low_pass)
low_back.defvjp(back_keep, back_low)
ALPHA = 300.0 ** 0.25
NEG_LARGE = -1e+30
EPSILON = 1e-05

def matmul(first_op, second_op):
    return jnp.dot(first_op, second_op, precision=lax.Precision.HIGHEST, preferred_element_type=jnp.float32)

def both_round(values):
    return low(low_back(values))

def layer_norm(values, gain_row, shift_row):
    centred = values - lax.optimization_barrier(jnp.mean(values, axis=-1, keepdims=True))
    spread = lax.optimization_barrier(jnp.mean(centred * centred, axis=-1, keepdims=True))
    return centred * lax.rsqrt(spread + EPSILON) * gain_row + shift_row

def attend(queries, keys_all, values_all, allowed):
    query_heads = queries.reshape(queries.shape[0], H, HD)
    key_heads = keys_all.reshape(keys_all.shape[0], H, HD)
    value_heads = values_all.reshape(values_all.shape[0], H, HD)
    scores = jnp.einsum('qhd,khd->hqk', query_heads, key_heads, precision=lax.Precision.HIGHEST) * HD ** (-0.5)
    scores = jnp.where(allowed[None], low_back(scores), NEG_LARGE)
    attn_probs = jax.nn.softmax(scores, axis=-1)
    mixed = jnp.einsum('hqk,khd->qhd', low(attn_probs), value_heads, precision=lax.Precision.HIGHEST)
    return mixed.reshape(queries.shape[0], D)

def pack_layer(weights, packed):
    w_qkv, w_so, w_cq, w_ckv, w_co, w_in, w_out, gain_cols, shift_cols = weights
    rows_in, memory_rows, bucket, lengths, memory_live = packed
    slot_len = jnp.right_shift(jnp.int32(TOK_DEV), bucket)
    row_ids = jnp.arange(TOK_DEV, dtype=jnp.int32)
    slot_ids = row_ids // slot_len
    slot_table = slot_ids[:, None] == jnp.arange(SLOTS, dtype=jnp.int32)[None, :]
    key_limit = lax.optimization_barrier(jnp.sum(jnp.where(slot_table, lengths[None, :], 0), axis=1))
    visible = row_ids % slot_len < key_limit
    self_allowed = (slot_ids[:, None] == slot_ids[None, :]) & (row_ids[None, :] <= row_ids[:, None]) & visible[None, :]
    memory_ids = jnp.arange(MEM_ROWS, dtype=jnp.int32)
    key_slot = memory_ids // MEM_PIECE % SLOTS
    cross_allowed = (slot_ids[:, None] == key_slot[None, :]) & (memory_live == 1)[None, :]
    united = both_round(matmul(rows_in, w_qkv))
    self_mixed = both_round(attend(united[:, :D], united[:, D:2 * D], united[:, 2 * D:], self_allowed))
    first_out = layer_norm(ALPHA * rows_in + low_back(matmul(self_mixed, w_so)), gain_cols[:, 0], shift_cols[:, 0])
    cross_query = both_round(matmul(low(first_out), w_cq))
    key_value = both_round(matmul(memory_rows, w_ckv))
    cross_mixed = both_round(attend(cross_query, key_value[:, :D], key_value[:, D:], cross_allowed))
    second_out = layer_norm(ALPHA * first_out + low_back(matmul(cross_mixed, w_co)), gain_cols[:, 1], shift_cols[:, 1])
    hidden = low_back(matmul(low(second_out), w_in))
    activated = low(jax.nn.gelu(hidden, approximate=False))
    return layer_norm(ALPHA * second_out + low_back(matmul(activated, w_out)), gain_cols[:, 2], shift_cols[:, 2])

def reference(target_in, memory_in, bucket_ids, target_lengths, memory_mask, self_qkv, self_out, cross_q, cross_kv, cross_out, ffn_in, ffn_out, norm_gains, norm_biases, grad_out):
    pack_count = N_DP * N_MEM
    buckets = bucket_ids.reshape(pack_count)
    lengths = target_lengths.reshape(pack_count, SLOTS)
    live_all = memory_mask.reshape(pack_count, MEM_ROWS)

    def forward(rows_all, memory_all, *masters):
        weights = tuple((low(master) for master in masters))
        pack_step = jax.checkpoint(partial(pack_layer, weights))
        packed = (rows_all.reshape(pack_count, TOK_DEV, D), memory_all.reshape(pack_count, MEM_ROWS, D), buckets, lengths, live_all)
        return lax.map(pack_step, packed).reshape(TOKENS, D)
    masters = (self_qkv, self_out, cross_q, cross_kv, cross_out, ffn_in, ffn_out, norm_gains, norm_biases)
    layer_out, pullback = jax.vjp(forward, target_in.astype(jnp.float32), memory_in.astype(jnp.float32), *masters)
    gradients = pullback(grad_out.astype(jnp.float32))
    return (layer_out.astype(jnp.bfloat16), gradients[0].astype(jnp.bfloat16), gradients[1].astype(jnp.bfloat16), gradients[2], gradients[3], gradients[4], gradients[5], gradients[6], gradients[7], gradients[8], gradients[9], gradients[10])
```

```python
import functools

import jax
import jax.numpy as jnp
from jax import lax
from jax.experimental import pallas as pl
from jax.experimental.pallas import tpu as pltpu
from jax.sharding import PartitionSpec as P

HD = 64
LANES = 128
ALPHA = 300.0**0.25
NEG_LARGE = -1e30
EPSILON = 1e-05
VMEM_BYTES = 52 * 1024 * 1024
SCALE = HD**-0.5

BF16 = jnp.bfloat16
F32 = jnp.float32


def plain_dot(first_op, second_op):
    return jnp.dot(first_op, second_op, preferred_element_type=F32)


def lead_dot(first_op, second_op):
    return lax.dot_general(
        first_op, second_op, (((0,), (0,)), ((), ())), preferred_element_type=F32
    )


def back_dot(first_op, second_op):
    return lax.dot_general(
        first_op, second_op, (((1,), (1,)), ((), ())), preferred_element_type=F32
    )


def pick_entry(values, wanted):
    return jnp.sum(jnp.where(jnp.arange(values.shape[0]) == wanted, values, 0))


def kernel_params():
    return pltpu.CompilerParams(vmem_limit_bytes=VMEM_BYTES)


def whole_spec(shape):
    return pl.BlockSpec(shape, lambda *_: (0,) * len(shape))


def head_lanes(rows, head):
    lane = lax.broadcasted_iota(jnp.int32, (rows, LANES), 1)
    return (lane < HD) if head == 0 else (lane >= HD)


def visible(query_ids, key_ids, slot_len, first_len, second_len):
    query_slot = (query_ids >= slot_len).astype(jnp.int32)
    key_slot = (key_ids >= slot_len).astype(jnp.int32)
    place = key_ids - key_slot * slot_len
    limit = jnp.where(key_slot == 0, first_len, second_len)
    return (query_slot == key_slot) & (key_ids <= query_ids) & (place < limit)


def pair_forward(query, keys, values, bias):
    rows, key_rows = query.shape[0], keys.shape[0]
    mixed, peaks = [], []
    for head in range(2):
        mine = head_lanes(rows, head)
        masked = jnp.where(mine, query * BF16(SCALE), BF16(0))
        scores = back_dot(masked, keys) + bias
        peak = jnp.max(scores, axis=1, keepdims=True)
        raised = jnp.exp(scores - peak).astype(BF16)
        widened = jnp.where(head_lanes(key_rows, head), values, BF16(1))
        mixed.append(plain_dot(raised, widened))
        peaks.append(peak)
    first = head_lanes(rows, 0)
    totals = pltpu.roll(jnp.where(first, mixed[1], mixed[0]), HD, 1)
    joined = jnp.where(first, mixed[0], mixed[1])
    log_totals = jnp.where(first, peaks[0], peaks[1]) + jnp.log(totals)
    return joined / totals, log_totals


def pair_backward(query, keys, values, upstream, bias, log_rows, delta_rows):
    rows, key_rows = query.shape[0], keys.shape[0]
    grad_q, grad_k, grad_v = None, None, None
    for head in range(2):
        mine = head_lanes(rows, head)
        masked = jnp.where(mine, query * BF16(SCALE), BF16(0))
        masked_up = jnp.where(mine, upstream, BF16(0))
        scores = back_dot(keys, masked) + bias
        probs = jnp.exp(scores - log_rows[head])
        grad_probs = back_dot(values, masked_up)
        grad_scores = (probs * (grad_probs - delta_rows[head])).astype(BF16)
        part_v = plain_dot(probs.astype(BF16), masked_up)
        part_k = plain_dot(grad_scores, masked)
        masked_keys = jnp.where(head_lanes(key_rows, head), keys, BF16(0))
        part_q = lead_dot(grad_scores, masked_keys)
        grad_q = part_q if grad_q is None else grad_q + part_q
        grad_k = part_k if grad_k is None else grad_k + part_k
        grad_v = part_v if grad_v is None else grad_v + part_v
    return grad_q * SCALE, grad_k, grad_v


def stat_rows(log_block, mixed, upstream):
    log_turned = log_block.T
    products = (mixed.astype(F32) * upstream.astype(F32)).T
    log_rows = [log_turned[:1], log_turned[HD : HD + 1]]
    delta_rows = [jnp.sum(products[h * HD : (h + 1) * HD], axis=0, keepdims=True) for h in range(2)]
    return log_rows, delta_rows


def self_forward_kernel(meta, q_ref, k_ref, v_ref, mixed_ref, log_ref, bias):
    rows = q_ref.shape[0]

    @pl.when(pl.program_id(0) == 0)
    def _():
        query_ids = lax.broadcasted_iota(jnp.int32, (rows, rows), 0)
        key_ids = lax.broadcasted_iota(jnp.int32, (rows, rows), 1)
        seen = visible(query_ids, key_ids, meta[0], meta[1], meta[2])
        bias[...] = jnp.where(seen, 0.0, NEG_LARGE)

    half = rows // 2
    for start, stop in ((0, half), (half, rows)):
        mixed, log_totals = pair_forward(
            q_ref[start:stop, :], k_ref[:stop, :], v_ref[:stop, :], bias[start:stop, :stop]
        )
        mixed_ref[start:stop, :] = mixed.astype(BF16)
        log_ref[start:stop, :] = log_totals


def self_forward(meta, united):
    rows, width = united.shape[0], united.shape[1] // 3
    pairs = width // LANES
    spec = lambda third: pl.BlockSpec((rows, LANES), lambda i, _: (0, third * pairs + i))
    out_spec = pl.BlockSpec((rows, LANES), lambda i, _: (0, i))
    return pl.pallas_call(
        self_forward_kernel,
        grid_spec=pltpu.PrefetchScalarGridSpec(
            num_scalar_prefetch=1,
            grid=(pairs,),
            in_specs=[spec(0), spec(1), spec(2)],
            out_specs=[out_spec, out_spec],
            scratch_shapes=[pltpu.VMEM((rows, rows), F32)],
        ),
        out_shape=[
            jax.ShapeDtypeStruct((rows, width), BF16),
            jax.ShapeDtypeStruct((rows, width), F32),
        ],
        compiler_params=kernel_params(),
        cost_estimate=pl.CostEstimate(
            flops=12 * rows * rows * width, bytes_accessed=12 * rows * width, transcendentals=0
        ),
        name="self_forward",
    )(meta, united, united, united)


def self_backward_kernel(
    meta, q_ref, k_ref, v_ref, mixed_ref, up_ref, log_ref, grad_ref, bias
):
    rows = q_ref.shape[0]
    width = grad_ref.shape[1] // 3
    pair = pl.program_id(0)

    @pl.when(pair == 0)
    def _():
        key_ids = lax.broadcasted_iota(jnp.int32, (rows, rows), 0)
        query_ids = lax.broadcasted_iota(jnp.int32, (rows, rows), 1)
        seen = visible(query_ids, key_ids, meta[0], meta[1], meta[2])
        bias[...] = jnp.where(seen, 0.0, NEG_LARGE)

    log_rows, delta_rows = stat_rows(log_ref[...], mixed_ref[...], up_ref[...])
    half = rows // 2
    parts = []
    for start, stop in ((0, half), (half, rows)):
        parts.append(
            pair_backward(
                q_ref[start:stop, :],
                k_ref[:stop, :],
                v_ref[:stop, :],
                up_ref[start:stop, :],
                bias[:stop, start:stop],
                [row[:, start:stop] for row in log_rows],
                [row[:, start:stop] for row in delta_rows],
            )
        )
    low, high = parts
    columns = lambda third: pl.ds(pl.multiple_of(third * width + pair * LANES, LANES), LANES)
    grad_ref[:half, columns(0)] = low[0].astype(BF16)
    grad_ref[half:, columns(0)] = high[0].astype(BF16)
    for third in (1, 2):
        grad_ref[:half, columns(third)] = (low[third] + high[third][:half]).astype(BF16)
        grad_ref[half:, columns(third)] = high[third][half:].astype(BF16)


def self_backward(meta, united, mixed, upstream, log_totals):
    rows, width = united.shape[0], united.shape[1] // 3
    pairs = width // LANES
    spec = lambda third: pl.BlockSpec((rows, LANES), lambda i, _: (0, third * pairs + i))
    return pl.pallas_call(
        self_backward_kernel,
        grid_spec=pltpu.PrefetchScalarGridSpec(
            num_scalar_prefetch=1,
            grid=(pairs,),
            in_specs=[spec(0), spec(1), spec(2), spec(0), spec(0), spec(0)],
            out_specs=whole_spec((rows, 3 * width)),
            scratch_shapes=[pltpu.VMEM((rows, rows), F32)],
        ),
        out_shape=jax.ShapeDtypeStruct((rows, 3 * width), BF16),
        compiler_params=kernel_params(),
        cost_estimate=pl.CostEstimate(
            flops=30 * rows * rows * width, bytes_accessed=20 * rows * width, transcendentals=0
        ),
        name="self_backward",
    )(meta, united, united, united, mixed, upstream, log_totals)


def join_keys(near_ref, far_ref, joined):
    slots, piece = near_ref.shape[0], near_ref.shape[1]
    for slot in range(slots):
        joined[slot, :piece, :] = near_ref[slot]
        joined[slot, piece:, :] = far_ref[slot]


def cross_forward_kernel(
    meta, q_ref, kn_ref, vn_ref, kf_ref, vf_ref, bias_ref, mixed_ref, log_ref, keys, values
):
    half = q_ref.shape[0] // 2
    join_keys(kn_ref, kf_ref, keys)
    join_keys(vn_ref, vf_ref, values)
    for part in range(2):
        slot = part * meta[0]
        rows = slice(part * half, (part + 1) * half)
        mixed, log_totals = pair_forward(q_ref[rows, :], keys[slot], values[slot], bias_ref[slot])
        mixed_ref[rows, :] = mixed.astype(BF16)
        log_ref[rows, :] = log_totals


def cross_forward(meta, query, near, far, bias):
    rows, width = query.shape
    slots, piece = near.shape[0], near.shape[1]
    pairs = width // LANES
    row_spec = pl.BlockSpec((rows, LANES), lambda i, _: (0, i))
    spec = lambda half: pl.BlockSpec((slots, piece, LANES), lambda i, _: (0, 0, half * pairs + i))
    return pl.pallas_call(
        cross_forward_kernel,
        grid_spec=pltpu.PrefetchScalarGridSpec(
            num_scalar_prefetch=1,
            grid=(pairs,),
            in_specs=[row_spec, spec(0), spec(1), spec(0), spec(1), whole_spec(bias.shape)],
            out_specs=[row_spec, row_spec],
            scratch_shapes=[pltpu.VMEM((slots, 2 * piece, LANES), BF16)] * 2,
        ),
        out_shape=[
            jax.ShapeDtypeStruct((rows, width), BF16),
            jax.ShapeDtypeStruct((rows, width), F32),
        ],
        compiler_params=kernel_params(),
        cost_estimate=pl.CostEstimate(
            flops=32 * rows * piece * width, bytes_accessed=24 * rows * width, transcendentals=0
        ),
        name="cross_forward",
    )(meta, query, near, near, far, far, bias)


def cross_backward_kernel(
    meta,
    q_ref,
    kn_ref,
    vn_ref,
    kf_ref,
    vf_ref,
    bias_ref,
    mixed_ref,
    up_ref,
    log_ref,
    grad_q_ref,
    grad_kv_ref,
    keys,
    values,
):
    half = q_ref.shape[0] // 2
    slots, piece = kn_ref.shape[0], kn_ref.shape[1]
    width = grad_kv_ref.shape[1] // 2
    join_keys(kn_ref, kf_ref, keys)
    join_keys(vn_ref, vf_ref, values)
    log_rows, delta_rows = stat_rows(log_ref[...], mixed_ref[...], up_ref[...])
    parts = []
    for part in range(2):
        slot = part * meta[0]
        rows = slice(part * half, (part + 1) * half)
        bias_column = bias_ref[slot]
        grads = pair_backward(
            q_ref[rows, :],
            keys[slot],
            values[slot],
            up_ref[rows, :],
            jnp.concatenate([bias_column] * (half // LANES), axis=1),
            [row[:, rows] for row in log_rows],
            [row[:, rows] for row in delta_rows],
        )
        grad_q_ref[rows, :] = grads[0].astype(BF16)
        parts.append(grads)
    split = meta[0].astype(F32)
    start = pl.program_id(0) * LANES
    for which in range(2):
        early, late = parts[0][1 + which], parts[1][1 + which]
        columns = pl.ds(pl.multiple_of(which * width + start, LANES), LANES)
        by_slot = (early + late * (1.0 - split), late * split)
        for slot in range(slots):
            for source in range(2):
                first = (source * slots + slot) * piece
                grad_kv_ref[first : first + piece, columns] = by_slot[slot][
                    source * piece : (source + 1) * piece
                ].astype(BF16)


def cross_backward(meta, query, near, far, bias, mixed, upstream, log_totals):
    rows, width = query.shape
    slots, piece = near.shape[0], near.shape[1]
    pairs = width // LANES
    memory_rows = 2 * slots * piece
    row_spec = pl.BlockSpec((rows, LANES), lambda i, _: (0, i))
    spec = lambda half: pl.BlockSpec((slots, piece, LANES), lambda i, _: (0, 0, half * pairs + i))
    return pl.pallas_call(
        cross_backward_kernel,
        grid_spec=pltpu.PrefetchScalarGridSpec(
            num_scalar_prefetch=1,
            grid=(pairs,),
            in_specs=[row_spec, spec(0), spec(1), spec(0), spec(1), whole_spec(bias.shape)]
            + [row_spec] * 3,
            out_specs=[row_spec, whole_spec((memory_rows, 2 * width))],
            scratch_shapes=[pltpu.VMEM((slots, 2 * piece, LANES), BF16)] * 2,
        ),
        out_shape=[
            jax.ShapeDtypeStruct((rows, width), BF16),
            jax.ShapeDtypeStruct((memory_rows, 2 * width), BF16),
        ],
        compiler_params=kernel_params(),
        cost_estimate=pl.CostEstimate(
            flops=80 * rows * piece * width, bytes_accessed=40 * rows * width, transcendentals=0
        ),
        name="cross_backward",
    )(meta, query, near, near, far, far, bias, mixed, upstream, log_totals)


def swap_core(values):
    size = lax.axis_size("dp")
    return lax.ppermute(values, "dp", [(i, i ^ 1) for i in range(size)])


def swap_next(values):
    size = lax.axis_size("dp")
    return lax.ppermute(values, "dp", [(i, i ^ 2) for i in range(size)])


def swap_mem(values):
    return lax.ppermute(values, "mem", [(0, 1), (1, 0)])


def swap_outer(values, far):
    size = lax.axis_size("dp")
    return lax.ppermute(values, "dp", [(i, i ^ (4 * far)) for i in range(size)])


def outer_groups():
    size = lax.axis_size("dp")
    return [list(range(base, size, 4)) for base in range(4)]


def place_bits():
    dp, mem = lax.axis_index("dp"), lax.axis_index("mem")
    return jnp.stack([(dp >> 1) & 1, dp & 1, mem]).astype(jnp.int32)


def outer_gather(shard, direct):
    outer, rows = lax.axis_size("dp") // 4, shard.shape[0]
    if not direct:
        stacked = lax.all_gather(shard, "dp", axis_index_groups=outer_groups(), axis=0, tiled=True)
        return stacked.reshape(outer, rows, -1)
    place = lax.axis_index("dp") >> 2
    blocks = jnp.stack([shard] + [swap_outer(shard, far) for far in range(1, outer)])
    bit = 1
    while bit < outer:
        turned = jnp.stack([blocks[i ^ bit] for i in range(outer)])
        blocks = jnp.where((place & bit) != 0, turned, blocks)
        bit *= 2
    return blocks


FIRST = (swap_next, swap_mem)
SECOND = (swap_mem, swap_next)


class Wave:
    def __init__(self, shard, cut, direct):
        self.rows, self.columns, self.cut = shard.shape[0], shard.shape[1], cut
        stacked = outer_gather(shard, direct)
        self.outer = stacked.shape[0]
        self.halves = []
        for half, part in enumerate((stacked[:, :, :cut], stacked[:, :, cut:])):
            near = jnp.stack((part, FIRST[half](part)))
            far = SECOND[half](near)
            self.halves.append((near, far, swap_core(near), swap_core(far)))


class Weight:
    def __init__(self, wave, start, width, whole=None):
        self.wave, self.start, self.width, self.whole = wave, start, width, whole
        if whole is not None:
            self.arrays, self.rows, self.outer = [whole], whole.shape[4], whole.shape[0]
        else:
            self.rows, self.outer = wave.rows, wave.outer
            used = [start < wave.cut, start + width > wave.cut]
            self.arrays = [a for half in range(2) if used[half] for a in wave.halves[half]]

    def copies(self, kind, start, size, bits, find, target):
        if self.whole is not None:
            source = find(self.whole)
            if kind == "columns":
                return [(source.at[:, :, :, :, :, pl.ds(start, size)], target)]
            return [(source.at[start], target)]
        wave, pairs = self.wave, []
        for half in range(2):
            if kind == "columns" and (self.start + start >= wave.cut) != (half == 1):
                continue
            for number, array in enumerate(wave.halves[half]):
                for first in range(2):
                    second, core = number & 1, number >> 1
                    near, mem = (first, second) if half == 0 else (second, first)
                    place = (bits[0] ^ near, bits[1] ^ core, bits[2] ^ mem)
                    if kind == "columns":
                        local = self.start + start - half * wave.cut
                        source = find(array).at[first, :, :, pl.ds(local, size)]
                        pairs.append((source, target.at[:, place[0], place[1], place[2]]))
                    else:
                        source = find(array).at[first, start]
                        columns = pl.ds(half * wave.cut, array.shape[-1])
                        pairs.append((source, target.at[place[0], place[1], place[2], :, columns]))
        return pairs


def weight_call(name, bits, weights, plan, inputs, outs, scratch, body, flops):
    arrays = []
    for weight in weights:
        arrays += [a for a in weight.arrays if not any(a is b for b in arrays)]
    kind, size = plan[0][1], plan[0][3]
    lead = weights[plan[0][0]]
    if kind == "columns":
        chunk = (lead.outer, 2, 2, 2, lead.rows, size)
    else:
        chunk = (2, 2, 2, lead.rows, lead.width)
    n_in, n_arrays, n_out = len(inputs), len(arrays), len(outs)

    def kernel(bits_ref, *refs):
        ins, refs = refs[:n_in], refs[n_in:]
        pieces, refs = refs[:n_arrays], refs[n_arrays:]
        out_refs, refs = refs[:n_out], refs[n_out:]
        held, sems = refs[-2:]
        bits_now = [bits_ref[i] for i in range(3)]

        def find(array):
            return next(ref for ref, known in zip(pieces, arrays) if known is array)

        def issue(number):
            which, kind, start, size = plan[number]
            slot = number % 2
            for source, target in weights[which].copies(
                kind, start, size, bits_now, find, held.at[slot]
            ):
                pltpu.make_async_copy(source, target, sems.at[slot]).start()

        taken = [0]

        def fetch():
            number = taken[0]
            taken[0] += 1
            if number + 1 < len(plan):
                issue(number + 1)
            slot = number % 2
            pltpu.make_async_copy(held.at[slot], held.at[slot], sems.at[slot]).wait()
            return held[slot].reshape(-1, chunk[-1])

        issue(0)
        body(fetch, ins, out_refs, refs[:-2])

    moved = sum(a.size * a.dtype.itemsize for a in inputs) + 2 * len(plan) * lead.outer * size
    return pl.pallas_call(
        kernel,
        in_specs=[pl.BlockSpec(memory_space=pltpu.SMEM)]
        + [pl.BlockSpec(memory_space=pltpu.VMEM)] * n_in
        + [pl.BlockSpec(memory_space=pl.ANY)] * n_arrays,
        out_specs=[pl.BlockSpec(memory_space=pltpu.VMEM)] * n_out,
        out_shape=[jax.ShapeDtypeStruct(shape, kind) for shape, kind in outs],
        scratch_shapes=[pltpu.VMEM(shape, kind) for shape, kind in scratch]
        + [pltpu.VMEM((2, *chunk), BF16), pltpu.SemaphoreType.DMA((2,))],
        compiler_params=kernel_params(),
        cost_estimate=pl.CostEstimate(flops=flops, bytes_accessed=moved, transcendentals=0),
        name=name,
    )(bits, *inputs, *arrays)


def columns_plan(which, width, size):
    return [(which, "columns", start, size) for start in range(0, width, size)]


def row_blocks(rows, size, step):
    def run(i, carry):
        step(pl.ds(pl.multiple_of(i * size, size), size))
        return carry

    lax.fori_loop(0, rows // size, run, 0)


def normed_parts(values):
    centred = values - jnp.mean(values, axis=-1, keepdims=True)
    spread = jnp.mean(centred * centred, axis=-1, keepdims=True)
    rate = lax.rsqrt(spread + EPSILON)
    return centred * rate, rate


def norm_gradient(normed, rate, gain, cotangent):
    inner = cotangent * gain
    mean_inner = jnp.mean(inner, axis=-1, keepdims=True)
    mean_both = jnp.mean(inner * normed, axis=-1, keepdims=True)
    return rate * (inner - mean_inner - normed * mean_both)


def add_stats(stats, normed, cotangent):
    fold = lambda values: jnp.sum(values.reshape(-1, 8, values.shape[-1]), axis=0)
    stats[:8, :] += fold(cotangent * normed)
    stats[8:, :] += fold(cotangent)


def norm_table(bits, weight):
    features = weight.outer * 8 * weight.rows

    def body(fetch, ins, outs, scratch):
        outs[0][...] = fetch().astype(F32).T[:8]

    return weight_call(
        "norm_table", bits, [weight], [(0, "columns", 0, LANES)], [],
        [((8, features), F32)], [], body, 0,
    )[0]


def project(name, bits, weight, sources, size):
    def body(fetch, ins, outs, scratch):
        for start in range(0, weight.width, size):
            chunk = fetch()
            for source, target in zip(ins, outs):
                target[:, start : start + size] = plain_dot(source[...], chunk).astype(BF16)

    flops = sum(2 * source.size * weight.width for source in sources)
    return weight_call(
        name, bits, [weight], columns_plan(0, weight.width, size), sources,
        [((source.shape[0], weight.width), BF16) for source in sources], [], body, flops,
    )


def mix_norm(name, bits, weight, mixed, residual, table, index, query_weight=None):
    rows, width = mixed.shape
    size = 512 if width % 512 == 0 else width

    def body(fetch, ins, outs, scratch):
        mixed_ref, residual_ref, table_ref = ins
        summed, out, out_low = outs[:3]
        for start in range(0, width, size):
            part = plain_dot(mixed_ref[...], fetch())
            columns = slice(start, start + size)
            summed[:, columns] = ALPHA * residual_ref[:, columns].astype(F32) + part
        gain, shift = table_ref[index : index + 1, :], table_ref[3 + index : 4 + index, :]

        def step(block):
            normed, _ = normed_parts(summed[block, :])
            values = normed * gain + shift
            out[block, :] = values
            out_low[block, :] = values.astype(BF16)

        row_blocks(rows, 32, step)
        if query_weight is not None:
            for start in range(0, width, size):
                part = plain_dot(out_low[...], fetch())
                outs[3][:, start : start + size] = part.astype(BF16)

    weights = [weight] + ([query_weight] if query_weight is not None else [])
    plan = [entry for i in range(len(weights)) for entry in columns_plan(i, width, size)]
    outs = [((rows, width), F32), ((rows, width), F32), ((rows, width), BF16)]
    if query_weight is not None:
        outs.append(((rows, width), BF16))
    flops = 2 * rows * width * width * len(weights)
    return weight_call(
        name, bits, weights, plan, [mixed, residual, table], outs, [], body, flops
    )


def feed_in(bits, weight, source):
    rows, size = source.shape[0], 512

    def body(fetch, ins, outs, scratch):
        held = scratch[0]
        for start in range(0, weight.width, size):
            held[...] = plain_dot(ins[0][...], fetch())

            def step(block):
                hidden = held[block, :]
                below = 0.5 + 0.5 * lax.erf(hidden * (0.5**0.5))
                density = jnp.exp(-0.5 * hidden * hidden) * (2.0 * jnp.pi) ** -0.5
                outs[0][block, start : start + size] = (hidden * below).astype(BF16)
                outs[1][block, start : start + size] = (below + hidden * density).astype(BF16)

            row_blocks(rows, 64, step)

    out = ((rows, weight.width), BF16)
    return weight_call(
        "feed_in", bits, [weight], columns_plan(0, weight.width, size), [source], [out, out],
        [((rows, size), F32)], body, 2 * source.size * weight.width,
    )


def feed_out(bits, weight, activated, residual, table, cotangent):
    rows, width = residual.shape
    size = 512 if width % 512 == 0 else width

    def body(fetch, ins, outs, scratch):
        act_ref, residual_ref, table_ref, up_ref = ins
        layer_out, grad, grad_low, stats = outs
        summed = scratch[0]
        for start in range(0, width, size):
            columns = slice(start, start + size)
            part = plain_dot(act_ref[...], fetch())
            summed[:, columns] = ALPHA * residual_ref[:, columns] + part
        gain, shift = table_ref[2:3, :], table_ref[5:6, :]
        stats[...] = jnp.zeros_like(stats)

        def step(block):
            normed, rate = normed_parts(summed[block, :])
            layer_out[block, :] = (normed * gain + shift).astype(BF16)
            upstream = up_ref[block, :].astype(F32)
            values = norm_gradient(normed, rate, gain, upstream)
            grad[block, :] = values
            grad_low[block, :] = values.astype(BF16)
            add_stats(stats, normed, upstream)

        row_blocks(rows, 32, step)

    outs = [((rows, width), BF16), ((rows, width), F32), ((rows, width), BF16), ((16, width), F32)]
    return weight_call(
        "feed_out", bits, [weight], columns_plan(0, width, size),
        [activated, residual, table, cotangent], outs, [((rows, width), F32)], body,
        2 * activated.size * width,
    )


def feed_back(bits, weight, cotangent, slope):
    rows, features = slope.shape
    size = features // weight.outer

    def body(fetch, ins, outs, scratch):
        for block in range(weight.outer):
            part = back_dot(ins[0][...], fetch())
            columns = slice(block * size, (block + 1) * size)
            outs[0][:, columns] = (part * ins[1][:, columns].astype(F32)).astype(BF16)

    return weight_call(
        "feed_back", bits, [weight], [(0, "outer", i, 1) for i in range(weight.outer)],
        [cotangent, slope], [((rows, features), BF16)], [], body, 2 * cotangent.size * features,
    )[0]


def norm_back(name, bits, weight, cotangent, carried, summed, table, index, mix_weight):
    rows, width = summed.shape
    size = min(1024, weight.width)

    def body(fetch, ins, outs, scratch):
        up_ref, carried_ref, summed_ref, table_ref = ins
        grad, grad_low, grad_mixed, stats = outs
        total = scratch[0]
        for start in range(0, weight.width, size):
            part = back_dot(up_ref[:, start : start + size], fetch())
            total[...] = part + (ALPHA * carried_ref[...] if start == 0 else total[...])
        gain = table_ref[index : index + 1, :]
        stats[...] = jnp.zeros_like(stats)

        def step(block):
            normed, rate = normed_parts(summed_ref[block, :])
            upstream = total[block, :]
            values = norm_gradient(normed, rate, gain, upstream)
            grad[block, :] = values
            grad_low[block, :] = values.astype(BF16)
            add_stats(stats, normed, upstream)

        row_blocks(rows, 32, step)
        grad_mixed[...] = back_dot(grad_low[...], fetch()).astype(BF16)

    outs = [((rows, width), F32), ((rows, width), BF16), ((rows, width), BF16), ((16, width), F32)]
    return weight_call(
        name, bits, [weight, mix_weight],
        columns_plan(0, weight.width, size) + columns_plan(1, width, size),
        [cotangent, carried, summed, table], outs, [((rows, width), F32)], body,
        2 * cotangent.size * width + 2 * rows * width * width,
    )


def input_back(name, bits, weight, cotangent, carried, size):
    rows, features = cotangent.shape[0], weight.outer * 8 * weight.rows
    step = min(rows, 512)
    starts = list(range(0, weight.width, size))

    def body(fetch, ins, outs, scratch):
        for start in starts:
            chunk = fetch()
            for row in range(0, rows, step):
                block = slice(row, row + step)
                part = back_dot(ins[0][block, start : start + size], chunk)
                if start == 0 and carried is not None:
                    part += ALPHA * ins[1][block, :]
                elif start > 0:
                    part += scratch[0][block, :]
                if start == starts[-1]:
                    outs[0][block, :] = part.astype(BF16)
                else:
                    scratch[0][block, :] = part

    return weight_call(
        name, bits, [weight], columns_plan(0, weight.width, size),
        [cotangent] + ([carried] if carried is not None else []), [((rows, features), BF16)],
        [((rows, features), F32)], body, 2 * cotangent.size * features,
    )[0]


def weight_grad(bits, sources, cotangent, outer):
    features = sources[0].shape[1]
    total_rows, width = cotangent.shape
    shard_rows = features // (8 * outer)
    chunk = min(512, width)

    def kernel(bits_ref, *refs):
        source_refs = refs[: len(sources)]
        grads, own_ref, other_ref, turned = refs[len(sources) :]

        @pl.when(pl.program_id(0) == 0)
        def _():
            filled = 0
            for ref in source_refs:
                stop = filled + ref.shape[0]
                for block in range(features // LANES):
                    turned_block = ref[:, block * LANES : (block + 1) * LANES].T
                    for part in range(LANES // shard_rows):
                        device = block * (LANES // shard_rows) + part
                        mem, core, near = device & 1, (device >> 1) & 1, (device >> 2) & 1
                        place = (core ^ bits_ref[1]) * 2 + (mem ^ bits_ref[2])
                        place = (place * 2 + (near ^ bits_ref[0])) * outer + (device >> 3)
                        target = pl.ds(pl.multiple_of(place * shard_rows, shard_rows), shard_rows)
                        turned[target, filled:stop] = turned_block[
                            part * shard_rows : (part + 1) * shard_rows
                        ]
                filled = stop

        half = features // 2
        for number, ref in enumerate((own_ref, other_ref)):
            product = plain_dot(turned[number * half : (number + 1) * half, :], grads[...])
            ref[...] = product.astype(BF16).reshape(ref.shape)

    shape = (2, 2, outer, shard_rows)
    out_spec = pl.BlockSpec((*shape, chunk), lambda i, _: (0, 0, 0, 0, i))
    return pl.pallas_call(
        kernel,
        grid_spec=pltpu.PrefetchScalarGridSpec(
            num_scalar_prefetch=1,
            grid=(width // chunk,),
            in_specs=[whole_spec(source.shape) for source in sources]
            + [pl.BlockSpec((total_rows, chunk), lambda i, _: (0, i))],
            out_specs=[out_spec, out_spec],
            scratch_shapes=[pltpu.VMEM((features, total_rows), BF16)],
        ),
        out_shape=[jax.ShapeDtypeStruct((*shape, width), BF16)] * 2,
        compiler_params=kernel_params(),
        cost_estimate=pl.CostEstimate(
            flops=2 * total_rows * features * width,
            bytes_accessed=2 * (total_rows + features) * width,
            transcendentals=0,
        ),
        name="weight_grad",
    )(bits, *sources, cotangent)


def relative_rows(bits, values, outer):
    rows = values.shape[0] // (8 * outer)
    blocks = values.reshape(outer, 2, 2, 2, rows, -1)
    for axis, bit in ((1, bits[0]), (2, bits[1]), (3, bits[2])):
        blocks = jnp.where(bit == 1, jnp.flip(blocks, axis), blocks)
    blocks = blocks.transpose(2, 3, 1, 0, 4, 5)
    return blocks[0], blocks[1]


def add_up(*terms):
    return sum(term.astype(F32) for term in terms).astype(BF16)


def scatter_pieces(own, other, cut, direct):
    far = swap_core(other)
    halves = []
    for half in range(2):
        columns = slice(0, cut) if half == 0 else slice(cut, None)
        near, far_part = own[..., columns], far[..., columns]
        if half == 0:
            first = swap_mem(add_up(near[1], far_part[1]))
            second = swap_next(add_up(near[0, 1], far_part[0, 1], first[1]))
        else:
            first = swap_next(add_up(near[:, 1], far_part[:, 1]))
            second = swap_mem(add_up(near[1, 0], far_part[1, 0], first[1]))
        halves.append(add_up(near[0, 0], far_part[0, 0], first[0], second))
    joined = jnp.concatenate(halves, axis=-1)
    if not direct:
        joined = joined.reshape(-1, joined.shape[-1])
        return lax.psum_scatter(
            joined, "dp", axis_index_groups=outer_groups(), scatter_dimension=0, tiled=True
        ).astype(F32)
    place = lax.axis_index("dp") >> 2
    block = lambda far: lax.dynamic_index_in_dim(joined, place ^ far, 0, False)
    parts = [block(0)] + [swap_outer(block(far), far) for far in range(1, joined.shape[0])]
    return sum(part.astype(F32) for part in parts)


def per_device(
    target_in,
    memory_in,
    bucket_ids,
    target_lengths,
    memory_mask,
    self_qkv,
    self_out,
    cross_q,
    cross_kv,
    cross_out,
    ffn_in,
    ffn_out,
    norm_gains,
    norm_biases,
    grad_out,
):
    both = ("dp", "mem")
    row_count, model_width = target_in.shape
    shard_rows = self_qkv.shape[0]
    outer = lax.axis_size("dp") // 4
    staged = shard_rows % 16 == 0 and shard_rows <= LANES and model_width % LANES == 0
    bits = place_bits()
    own_index = lax.axis_index("mem")
    slot_count, mem_piece = memory_in.shape[3], memory_in.shape[4]

    norm_shard = jnp.concatenate((norm_gains, norm_biases), axis=1)
    norm_columns = norm_shard.shape[1]
    norm_shard = jnp.pad(norm_shard, ((0, 0), (0, LANES - norm_columns)))

    def gather(parts, cut, direct=False):
        shard = jnp.concatenate([part.astype(BF16) for part in parts], axis=1)
        widths = [part.shape[1] for part in parts]
        starts = [sum(widths[:i]) for i in range(len(widths))]
        if staged:
            wave = Wave(shard, sum(widths[:cut]) if cut else widths[0] // 2, direct)
            return [Weight(wave, at, size) for at, size in zip(starts, widths)]
        full = lax.all_gather(shard, both, axis=0, tiled=True)
        rows = full.shape[0] // 32
        return [
            Weight(None, 0, size, full[:, at : at + size].reshape(4, 2, 2, 2, rows, size))
            for at, size in zip(starts, widths)
        ]

    def give(source, cotangent):
        if staged:
            return weight_grad(bits, source, cotangent, outer)
        return lead_dot(jnp.concatenate(source, axis=0), cotangent).astype(BF16)

    def spread(parts, direct=False):
        if not staged:
            return lax.psum_scatter(
                parts[0] if len(parts) == 1 else jnp.concatenate(parts, axis=-1),
                both,
                scatter_dimension=0,
                tiled=True,
            ).astype(F32)
        own, other = (
            parts[0]
            if len(parts) == 1
            else [jnp.concatenate([part[side] for part in parts], axis=-1) for side in range(2)]
        )
        return scatter_pieces(own, other, own.shape[-1] // 2 // LANES * LANES, direct)

    def at_mem(values, index):
        return lax.dynamic_index_in_dim(values, index, 0, False)

    mem_rows = memory_in[0, :, 0]
    mem_live = memory_mask[0, :, 0]
    near_rows = at_mem(mem_rows, own_index)
    near_live = at_mem(mem_live, own_index)
    far_rows = swap_mem(at_mem(mem_rows, 1 - own_index))
    far_live = swap_mem(at_mem(mem_live, 1 - own_index))

    (w_qkv,) = gather((self_qkv,), 0, True)
    w_cq, w_co, w_norm, w_ckv, w_so = gather((cross_q, cross_out, norm_shard, cross_kv, self_out), 3)
    (w_in,) = gather((ffn_in,), 0)
    (w_out,) = gather((ffn_out,), 0)

    bucket = pick_entry(bucket_ids[0], own_index)
    lengths = target_lengths[0, 0]
    self_meta = jnp.stack([jnp.right_shift(jnp.int32(row_count), bucket), lengths[0], lengths[1]])
    cross_meta = bucket[None]
    live = jnp.concatenate((near_live, far_live), axis=1)
    key_bias = jnp.where(live == 1, 0.0, NEG_LARGE).astype(F32)
    key_columns = jnp.broadcast_to(key_bias[:, :, None], (*key_bias.shape, LANES))
    near_flat = near_rows.reshape(-1, model_width)
    far_flat = far_rows.reshape(-1, model_width)
    slotted = (slot_count, mem_piece, 2 * model_width)

    (united,) = project("self_project", bits, w_qkv, [target_in], 512)
    self_mixed, self_log = self_forward(self_meta, united)
    table = norm_table(bits, w_norm)
    near_kv, far_kv = project("cross_project", bits, w_ckv, [near_flat, far_flat], 512)
    near_kv, far_kv = near_kv.reshape(slotted), far_kv.reshape(slotted)
    sum_one, first_out, first_low, cross_query = mix_norm(
        "self_mix", bits, w_so, self_mixed, target_in, table, 0, w_cq
    )
    cross_mixed, cross_log = cross_forward(
        cross_meta, cross_query, near_kv, far_kv, key_bias[:, None, :]
    )
    sum_two, second_out, second_low = mix_norm(
        "cross_mix", bits, w_co, cross_mixed, first_out, table, 1
    )
    activated, slope = feed_in(bits, w_in, second_low)
    layer_out, grad_three, grad_ffn, stats_three = feed_out(
        bits, w_out, activated, second_out, table, grad_out
    )

    out_shard = spread([give([activated], grad_ffn)])
    grad_hidden = feed_back(bits, w_out, grad_ffn, slope)
    in_shard = spread([give([second_low], grad_hidden)])
    grad_two, grad_cross_out, grad_cross_mixed, stats_two = norm_back(
        "cross_back", bits, w_in, grad_hidden, grad_three, sum_two, table, 1, w_co
    )
    co_grad = give([cross_mixed], grad_cross_out)
    grad_query_low, grad_kv = cross_backward(
        cross_meta,
        cross_query,
        near_kv,
        far_kv,
        key_columns,
        cross_mixed,
        grad_cross_mixed,
        cross_log,
    )
    cq_grad = give([first_low], grad_query_low)
    ckv_grad = give([near_flat, far_flat], grad_kv)
    first_shards = spread([co_grad, cq_grad, ckv_grad])
    grad_memory = input_back("memory_back", bits, w_ckv, grad_kv, None, model_width)
    half_rows = near_flat.shape[0]
    grad_near = grad_memory[:half_rows].reshape(near_rows.shape)
    grad_far = swap_mem(grad_memory[half_rows:].reshape(near_rows.shape))
    grad_pair = jnp.stack((grad_near, grad_far))
    memory_grad = jnp.where(own_index == 0, grad_pair, grad_pair[::-1])[None, :, None]

    grad_one, grad_self_out, grad_self_mixed, stats_one = norm_back(
        "self_back", bits, w_cq, grad_query_low, grad_two, sum_one, table, 0, w_so
    )
    stats = [jnp.sum(s.reshape(2, 8, model_width), axis=1) for s in (stats_one, stats_two, stats_three)]
    norm_grads = jnp.stack([s[0] for s in stats] + [s[1] for s in stats], axis=1).astype(BF16)
    norm_grads = jnp.pad(norm_grads, ((0, 0), (0, LANES - norm_columns)))
    if staged:
        norm_grads = relative_rows(bits, norm_grads, outer)
    so_shard = spread([give([self_mixed], grad_self_out), norm_grads])
    grad_united = self_backward(self_meta, united, self_mixed, grad_self_mixed, self_log)
    qkv_shard = spread([give([target_in], grad_united)], True)
    target_grad = input_back(
        "target_back", bits, w_qkv, grad_united, grad_one, w_qkv.width // 2
    )

    return (
        layer_out,
        target_grad,
        memory_grad,
        qkv_shard,
        so_shard[:, :model_width],
        first_shards[:, model_width : 2 * model_width],
        first_shards[:, 2 * model_width :],
        first_shards[:, :model_width],
        in_shard,
        out_shard,
        so_shard[:, model_width : model_width + 3],
        so_shard[:, model_width + 3 : model_width + norm_columns],
    )


def solution(mesh):
    rows = P(("dp", "mem"), None)
    memory = P("dp", None, "mem", None, None, None)
    return jax.shard_map(
        per_device,
        mesh=mesh,
        in_specs=(
            rows,
            memory,
            P("dp", None),
            P("dp", "mem", None),
            P("dp", None, "mem", None, None),
        )
        + (rows,) * 10,
        out_specs=(rows, rows, memory) + (rows,) * 9,
        check_vma=False,
    )
```

```python
import math

import jax
import jax.numpy as jnp
from jax import lax
from jax.experimental import pallas as pl
from jax.experimental.pallas import tpu as pltpu
from jax.sharding import PartitionSpec as P

HD = 64
LANES = 128
ALPHA = 300.0**0.25
NEG_LARGE = -1e30
EPSILON = 1e-05
VMEM_BYTES = 62 * 1024 * 1024
SCALE = HD**-0.5
BF16 = jnp.bfloat16
F32 = jnp.float32


def plain_dot(first_op, second_op):
    return jnp.dot(first_op, second_op, preferred_element_type=F32)


def lead_dot(first_op, second_op):
    return lax.dot_general(
        first_op, second_op, (((0,), (0,)), ((), ())), preferred_element_type=F32
    )


def back_dot(first_op, second_op):
    return lax.dot_general(
        first_op, second_op, (((1,), (1,)), ((), ())), preferred_element_type=F32
    )


def pick_entry(values, wanted):
    return jnp.sum(jnp.where(jnp.arange(values.shape[0]) == wanted, values, 0))


def kernel_params():
    return pltpu.CompilerParams(vmem_limit_bytes=VMEM_BYTES)


class Order:
    def __init__(self):
        self.last, self.due, self.parted = None, [], False

    def before(self, *arrays):
        self.due += arrays

    def part(self):
        self.parted = True

    def launch(self, kernel, name, operands, in_specs, out_specs, out_shape, scratch, grid, aliases):
        ties = self.due + ([self.last] if self.last is not None else [])
        ties = [tie for tie in ties if not any(tie is operand for operand in operands)]
        self.due = []
        count, n_ties = len(operands), len(ties)

        def tied(*refs):
            kernel(*refs[:count], *refs[count + n_ties :])

        specs = list(in_specs) + [pl.BlockSpec(memory_space=pltpu.HBM)] * n_ties
        cost = pl.CostEstimate(
            flops=10**12 if self.parted else 10**6, bytes_accessed=1, transcendentals=0
        )
        self.parted = False
        if grid is None:
            run = pl.pallas_call(
                tied,
                in_specs=[pl.BlockSpec(memory_space=pltpu.SMEM)] + specs,
                out_specs=out_specs,
                out_shape=out_shape,
                scratch_shapes=scratch,
                input_output_aliases=aliases,
                compiler_params=kernel_params(),
                cost_estimate=cost,
                name=name,
            )
        else:
            run = pl.pallas_call(
                tied,
                grid_spec=pltpu.PrefetchScalarGridSpec(
                    num_scalar_prefetch=1,
                    grid=grid,
                    in_specs=specs,
                    out_specs=out_specs,
                    scratch_shapes=scratch,
                ),
                out_shape=out_shape,
                input_output_aliases=aliases,
                compiler_params=kernel_params(),
                cost_estimate=cost,
                name=name,
            )
        results = run(*operands, *ties)
        self.last = results[0]
        return results


def whole_spec(shape):
    return pl.BlockSpec(shape, lambda *_: (0,) * len(shape))


def head_lanes(rows, head):
    lane = lax.broadcasted_iota(jnp.int32, (rows, LANES), 1)
    return (lane < HD) if head == 0 else (lane >= HD)


def visible(query_ids, key_ids, slot_len, first_len, second_len):
    query_slot = (query_ids >= slot_len).astype(jnp.int32)
    key_slot = (key_ids >= slot_len).astype(jnp.int32)
    place = key_ids - key_slot * slot_len
    limit = jnp.where(key_slot == 0, first_len, second_len)
    return (query_slot == key_slot) & (key_ids <= query_ids) & (place < limit)


def pair_forward(query, keys, values, bias):
    rows, key_rows = query.shape[0], keys.shape[0]
    mixed, peaks = [], []
    for head in range(2):
        mine = head_lanes(rows, head)
        masked = jnp.where(mine, query * BF16(SCALE), BF16(0))
        scores = back_dot(masked, keys) + bias
        peak = jnp.max(scores, axis=1, keepdims=True)
        raised = jnp.exp(scores - peak).astype(BF16)
        widened = jnp.where(head_lanes(key_rows, head), values, BF16(1))
        mixed.append(plain_dot(raised, widened))
        peaks.append(peak)
    first = head_lanes(rows, 0)
    totals = pltpu.roll(jnp.where(first, mixed[1], mixed[0]), HD, 1)
    joined = jnp.where(first, mixed[0], mixed[1])
    log_totals = jnp.where(first, peaks[0], peaks[1]) + jnp.log(totals)
    return joined / totals, log_totals


def pair_backward(query, keys, values, upstream, bias, log_rows, delta_rows):
    rows, key_rows = query.shape[0], keys.shape[0]
    grad_q, grad_k, grad_v = None, None, None
    for head in range(2):
        mine = head_lanes(rows, head)
        masked = jnp.where(mine, query * BF16(SCALE), BF16(0))
        masked_up = jnp.where(mine, upstream, BF16(0))
        scores = back_dot(keys, masked) + bias
        probs = jnp.exp(scores - log_rows[head])
        grad_probs = back_dot(values, masked_up)
        grad_scores = (probs * (grad_probs - delta_rows[head])).astype(BF16)
        part_v = plain_dot(probs.astype(BF16), masked_up)
        part_k = plain_dot(grad_scores, masked)
        masked_keys = jnp.where(head_lanes(key_rows, head), keys, BF16(0))
        part_q = lead_dot(grad_scores, masked_keys)
        grad_q = part_q if grad_q is None else grad_q + part_q
        grad_k = part_k if grad_k is None else grad_k + part_k
        grad_v = part_v if grad_v is None else grad_v + part_v
    return grad_q * SCALE, grad_k, grad_v


def stat_rows(log_block, mixed, upstream):
    log_turned = log_block.T
    products = (mixed.astype(F32) * upstream.astype(F32)).T
    log_rows = [log_turned[:1], log_turned[HD : HD + 1]]
    delta_rows = [jnp.sum(products[h * HD : (h + 1) * HD], axis=0, keepdims=True) for h in range(2)]
    return log_rows, delta_rows


def self_forward_kernel(meta, q_ref, k_ref, v_ref, mixed_ref, log_ref, bias):
    rows = q_ref.shape[0]

    @pl.when(pl.program_id(0) == 0)
    def _():
        query_ids = lax.broadcasted_iota(jnp.int32, (rows, rows), 0)
        key_ids = lax.broadcasted_iota(jnp.int32, (rows, rows), 1)
        seen = visible(query_ids, key_ids, meta[0], meta[1], meta[2])
        bias[...] = jnp.where(seen, 0.0, NEG_LARGE)

    half = rows // 2
    for start, stop in ((0, half), (half, rows)):
        mixed, log_totals = pair_forward(
            q_ref[start:stop, :], k_ref[:stop, :], v_ref[:stop, :], bias[start:stop, :stop]
        )
        mixed_ref[start:stop, :] = mixed.astype(BF16)
        log_ref[start:stop, :] = log_totals


def self_forward(order, meta, united):
    rows, width = united.shape[0], united.shape[1] // 3
    pairs = width // LANES
    spec = lambda third: pl.BlockSpec((rows, LANES), lambda i, _: (0, third * pairs + i))
    return order.launch(
        self_forward_kernel,
        "self_forward",
        [meta, united, united, united],
        [spec(0), spec(1), spec(2)],
        [spec(0), spec(0)],
        [jax.ShapeDtypeStruct((rows, width), kind) for kind in (BF16, F32)],
        [pltpu.VMEM((rows, rows), F32)],
        (pairs,),
        {},
    )


def self_backward_kernel(
    meta, q_ref, k_ref, v_ref, mixed_ref, up_ref, log_ref, grad_ref, bias
):
    rows = q_ref.shape[0]
    width = grad_ref.shape[1] // 3
    pair = pl.program_id(0)

    @pl.when(pair == 0)
    def _():
        key_ids = lax.broadcasted_iota(jnp.int32, (rows, rows), 0)
        query_ids = lax.broadcasted_iota(jnp.int32, (rows, rows), 1)
        seen = visible(query_ids, key_ids, meta[0], meta[1], meta[2])
        bias[...] = jnp.where(seen, 0.0, NEG_LARGE)

    log_rows, delta_rows = stat_rows(log_ref[...], mixed_ref[...], up_ref[...])
    half = rows // 2
    parts = []
    for start, stop in ((0, half), (half, rows)):
        parts.append(
            pair_backward(
                q_ref[start:stop, :],
                k_ref[:stop, :],
                v_ref[:stop, :],
                up_ref[start:stop, :],
                bias[:stop, start:stop],
                [row[:, start:stop] for row in log_rows],
                [row[:, start:stop] for row in delta_rows],
            )
        )
    low, high = parts
    columns = lambda third: pl.ds(pl.multiple_of(third * width + pair * LANES, LANES), LANES)
    grad_ref[:half, columns(0)] = low[0].astype(BF16)
    grad_ref[half:, columns(0)] = high[0].astype(BF16)
    for third in (1, 2):
        grad_ref[:half, columns(third)] = (low[third] + high[third][:half]).astype(BF16)
        grad_ref[half:, columns(third)] = high[third][half:].astype(BF16)


def self_backward(order, meta, united, mixed, upstream, log_totals, first, pairs):
    rows, width = mixed.shape
    third = width // LANES
    spec = lambda at: pl.BlockSpec((rows, LANES), lambda i, _: (0, at * third + first + i))
    shape = (rows, 3 * pairs * LANES)
    return order.launch(
        self_backward_kernel,
        "self_backward",
        [meta, united, united, united, mixed, upstream, log_totals],
        [spec(0), spec(1), spec(2), spec(0), spec(0), spec(0)],
        [whole_spec(shape)],
        [jax.ShapeDtypeStruct(shape, BF16)],
        [pltpu.VMEM((rows, rows), F32)],
        (pairs,),
        {},
    )[0]


def join_keys(near_ref, far_ref, joined):
    slots, piece = near_ref.shape[0], near_ref.shape[1]
    for slot in range(slots):
        joined[slot, :piece, :] = near_ref[slot]
        joined[slot, piece:, :] = far_ref[slot]


def cross_forward_kernel(
    meta, q_ref, kn_ref, vn_ref, kf_ref, vf_ref, bias_ref, mixed_ref, log_ref, keys, values
):
    half = q_ref.shape[0] // 2
    join_keys(kn_ref, kf_ref, keys)
    join_keys(vn_ref, vf_ref, values)
    for part in range(2):
        slot = part * meta[0]
        rows = slice(part * half, (part + 1) * half)
        mixed, log_totals = pair_forward(q_ref[rows, :], keys[slot], values[slot], bias_ref[slot])
        mixed_ref[rows, :] = mixed.astype(BF16)
        log_ref[rows, :] = log_totals


def cross_specs(rows, slots, piece, pairs):
    row_spec = pl.BlockSpec((rows, LANES), lambda i, _: (0, i))
    half = lambda at: pl.BlockSpec((slots, piece, LANES), lambda i, _: (0, 0, at * pairs + i))
    return row_spec, [row_spec, half(0), half(1), half(0), half(1)]


def cross_forward(order, meta, query, near, far, bias):
    rows, width = query.shape
    slots, piece = near.shape[0], near.shape[1]
    pairs = width // LANES
    row_spec, specs = cross_specs(rows, slots, piece, pairs)
    return order.launch(
        cross_forward_kernel,
        "cross_forward",
        [meta, query, near, near, far, far, bias],
        specs + [whole_spec(bias.shape)],
        [row_spec, row_spec],
        [jax.ShapeDtypeStruct((rows, width), kind) for kind in (BF16, F32)],
        [pltpu.VMEM((slots, 2 * piece, LANES), BF16)] * 2,
        (pairs,),
        {},
    )


def cross_backward_kernel(
    meta,
    q_ref,
    kn_ref,
    vn_ref,
    kf_ref,
    vf_ref,
    bias_ref,
    mixed_ref,
    up_ref,
    log_ref,
    grad_q_ref,
    grad_near_ref,
    grad_far_ref,
    keys,
    values,
):
    half = q_ref.shape[0] // 2
    slots, piece = kn_ref.shape[0], kn_ref.shape[1]
    width = grad_near_ref.shape[1] // 2
    join_keys(kn_ref, kf_ref, keys)
    join_keys(vn_ref, vf_ref, values)
    log_rows, delta_rows = stat_rows(log_ref[...], mixed_ref[...], up_ref[...])
    parts = []
    for part in range(2):
        slot = part * meta[0]
        rows = slice(part * half, (part + 1) * half)
        bias_column = bias_ref[slot]
        grads = pair_backward(
            q_ref[rows, :],
            keys[slot],
            values[slot],
            up_ref[rows, :],
            jnp.concatenate([bias_column] * (half // LANES), axis=1),
            [row[:, rows] for row in log_rows],
            [row[:, rows] for row in delta_rows],
        )
        grad_q_ref[rows, :] = grads[0].astype(BF16)
        parts.append(grads)
    split = meta[0].astype(F32)
    start = pl.program_id(0) * LANES
    for which in range(2):
        early, late = parts[0][1 + which], parts[1][1 + which]
        columns = pl.ds(pl.multiple_of(which * width + start, LANES), LANES)
        by_slot = (early + late * (1.0 - split), late * split)
        for slot in range(slots):
            for source, target in enumerate((grad_near_ref, grad_far_ref)):
                target[slot * piece : (slot + 1) * piece, columns] = by_slot[slot][
                    source * piece : (source + 1) * piece
                ].astype(BF16)


def cross_backward(order, meta, query, near, far, bias, mixed, upstream, log_totals):
    rows, width = query.shape
    slots, piece = near.shape[0], near.shape[1]
    pairs = width // LANES
    memory = (slots * piece, 2 * width)
    row_spec, specs = cross_specs(rows, slots, piece, pairs)
    return order.launch(
        cross_backward_kernel,
        "cross_backward",
        [meta, query, near, near, far, far, bias, mixed, upstream, log_totals],
        specs + [whole_spec(bias.shape)] + [row_spec] * 3,
        [row_spec, whole_spec(memory), whole_spec(memory)],
        [jax.ShapeDtypeStruct(shape, BF16) for shape in ((rows, width), memory, memory)],
        [pltpu.VMEM((slots, 2 * piece, LANES), BF16)] * 2,
        (pairs,),
        {},
    )


def swap_core(values):
    size = lax.axis_size("dp")
    return lax.ppermute(values, "dp", [(i, i ^ 1) for i in range(size)])


def swap_next(values):
    size = lax.axis_size("dp")
    return lax.ppermute(values, "dp", [(i, i ^ 2) for i in range(size)])


def swap_mem(values):
    return lax.ppermute(values, "mem", [(0, 1), (1, 0)])


def swap_outer(values, far):
    size = lax.axis_size("dp")
    return lax.ppermute(values, "dp", [(i, i ^ (4 * far)) for i in range(size)])


def outer_groups():
    size = lax.axis_size("dp")
    return [list(range(base, size, 4)) for base in range(4)]


def place_bits():
    dp, mem = lax.axis_index("dp"), lax.axis_index("mem")
    return jnp.stack([(dp >> 1) & 1, dp & 1, mem]).astype(jnp.int32)


def outer_gather(shard, direct):
    outer, rows = lax.axis_size("dp") // 4, shard.shape[0]
    if not direct:
        stacked = lax.all_gather(shard, "dp", axis_index_groups=outer_groups(), axis=0, tiled=True)
        return stacked.reshape(outer, rows, -1)
    place = lax.axis_index("dp") >> 2
    blocks = jnp.stack([shard] + [swap_outer(shard, far) for far in range(1, outer)])
    bit = 1
    while bit < outer:
        turned = jnp.stack([blocks[i ^ bit] for i in range(outer)])
        blocks = jnp.where((place & bit) != 0, turned, blocks)
        bit *= 2
    return blocks


FIRST = (swap_next, swap_mem)
SECOND = (swap_mem, swap_next)


def gate(order, bits, arrays):
    def kernel(*refs):
        pass

    return order.launch(
        kernel,
        "gate",
        [bits, *arrays],
        [pl.BlockSpec(memory_space=pltpu.HBM)] * len(arrays),
        [pl.BlockSpec(memory_space=pltpu.HBM)] * len(arrays),
        [jax.ShapeDtypeStruct(array.shape, array.dtype) for array in arrays],
        [],
        None,
        {1 + i: i for i in range(len(arrays))},
    )


class Moves:
    def __init__(self, order, bits):
        self.order, self.bits = order, bits
        self.sources, self.shapes, self.moves, self.aliases, self.then = [], [], [], {}, []

    def source(self, array):
        self.sources.append(array)
        return len(self.sources) - 1

    def target(self, shape, held=None):
        self.shapes.append(shape)
        if held is not None:
            self.aliases[1 + self.source(held)] = len(self.shapes) - 1
        return len(self.shapes) - 1

    def move(self, source, source_at, shape, *goals):
        self.moves.append((source, source_at, shape, goals))

    def run(self):
        moves, n_in, n_out = self.moves, len(self.sources), len(self.shapes)
        most = max(len(move[3]) for move in moves)

        def kernel(bits_ref, *refs):
            bits = [bits_ref[i] for i in range(3)]
            taken, given = refs[:n_in], refs[n_in : n_in + n_out]
            slots, sems = refs[n_in + n_out : -1], refs[-1]
            loads, stores = [], []
            for number, (source, source_at, _, goals) in enumerate(moves):
                slot = slots[number]
                loads.append(
                    pltpu.make_async_copy(taken[source].at[source_at], slot, sems.at[0, number])
                )
                stores.append(
                    [
                        pltpu.make_async_copy(
                            slot, given[which].at[at(bits) if callable(at) else at], sems.at[1 + i, number]
                        )
                        for i, (which, at) in enumerate(goals)
                    ]
                )
            for load in loads:
                load.start()
            for load, group in zip(loads, stores):
                load.wait()
                for store in group:
                    store.start()
            for group in stores:
                for store in group:
                    store.wait()

        filled = self.order.launch(
            kernel,
            "move_blocks",
            [self.bits, *self.sources],
            [pl.BlockSpec(memory_space=pltpu.HBM)] * n_in,
            [pl.BlockSpec(memory_space=pltpu.HBM)] * n_out,
            [jax.ShapeDtypeStruct(shape, BF16) for shape in self.shapes],
            [pltpu.VMEM(shape, BF16) for _, _, shape, _ in moves]
            + [pltpu.SemaphoreType.DMA((1 + most, len(moves)))],
            None,
            self.aliases,
        )
        for step in self.then:
            step(filled)


def cast_shards(order, bits, groups):
    shapes = [(group[0].shape[0], sum(part.shape[1] for part in group)) for group in groups]
    parts = [part for group in groups for part in group]

    def kernel(bits_ref, *refs):
        number = 0
        for group, target in zip(groups, refs[len(parts) :]):
            start = 0
            for part in group:
                stop = start + part.shape[1]
                target[:, start:stop] = refs[number][...].astype(BF16)
                start, number = stop, number + 1

    return order.launch(
        kernel,
        "cast_shards",
        [bits, *parts],
        [pl.BlockSpec(memory_space=pltpu.VMEM)] * len(parts),
        [pl.BlockSpec(memory_space=pltpu.VMEM)] * len(shapes),
        [jax.ShapeDtypeStruct(shape, BF16) for shape in shapes],
        [],
        None,
        {},
    )


class Wave:
    def __init__(self, order, bits, shard, cut, direct):
        self.order, self.bits, self.cut, self.direct = order, bits, cut, direct
        self.rows, self.columns = shard.shape
        self.stacked = outer_gather(shard, direct)
        self.outer = self.stacked.shape[0]
        self.windows = (pl.ds(0, cut), pl.ds(cut, self.columns - cut))

    def first(self, moves):
        def send(parts):
            self.pairs = [(part, FIRST[half](part)) for half, part in enumerate(parts)]

        if self.direct:
            send((self.stacked[:, :, : self.cut], self.stacked[:, :, self.cut :]))
            return
        source = moves.source(self.stacked)
        targets = [moves.target((self.outer, self.rows, w.size)) for w in self.windows]
        for place in range(self.outer):
            for target, window in zip(targets, self.windows):
                shape = (self.rows, window.size)
                moves.move(source, (place, slice(None), window), shape, (target, (place,)))
        moves.then.append(lambda filled: send([filled[target] for target in targets]))

    def place(self, half, second, first, block, window):
        near, mem = (first, second) if half == 0 else (second, first)
        return lambda bits: (block, bits[0] ^ near, bits[2] ^ mem, slice(None), window)

    def second(self, moves):
        sources = [[moves.source(part) for part in pair] for pair in self.pairs]
        targets = [moves.target((2, *pair[0].shape)) for pair in self.pairs]
        own = moves.target((self.outer, 2, 2, self.rows, self.columns))
        for block in range(self.outer):
            for half, window in enumerate(self.windows):
                for side in range(2):
                    goal = (targets[half], (side, block))
                    again = (own, self.place(half, 0, side, block, window))
                    shape = (self.rows, window.size)
                    moves.move(sources[half][side], (block,), shape, goal, again)

        def send(filled):
            self.own = filled[own]
            self.far = [SECOND[half](filled[target]) for half, target in enumerate(targets)]

        moves.then.append(send)

    def third(self, moves):
        own = moves.target(self.own.shape, self.own)
        for half, window in enumerate(self.windows):
            source = moves.source(self.far[half])
            for block in range(self.outer):
                for side in range(2):
                    goal = (own, self.place(half, 1, side, block, window))
                    moves.move(source, (side, block), (self.rows, window.size), goal)

        def send(filled):
            shape = (2 * self.outer, 2 * self.rows, self.columns)
            self.own = filled[own].reshape(shape)
            self.other = swap_core(self.own)

        moves.then.append(send)


class Weight:
    def __init__(self, wave, start, width, whole=None):
        self.wave, self.start, self.width, self.whole = wave, start, width, whole
        if whole is not None:
            self.blocks, self.rows = whole.shape[0], whole.shape[2]
        else:
            self.blocks, self.rows = 2 * wave.outer, 2 * wave.rows
        self.features = self.blocks * 2 * self.rows

    def pieces(self):
        return [self.whole] if self.whole is not None else [self.wave.own, self.wave.other]

    def copies(self, kind, start, size, bits, find, target):
        if kind == "columns":
            blocks, columns = slice(None), pl.ds(self.start + start, size)
        else:
            blocks, columns = pl.ds(start, size), pl.ds(self.start, self.width)
        if self.whole is not None:
            return [(find(self.whole).at[blocks, :, :, columns], target)]
        return [
            (find(array).at[blocks, :, columns], target.at[:, bits[1] ^ core])
            for core, array in enumerate((self.wave.own, self.wave.other))
        ]


def weight_call(order, name, bits, weights, plan, inputs, outs, scratch, body):
    arrays = []
    for weight in weights:
        arrays += [a for a in weight.pieces() if not any(a is b for b in arrays)]
    kind, size = plan[0][1], plan[0][3]
    lead = weights[plan[0][0]]
    if kind == "columns":
        chunk = (lead.blocks, 2, lead.rows, size)
    else:
        chunk = (size, 2, lead.rows, lead.width)
    n_in, n_arrays, n_out = len(inputs), len(arrays), len(outs)

    def kernel(bits_ref, *refs):
        ins, refs = refs[:n_in], refs[n_in:]
        pieces, refs = refs[:n_arrays], refs[n_arrays:]
        out_refs, refs = refs[:n_out], refs[n_out:]
        held, sems = refs[-2:]
        bits_now = [bits_ref[i] for i in range(3)]

        def find(array):
            return next(ref for ref, known in zip(pieces, arrays) if known is array)

        def issue(number):
            which, kind, start, size = plan[number]
            slot = number % 2
            for source, target in weights[which].copies(
                kind, start, size, bits_now, find, held.at[slot]
            ):
                pltpu.make_async_copy(source, target, sems.at[slot]).start()

        taken = [0]

        def fetch():
            number = taken[0]
            taken[0] += 1
            if number + 1 < len(plan):
                issue(number + 1)
            slot = number % 2
            pltpu.make_async_copy(held.at[slot], held.at[slot], sems.at[slot]).wait()
            return held[slot].reshape(-1, chunk[-1])

        issue(0)
        body(fetch, ins, out_refs, refs[:-2])

    return order.launch(
        kernel,
        name,
        [bits, *inputs, *arrays],
        [pl.BlockSpec(memory_space=pltpu.VMEM)] * n_in
        + [pl.BlockSpec(memory_space=pltpu.HBM)] * n_arrays,
        [pl.BlockSpec(memory_space=pltpu.VMEM)] * n_out,
        [jax.ShapeDtypeStruct(shape, kind) for shape, kind in outs],
        [pltpu.VMEM(shape, kind) for shape, kind in scratch]
        + [pltpu.VMEM((2, *chunk), BF16), pltpu.SemaphoreType.DMA((2,))],
        None,
        {},
    )


def columns_plan(which, width, size):
    return [(which, "columns", start, size) for start in range(0, width, size)]


def row_blocks(rows, size, step):
    def run(i, carry):
        step(pl.ds(pl.multiple_of(i * size, size), size))
        return carry

    lax.fori_loop(0, rows // size, run, 0)


def normed_parts(values):
    centred = values - jnp.mean(values, axis=-1, keepdims=True)
    spread = jnp.mean(centred * centred, axis=-1, keepdims=True)
    rate = lax.rsqrt(spread + EPSILON)
    return centred * rate, rate


def norm_gradient(normed, rate, gain, cotangent):
    inner = cotangent * gain
    mean_inner = jnp.mean(inner, axis=-1, keepdims=True)
    mean_both = jnp.mean(inner * normed, axis=-1, keepdims=True)
    return rate * (inner - mean_inner - normed * mean_both)


def add_stats(stats, normed, cotangent):
    fold = lambda values: jnp.sum(values.reshape(-1, 8, values.shape[-1]), axis=0)
    stats[:8, :] += fold(cotangent * normed)
    stats[8:, :] += fold(cotangent)


def norm_table(order, bits, weight):
    features = weight.features

    def body(fetch, ins, outs, scratch):
        outs[0][...] = fetch().astype(F32).T[:8]

    return weight_call(
        order, "norm_table", bits, [weight], [(0, "columns", 0, LANES)], [],
        [((8, features), F32)], [], body,
    )[0]


def project(order, name, bits, weight, sources, size):
    def body(fetch, ins, outs, scratch):
        for start in range(0, weight.width, size):
            chunk = fetch()
            for source, target in zip(ins, outs):
                target[:, start : start + size] = plain_dot(source[...], chunk).astype(BF16)

    return weight_call(
        order, name, bits, [weight], columns_plan(0, weight.width, size), sources,
        [((source.shape[0], weight.width), BF16) for source in sources], [], body,
    )


def mix_norm(order, name, bits, weight, mixed, residual, table, index, query_weight=None):
    rows, width = mixed.shape
    size = min(1024, width)

    def body(fetch, ins, outs, scratch):
        mixed_ref, residual_ref, table_ref = ins
        summed, out, out_low = outs[:3]
        for start in range(0, width, size):
            part = plain_dot(mixed_ref[...], fetch())
            columns = slice(start, start + size)
            summed[:, columns] = ALPHA * residual_ref[:, columns].astype(F32) + part
        gain, shift = table_ref[index : index + 1, :], table_ref[3 + index : 4 + index, :]

        def step(block):
            normed, _ = normed_parts(summed[block, :])
            values = normed * gain + shift
            out[block, :] = values
            out_low[block, :] = values.astype(BF16)

        row_blocks(rows, 128, step)
        if query_weight is not None:
            for start in range(0, width, size):
                part = plain_dot(out_low[...], fetch())
                outs[3][:, start : start + size] = part.astype(BF16)

    weights = [weight] + ([query_weight] if query_weight is not None else [])
    plan = [entry for i in range(len(weights)) for entry in columns_plan(i, width, size)]
    outs = [((rows, width), F32), ((rows, width), F32), ((rows, width), BF16)]
    if query_weight is not None:
        outs.append(((rows, width), BF16))
    return weight_call(
        order, name, bits, weights, plan, [mixed, residual, table], outs, [], body
    )


def feed_in(order, bits, weight, source):
    rows, size = source.shape[0], 1024

    def body(fetch, ins, outs, scratch):
        held = scratch[0]
        for start in range(0, weight.width, size):
            held[...] = plain_dot(ins[0][...], fetch())

            def step(block):
                hidden = held[block, :]
                below = 0.5 + 0.5 * lax.erf(hidden * (0.5**0.5))
                density = jnp.exp(-0.5 * hidden * hidden) * (2.0 * jnp.pi) ** -0.5
                outs[0][block, start : start + size] = (hidden * below).astype(BF16)
                outs[1][block, start : start + size] = (below + hidden * density).astype(BF16)

            row_blocks(rows, 256, step)

    out = ((rows, weight.width), BF16)
    return weight_call(
        order, "feed_in", bits, [weight], columns_plan(0, weight.width, size), [source], [out, out],
        [((rows, size), F32)], body,
    )


def feed_out(order, bits, weight, activated, residual, table, cotangent):
    rows, width = residual.shape
    size = 512 if width % 512 == 0 else width

    def body(fetch, ins, outs, scratch):
        act_ref, residual_ref, table_ref, up_ref = ins
        layer_out, grad, grad_low, stats = outs
        summed = scratch[0]
        for start in range(0, width, size):
            columns = slice(start, start + size)
            part = plain_dot(act_ref[...], fetch())
            summed[:, columns] = ALPHA * residual_ref[:, columns] + part
        gain, shift = table_ref[2:3, :], table_ref[5:6, :]
        stats[...] = jnp.zeros_like(stats)

        def step(block):
            normed, rate = normed_parts(summed[block, :])
            layer_out[block, :] = (normed * gain + shift).astype(BF16)
            upstream = up_ref[block, :].astype(F32)
            values = norm_gradient(normed, rate, gain, upstream)
            grad[block, :] = values
            grad_low[block, :] = values.astype(BF16)
            add_stats(stats, normed, upstream)

        row_blocks(rows, 128, step)

    outs = [((rows, width), BF16), ((rows, width), F32), ((rows, width), BF16), ((16, width), F32)]
    return weight_call(
        order, "feed_out", bits, [weight], columns_plan(0, width, size),
        [activated, residual, table, cotangent], outs, [((rows, width), F32)], body,
    )


def feed_back(order, bits, weight, cotangent, slope):
    rows, features = slope.shape
    size = 1024 if features % 1024 == 0 else features
    steps = features // size

    def body(fetch, ins, outs, scratch):
        for number in range(steps):
            part = back_dot(ins[0][...], fetch())
            columns = slice(number * size, (number + 1) * size)
            outs[0][:, columns] = (part * ins[1][:, columns].astype(F32)).astype(BF16)

    blocks = weight.blocks // steps
    return weight_call(
        order, "feed_back", bits, [weight], [(0, "rows", i * blocks, blocks) for i in range(steps)],
        [cotangent, slope], [((rows, features), BF16)], [], body,
    )[0]


def norm_back(order, name, bits, weight, cotangent, carried, summed, table, index, mix_weight):
    rows, width = summed.shape
    size = min(1024, weight.width)

    def body(fetch, ins, outs, scratch):
        up_ref, carried_ref, summed_ref, table_ref = ins
        grad, grad_low, grad_mixed, stats = outs
        total = scratch[0]
        for start in range(0, weight.width, size):
            part = back_dot(up_ref[:, start : start + size], fetch())
            total[...] = part + (ALPHA * carried_ref[...] if start == 0 else total[...])
        gain = table_ref[index : index + 1, :]
        stats[...] = jnp.zeros_like(stats)

        def step(block):
            normed, rate = normed_parts(summed_ref[block, :])
            upstream = total[block, :]
            values = norm_gradient(normed, rate, gain, upstream)
            grad[block, :] = values
            grad_low[block, :] = values.astype(BF16)
            add_stats(stats, normed, upstream)

        row_blocks(rows, 128, step)
        grad_mixed[...] = back_dot(grad_low[...], fetch()).astype(BF16)

    outs = [((rows, width), F32), ((rows, width), BF16), ((rows, width), BF16), ((16, width), F32)]
    return weight_call(
        order, name, bits, [weight, mix_weight],
        columns_plan(0, weight.width, size) + columns_plan(1, width, size),
        [cotangent, carried, summed, table], outs, [((rows, width), F32)], body,
    )


def input_back(order, name, bits, weight, cotangents, carried, spans):
    rows, features = cotangents[0].shape[0], weight.features
    step = 512 if rows % 512 == 0 else rows // 2
    count = len(cotangents)

    def body(fetch, ins, outs, scratch):
        for number, (which, first, _, size) in enumerate(spans):
            chunk = fetch()
            for row in range(0, rows, step):
                block = slice(row, row + step)
                part = back_dot(ins[which][block, first : first + size], chunk)
                if number == 0 and carried is not None:
                    part += ALPHA * ins[count][block, :]
                elif number > 0:
                    part += scratch[0][block, :]
                if number == len(spans) - 1:
                    outs[0][block, :] = part.astype(BF16)
                else:
                    scratch[0][block, :] = part

    return weight_call(
        order, name, bits, [weight], [(0, "columns", start, size) for _, _, start, size in spans],
        [*cotangents] + ([carried] if carried is not None else []),
        [((rows, features), BF16)], [((rows, features), F32)], body,
    )[0]


def turn_rows(order, bits, sources, outer):
    features = sources[0].shape[1]
    total_rows = sum(source.shape[0] for source in sources)
    shard_rows = features // (8 * outer)

    def kernel(bits_ref, *refs):
        targets, filled = refs[len(sources) :], 0
        for ref in refs[: len(sources)]:
            stop = filled + ref.shape[0]
            for block in range(features // LANES):
                turned_block = ref[:, block * LANES : (block + 1) * LANES].T
                for part in range(LANES // shard_rows):
                    device = block * (LANES // shard_rows) + part
                    mem, core, near = device & 1, (device >> 1) & 1, (device >> 2) & 1
                    place = (mem ^ bits_ref[2]) * 2 + (near ^ bits_ref[0])
                    place = place * outer + (device >> 3)
                    rows = pl.ds(pl.multiple_of(place * shard_rows, shard_rows), shard_rows)
                    values = turned_block[part * shard_rows : (part + 1) * shard_rows]
                    side = core ^ bits_ref[1]

                    @pl.when(side == 0)
                    def _():
                        targets[0][rows, filled:stop] = values

                    @pl.when(side == 1)
                    def _():
                        targets[1][rows, filled:stop] = values

            filled = stop

    return order.launch(
        kernel,
        "turn_rows",
        [bits, *sources],
        [pl.BlockSpec(memory_space=pltpu.VMEM)] * len(sources),
        [pl.BlockSpec(memory_space=pltpu.VMEM)] * 2,
        [jax.ShapeDtypeStruct((features // 2, total_rows), BF16)] * 2,
        [],
        None,
        {},
    )


def weight_grad(
    order, bits, turned, cotangents, outer, cut, extra=None, held=None, place=None
):
    half_features = turned[0][0].shape[0]
    each, width = cotangents[0].shape
    n_turned = len(turned)
    n_grads = len(cotangents)
    total_rows = n_grads // 2 * each
    shard_rows = half_features // (4 * outer)
    chunk = 512 if cut is None or cut % 512 == 0 else 256
    added = 0 if extra is None else LANES
    n_held = 2 if held is not None else 0
    if place is None:
        halves = [(0, 0, cut // chunk, cut), (1, 0, (width - cut) // chunk, width - cut)]
    else:
        halves = [(place[0], place[1] // chunk, width // chunk, place[2])]
    steps = [count for _, _, count, _ in halves]
    first_steps = [sum(steps[:i]) for i in range(len(steps))]

    def kernel(bits_ref, *refs):
        n_in = n_turned + n_grads
        targets = refs[n_in + n_held + (len(halves) if added else 0) :]
        step = pl.program_id(0)
        features = jnp.concatenate([ref[...] for ref in refs[:n_turned]], axis=1)
        grads = jnp.concatenate([ref[...] for ref in refs[n_turned:n_in]], axis=0)
        product = plain_dot(features, grads)
        blocks = product.astype(BF16).reshape(2, 2, outer, shard_rows, chunk)
        for number, (half, _, count, _) in enumerate(halves):

            @pl.when((step >= first_steps[number]) & (step < first_steps[number] + count))
            def _():
                for side in range(2):
                    target = targets[2 * number + side]
                    picked = blocks[1 - side] if half == 0 else blocks[:, 1 - side]
                    target[..., :chunk] = picked
                    if added:
                        beside = refs[n_in + number]
                        picked = beside[1 - side] if half == 0 else beside[:, 1 - side]
                        target[..., chunk:] = picked

    def out_spec(number):
        _, first, count, _ = halves[number]
        at = lambda i, _: (0, 0, 0, first + jnp.clip(i - first_steps[number], 0, count - 1))
        return pl.BlockSpec((2, outer, shard_rows, chunk + added), at)

    def turned_spec(start, size):
        return pl.BlockSpec((half_features, size), lambda i, _: (0, start // size))

    whole = (2, 2, outer, shard_rows, LANES)
    specs = [turned_spec(start, size) for _, start, size in turned]
    specs += [pl.BlockSpec((each, chunk), lambda i, _: (0, i))] * n_grads
    specs += [pl.BlockSpec(memory_space=pltpu.HBM)] * n_held
    specs += [whole_spec(whole)] * (len(halves) if added else 0)
    return order.launch(
        kernel,
        "weight_grad",
        [bits, *(part for part, _, _ in turned), *cotangents, *(held or ()), *(extra or ())],
        specs,
        [out_spec(number) for number in range(len(halves)) for _ in range(2)],
        [
            jax.ShapeDtypeStruct((2, outer, shard_rows, columns + added), BF16)
            for _, _, _, columns in halves
            for _ in range(2)
        ],
        [],
        (sum(steps),),
        {1 + n_turned + n_grads: 0, 2 + n_turned + n_grads: 1} if n_held else {},
    )


def relative_rows(bits, values, outer):
    rows = values.shape[0] // (8 * outer)
    blocks = values.reshape(outer, 2, 2, 2, rows, -1)
    for axis, bit in ((1, bits[0]), (2, bits[1]), (3, bits[2])):
        blocks = jnp.where(bit == 1, jnp.flip(blocks, axis), blocks)
    blocks = blocks.transpose(2, 3, 1, 0, 4, 5)
    return blocks[0], blocks[1]


def add_blocks(order, bits, sums, shapes):
    arrays = []
    for group, _, _ in sums:
        arrays += [a for a, _ in group if not any(a is b for b in arrays)]
    blocks = [group[0][0].shape[-3:] for group, _, _ in sums]
    find = lambda array: next(i for i, known in enumerate(arrays) if known is array)
    chunks = [(number, place) for place in range(blocks[0][0]) for number in range(len(sums))]

    def kernel(bits_ref, *refs):
        sources, refs = refs[: len(arrays)], refs[len(arrays) :]
        targets, refs = refs[: len(shapes)], refs[len(shapes) :]
        held, summed, (load_sems, store_sems) = refs[: len(sums)], refs[len(sums) : -2], refs[-2:]
        loads, stores = [], []
        for index, (number, place) in enumerate(chunks):
            loads.append([])
            for term, (array, at) in enumerate(sums[number][0]):
                load = pltpu.make_async_copy(
                    sources[find(array)].at[(*at, place)],
                    held[number].at[term, place],
                    load_sems.at[index, term],
                )
                load.start()
                loads[-1].append(load)
        for index, (number, place) in enumerate(chunks):
            group, which, column = sums[number]
            for load in loads[index]:
                load.wait()
            values = [held[number][term, place].astype(F32) for term in range(len(group))]
            summed[number][place] = sum(values[1:], values[0]).astype(BF16)
            store = pltpu.make_async_copy(
                summed[number].at[place],
                targets[which].at[place, :, pl.ds(column, blocks[number][2])],
                store_sems.at[index],
            )
            store.start()
            stores.append(store)
        for store in stores:
            store.wait()

    most = max(len(group) for group, _, _ in sums)
    return order.launch(
        kernel,
        "add_blocks",
        [bits, *arrays],
        [pl.BlockSpec(memory_space=pltpu.HBM)] * len(arrays),
        [pl.BlockSpec(memory_space=pltpu.HBM)] * len(shapes),
        [jax.ShapeDtypeStruct(shape, BF16) for shape in shapes],
        [pltpu.VMEM((len(group), *block), BF16) for (group, _, _), block in zip(sums, blocks)]
        + [pltpu.VMEM(block, BF16) for block in blocks]
        + [
            pltpu.SemaphoreType.DMA((len(chunks), most)),
            pltpu.SemaphoreType.DMA((len(chunks),)),
        ],
        None,
        {},
    )


class Spread:
    def __init__(self, parts):
        self.kept = (parts[1], parts[3])
        self.once = [FIRST_BACK[half](parts[2 * half]) for half in range(2)]

    def second(self):
        return [[(self.kept[half], (1,)), (self.once[half], (1,))] for half in range(2)]

    def send(self, sent):
        self.twice = [SECOND_BACK[half](part) for half, part in enumerate(sent)]

    def third(self):
        return [
            [(self.kept[half], (0,)), (self.once[half], (0,)), (self.twice[half], ())]
            for half in range(2)
        ]


def block_shape(group):
    return group[0][0].shape[-3:]


def spread_steps(order, bits, seconds, thirds, together=False):
    sums, shapes = [], []
    for wave in seconds:
        for group in wave.second():
            sums.append((group, len(shapes), 0))
            shapes.append(block_shape(group))
    joined = len(shapes)
    for number, wave in enumerate(thirds):
        if number == 0 or not together:
            shapes.append((*block_shape(wave.third()[0])[:2], 0))
        for group in wave.third():
            outer, rows, columns = shapes[-1]
            sums.append((group, len(shapes) - 1, columns))
            shapes[-1] = (outer, rows, columns + block_shape(group)[2])
    filled = add_blocks(order, bits, sums, shapes)
    for number, wave in enumerate(seconds):
        wave.send(filled[2 * number : 2 * number + 2])
    return filled[joined:]


def outer_sum(joined):
    joined = joined.reshape(-1, joined.shape[-1])
    return lax.psum_scatter(
        joined, "dp", axis_index_groups=outer_groups(), scatter_dimension=0, tiled=True
    )


def outer_sum_direct(joined):
    place = lax.axis_index("dp") >> 2
    block = lambda far: lax.dynamic_index_in_dim(joined, place ^ far, 0, False)
    parts = [block(0)] + [swap_outer(block(far), far) for far in range(1, joined.shape[0])]
    return sum(part.astype(F32) for part in parts)


FIRST_BACK = (swap_mem, swap_next)
SECOND_BACK = (swap_next, swap_mem)


def per_device(
    target_in,
    memory_in,
    bucket_ids,
    target_lengths,
    memory_mask,
    self_qkv,
    self_out,
    cross_q,
    cross_kv,
    cross_out,
    ffn_in,
    ffn_out,
    norm_gains,
    norm_biases,
    grad_out,
):
    both = ("dp", "mem")
    row_count, model_width = target_in.shape
    shard_rows = self_qkv.shape[0]
    outer = lax.axis_size("dp") // 4
    staged = shard_rows % 16 == 0 and shard_rows <= LANES and model_width % LANES == 0
    bits = place_bits()
    order = Order()
    own_index, pieces = lax.axis_index("mem"), lax.axis_size("mem")
    slot_count, mem_piece = memory_in.shape[3], memory_in.shape[4]

    norm_shard = jnp.concatenate((norm_gains, norm_biases), axis=1)
    norm_columns = norm_shard.shape[1]
    norm_shard = jnp.pad(norm_shard, ((0, 0), (0, LANES - norm_columns)))

    groups = [
        (self_qkv,),
        (cross_q, cross_out, norm_shard, cross_kv, self_out),
        (ffn_in,),
        (ffn_out,),
    ]
    if staged:
        shards = cast_shards(order, bits, groups[:1])
    else:
        shards = [jnp.concatenate([part.astype(BF16) for part in group], axis=1) for group in groups]

    def gather(index, cut, direct=False):
        shard = shards[index]
        widths = [part.shape[1] for part in groups[index]]
        starts = [sum(widths[:i]) for i in range(len(widths))]
        if staged:
            wave = Wave(order, bits, shard, cut, direct)
            return [Weight(wave, at, size) for at, size in zip(starts, widths)]
        full = lax.all_gather(shard, both, axis=0, tiled=True)
        rows = full.shape[0] // 16
        return [
            Weight(None, 0, size, full[:, at : at + size].reshape(8, 2, rows, size))
            for at, size in zip(starts, widths)
        ]

    def whole_sum(gradient):
        return lax.psum_scatter(gradient, both, scatter_dimension=0, tiled=True).astype(F32)

    class Turned:
        def __init__(self, *sources):
            self.sources = sources
            own, other = turn_rows(order, bits, sources, outer) if staged else (None, None)
            self.both = (own, swap_core(other)) if staged else ()

        def due(self):
            order.before(*self.both[1:])

    class Grad:
        def __init__(self, *places):
            self.sources = [source for _, source in places]
            self.turned = []
            for side in range(2 if staged else 0):
                for turned, source in places:
                    start = 0
                    for other in turned.sources:
                        if other is source:
                            break
                        start += other.shape[0]
                    stop = start + source.shape[0]
                    size = math.gcd(start, stop)
                    for at in range(start, stop, size):
                        self.turned.append((turned.both[side], at, size))

        def take(self, *cotangents):
            self.cotangents = cotangents
            if staged:
                self.cotangents += tuple(swap_core(part) for part in cotangents)

        def make(self, cut=None, **options):
            if staged:
                return weight_grad(
                    order, bits, self.turned, self.cotangents, outer, cut, **options
                )
            rows = [jnp.concatenate(part, axis=0) for part in (self.sources, self.cotangents)]
            return lead_dot(*rows).astype(BF16)

    def at_mem(values, index):
        return lax.dynamic_index_in_dim(values, index, 0, False)

    mem_rows = memory_in[0, :, 0]
    mem_live = memory_mask[0, :, 0]
    near_rows = at_mem(mem_rows, own_index)
    near_live = at_mem(mem_live, own_index)
    far_live = swap_mem(at_mem(mem_live, 1 - own_index))
    sent_rows = [at_mem(mem_rows[:, slot], 1 - own_index) for slot in range(slot_count)]

    (w_qkv,) = gather(0, model_width, True)
    far_parts = [swap_mem(sent_rows[0])]
    if staged:
        order.before(w_qkv.wave.stacked)
        shards += cast_shards(order, bits, groups[1:])
    w_cq, w_co, w_norm, w_ckv, w_so = gather(1, 2 * model_width + LANES)
    (w_in,) = gather(2, 3 * model_width // 2)
    (w_out,) = gather(3, 3 * model_width // 8)

    bucket = pick_entry(bucket_ids[0], own_index)
    lengths = target_lengths[0, 0]
    self_meta = jnp.stack([jnp.right_shift(jnp.int32(row_count), bucket), lengths[0], lengths[1]])
    cross_meta = bucket[None]
    live = jnp.concatenate((near_live, far_live), axis=1)
    key_bias = jnp.where(live == 1, 0.0, NEG_LARGE).astype(F32)
    key_columns = jnp.broadcast_to(key_bias[:, :, None], (*key_bias.shape, LANES))
    near_flat = near_rows.reshape(-1, model_width)
    slotted = (slot_count, mem_piece, 2 * model_width)

    def steps(*wanted):
        if staged:
            moves = Moves(order, bits)
            for weight, name in wanted:
                getattr(weight.wave, name)(moves)
            if moves.moves:
                moves.run()

    steps((w_qkv, "first"))
    order.before(far_parts[0], far_live)
    steps((w_qkv, "second"))
    order.part()
    first_turned = Turned(target_in, near_flat)
    steps((w_ckv, "first"))
    order.part()
    steps((w_qkv, "third"))
    first_turned.due()
    (united,) = project(order, "self_project", bits, w_qkv, [target_in], 1024)
    far_parts += [swap_mem(part) for part in gate(order, bits, sent_rows[1:])]
    order.part()
    steps((w_ckv, "second"))
    steps((w_in, "first"))
    self_mixed, self_log = self_forward(order, self_meta, united)
    far_flat = jnp.concatenate(far_parts, axis=0)
    order.part()
    steps((w_ckv, "third"))
    order.before(*far_parts[1:])
    order.part()
    steps((w_in, "second"))
    steps((w_out, "first"))
    table = norm_table(order, bits, w_norm)
    near_kv, far_kv = project(order, "cross_project", bits, w_ckv, [near_flat, far_flat], 1024)
    near_kv, far_kv = near_kv.reshape(slotted), far_kv.reshape(slotted)
    sum_one, first_out, first_low, cross_query = mix_norm(
        order, "self_mix", bits, w_so, self_mixed, target_in, table, 0, w_cq
    )
    order.part()
    steps((w_in, "third"))
    order.part()
    steps((w_out, "second"))
    cross_mixed, cross_log = cross_forward(
        order, cross_meta, cross_query, near_kv, far_kv, key_bias[:, None, :]
    )
    sum_two, second_out, second_low = mix_norm(
        order, "cross_mix", bits, w_co, cross_mixed, first_out, table, 1
    )
    steps((w_out, "third"))
    later = Turned(self_mixed, first_low, cross_mixed, second_low, far_flat)
    activated, slope = feed_in(order, bits, w_in, second_low)
    later.due()
    hidden = Turned(activated)
    layer_out, grad_three, grad_ffn, stats_three = feed_out(
        order, bits, w_out, activated, second_out, table, grad_out
    )
    qkv_grad = Grad((first_turned, target_in))
    so_grad = Grad((later, self_mixed))
    ckv_grad = Grad((first_turned, near_flat), (later, far_flat))
    cq_grad = Grad((later, first_low))
    co_grad = Grad((later, cross_mixed))
    in_grad = Grad((later, second_low))
    out_grad = Grad((hidden, activated))

    shards = {}

    def spread(name, parts):
        if staged:
            return Spread(parts)
        shards[name] = whole_sum(parts)
        return None

    def advance(seconds=(), thirds=()):
        if staged:
            waves = [wave for _, wave in thirds]
            joined = spread_steps(order, bits, seconds, waves)
            for (name, _), part in zip(thirds, joined):
                shards[name] = outer_sum(part)

    out_grad.take(grad_ffn)
    out_wave = spread("out", out_grad.make(model_width // 2))
    grad_hidden = feed_back(order, bits, w_out, grad_ffn, slope)
    in_grad.take(grad_hidden)
    grad_two, grad_cross_out, grad_cross_mixed, stats_two = norm_back(
        order, "cross_back", bits, w_in, grad_hidden, grad_three, sum_two, table, 1, w_co
    )
    co_grad.take(grad_cross_out)
    order.part()
    advance([out_wave])
    in_wave = spread("in", in_grad.make(2 * model_width))
    pair_width = 2 * model_width
    near_parts = co_grad.make(place=(0, 0, pair_width))
    grad_query_low, grad_near_kv, grad_far_kv = cross_backward(
        order,
        cross_meta,
        cross_query,
        near_kv,
        far_kv,
        key_columns,
        cross_mixed,
        grad_cross_mixed,
        cross_log,
    )
    cq_grad.take(grad_query_low)
    ckv_grad.take(grad_near_kv, grad_far_kv)
    order.part()
    advance([in_wave], [("out", out_wave)])

    def memory_back(cotangent):
        spans = [(0, start, start, model_width) for start in (0, model_width)]
        return input_back(order, "memory_back", bits, w_ckv, [cotangent], None, spans)

    grad_one, grad_self_out, grad_self_mixed, stats_one = norm_back(
        order, "self_back", bits, w_cq, grad_query_low, grad_two, sum_one, table, 0, w_so
    )
    so_grad.take(grad_self_out)
    stats = [jnp.sum(s.reshape(2, 8, model_width), axis=1) for s in (stats_one, stats_two, stats_three)]
    norm_grads = [
        jnp.pad(jnp.stack([s[i] for s in stats], axis=1), ((0, 0), (0, LANES - len(stats))))
        for i in range(2)
    ]
    norm_grads = jnp.concatenate(norm_grads, axis=1).astype(BF16)
    if staged:
        own, other = relative_rows(bits, norm_grads, outer)
        own = (own.astype(F32) + swap_core(other).astype(F32)).astype(BF16)
        norm_grads = (own[..., :LANES], own[..., LANES:])
        near_parts = cq_grad.make(place=(0, model_width, pair_width), held=near_parts)
        mid_wave = spread("mid", [*near_parts, *ckv_grad.make(place=(1, 0, pair_width))])
    else:
        parts = [near_parts, cq_grad.make(), ckv_grad.make()]
        mid_wave = spread("mid", jnp.concatenate(parts, axis=1))
    grad_far = swap_mem(memory_back(grad_far_kv))
    order.part()
    advance([], [("in", in_wave)])
    grad_united = self_backward(
        order,
        self_meta,
        united,
        self_mixed,
        grad_self_mixed,
        self_log,
        0,
        model_width // LANES,
    )
    qkv_grad.take(grad_united)
    order.part()
    advance([mid_wave])
    if staged:
        order.before(shards["out"])
    qkv_wave = spread("qkv", qkv_grad.make(w_qkv.width // 2))
    order.before(grad_far)
    grad_near = memory_back(grad_near_kv)
    half_width = model_width // 2
    if staged:
        so_wave = spread("so", so_grad.make(half_width, extra=norm_grads))
    else:
        part = so_grad.make()
        columns = [part[:, :half_width], norm_grads[:, :LANES], part[:, half_width:], norm_grads[:, LANES:]]
        so_wave = spread("so", jnp.concatenate(columns, axis=1))
    if staged:
        order.before(shards["in"])
        order.part()
        advance([qkv_wave], [("mid", mid_wave)])
    if staged:
        advance([so_wave])
        (joined,) = spread_steps(order, bits, [], [so_wave, qkv_wave], True)
        last = outer_sum_direct(joined)
        split = 2 * (half_width + LANES)
        shards["so"], shards["qkv"] = last[:, :split], last[:, split:]
    target_grad = input_back(
        order,
        "target_back",
        bits,
        w_qkv,
        [grad_united],
        grad_one,
        [(0, start, start, model_width) for start in range(0, w_qkv.width, model_width)],
    )
    if staged:
        moves = Moves(order, bits)
        target = moves.target((2, *near_flat.shape))
        for number, part in enumerate((grad_near, grad_far)):
            place = lambda bits, number=number: (bits[2] ^ number,)
            moves.move(moves.source(part), (slice(None),), near_flat.shape, (target, place))
        moves.then.append(lambda filled: shards.update(memory=filled[target]))
        moves.run()
        grad_pair = shards["memory"]
    else:
        grad_pair = jnp.stack((grad_near, grad_far))
        grad_pair = jnp.where(own_index == 0, grad_pair, grad_pair[::-1])
    qkv_shard = shards["qkv"]
    memory_grad = grad_pair.reshape(1, pieces, 1, *near_rows.shape)
    so_shard, mid_shard = shards["so"], shards["mid"].astype(F32)
    split = half_width + LANES

    return (
        layer_out,
        target_grad,
        memory_grad,
        qkv_shard,
        jnp.concatenate((so_shard[:, :half_width], so_shard[:, split : split + half_width]), axis=1),
        mid_shard[:, model_width : 2 * model_width],
        mid_shard[:, 2 * model_width :],
        mid_shard[:, :model_width],
        shards["in"].astype(F32),
        shards["out"].astype(F32),
        so_shard[:, half_width : half_width + 3],
        so_shard[:, split + half_width : split + half_width + 3],
    )


def solution(mesh):
    rows = P(("dp", "mem"), None)
    memory = P("dp", None, "mem", None, None, None)
    return jax.shard_map(
        per_device,
        mesh=mesh,
        in_specs=(
            rows,
            memory,
            P("dp", None),
            P("dp", "mem", None),
            P("dp", None, "mem", None, None),
        )
        + (rows,) * 10,
        out_specs=(rows, rows, memory) + (rows,) * 9,
        check_vma=False,
    )
```

```python
import math

import jax
import jax.numpy as jnp
from jax import lax
from jax.experimental import pallas as pl
from jax.experimental.pallas import tpu as pltpu
from jax.sharding import PartitionSpec as P

HD = 64
LANES = 128
ALPHA = 300.0**0.25
NEG_LARGE = -1e30
EPSILON = 1e-05
VMEM_BYTES = 64 * 1024 * 1024 - 128 * 1024
SCALE = HD**-0.5
BF16 = jnp.bfloat16
F32 = jnp.float32


def plain_dot(first_op, second_op):
    return jnp.dot(first_op, second_op, preferred_element_type=F32)


def lead_dot(first_op, second_op):
    return lax.dot_general(
        first_op, second_op, (((0,), (0,)), ((), ())), preferred_element_type=F32
    )


def back_dot(first_op, second_op):
    return lax.dot_general(
        first_op, second_op, (((1,), (1,)), ((), ())), preferred_element_type=F32
    )


def pick_entry(values, wanted):
    return jnp.sum(jnp.where(jnp.arange(values.shape[0]) == wanted, values, 0))


def kernel_params():
    return pltpu.CompilerParams(vmem_limit_bytes=VMEM_BYTES)


class Order:
    def __init__(self):
        self.last, self.due, self.parted = None, [], False

    def before(self, *arrays):
        self.due += arrays

    def part(self):
        self.parted = True

    def launch(self, kernel, name, operands, in_specs, out_specs, out_shape, scratch, grid, aliases):
        ties = self.due + ([self.last] if self.last is not None else [])
        ties = [tie for tie in ties if not any(tie is operand for operand in operands)]
        self.due = []
        count, n_ties = len(operands), len(ties)

        def tied(*refs):
            kernel(*refs[:count], *refs[count + n_ties :])

        specs = list(in_specs) + [pl.BlockSpec(memory_space=pltpu.HBM)] * n_ties
        cost = pl.CostEstimate(
            flops=10**12 if self.parted else 10**6, bytes_accessed=1, transcendentals=0
        )
        self.parted = False
        if grid is None:
            run = pl.pallas_call(
                tied,
                in_specs=[pl.BlockSpec(memory_space=pltpu.SMEM)] + specs,
                out_specs=out_specs,
                out_shape=out_shape,
                scratch_shapes=scratch,
                input_output_aliases=aliases,
                compiler_params=kernel_params(),
                cost_estimate=cost,
                name=name,
            )
        else:
            run = pl.pallas_call(
                tied,
                grid_spec=pltpu.PrefetchScalarGridSpec(
                    num_scalar_prefetch=1,
                    grid=grid,
                    in_specs=specs,
                    out_specs=out_specs,
                    scratch_shapes=scratch,
                ),
                out_shape=out_shape,
                input_output_aliases=aliases,
                compiler_params=kernel_params(),
                cost_estimate=cost,
                name=name,
            )
        results = run(*operands, *ties)
        self.last = results[0]
        return results


def whole_spec(shape):
    return pl.BlockSpec(shape, lambda *_: (0,) * len(shape))


def head_lanes(rows, head):
    lane = lax.broadcasted_iota(jnp.int32, (rows, LANES), 1)
    return (lane < HD) if head == 0 else (lane >= HD)


def visible(query_ids, key_ids, slot_len, first_len, second_len):
    query_slot = (query_ids >= slot_len).astype(jnp.int32)
    key_slot = (key_ids >= slot_len).astype(jnp.int32)
    place = key_ids - key_slot * slot_len
    limit = jnp.where(key_slot == 0, first_len, second_len)
    return (query_slot == key_slot) & (key_ids <= query_ids) & (place < limit)


def pair_forward(query, keys, values, bias):
    rows, key_rows = query.shape[0], keys.shape[0]
    mixed, peaks = [], []
    for head in range(2):
        mine = head_lanes(rows, head)
        masked = jnp.where(mine, query * BF16(SCALE), BF16(0))
        scores = back_dot(masked, keys) + bias
        peak = jnp.max(scores, axis=1, keepdims=True)
        raised = jnp.exp(scores - peak).astype(BF16)
        widened = jnp.where(head_lanes(key_rows, head), values, BF16(1))
        mixed.append(plain_dot(raised, widened))
        peaks.append(peak)
    first = head_lanes(rows, 0)
    totals = pltpu.roll(jnp.where(first, mixed[1], mixed[0]), HD, 1)
    joined = jnp.where(first, mixed[0], mixed[1])
    log_totals = jnp.where(first, peaks[0], peaks[1]) + jnp.log(totals)
    return joined / totals, log_totals


def pair_backward(query, keys, values, upstream, bias, log_rows, delta_rows):
    rows, key_rows = query.shape[0], keys.shape[0]
    grad_q, grad_k, grad_v = None, None, None
    for head in range(2):
        mine = head_lanes(rows, head)
        masked = jnp.where(mine, query * BF16(SCALE), BF16(0))
        masked_up = jnp.where(mine, upstream, BF16(0))
        scores = back_dot(keys, masked) + bias
        probs = jnp.exp(scores - log_rows[head])
        grad_probs = back_dot(values, masked_up)
        grad_scores = (probs * (grad_probs - delta_rows[head])).astype(BF16)
        part_v = plain_dot(probs.astype(BF16), masked_up)
        part_k = plain_dot(grad_scores, masked)
        masked_keys = jnp.where(head_lanes(key_rows, head), keys, BF16(0))
        part_q = lead_dot(grad_scores, masked_keys)
        grad_q = part_q if grad_q is None else grad_q + part_q
        grad_k = part_k if grad_k is None else grad_k + part_k
        grad_v = part_v if grad_v is None else grad_v + part_v
    return grad_q * SCALE, grad_k, grad_v


def stat_rows(log_block, mixed, upstream):
    log_turned = log_block.T
    products = (mixed.astype(F32) * upstream.astype(F32)).T
    log_rows = [log_turned[:1], log_turned[HD : HD + 1]]
    delta_rows = [jnp.sum(products[h * HD : (h + 1) * HD], axis=0, keepdims=True) for h in range(2)]
    return log_rows, delta_rows


def self_forward_kernel(meta, q_ref, k_ref, v_ref, mixed_ref, log_ref, bias):
    rows = q_ref.shape[0]

    @pl.when(pl.program_id(0) == 0)
    def _():
        query_ids = lax.broadcasted_iota(jnp.int32, (rows, rows), 0)
        key_ids = lax.broadcasted_iota(jnp.int32, (rows, rows), 1)
        seen = visible(query_ids, key_ids, meta[0], meta[1], meta[2])
        bias[...] = jnp.where(seen, 0.0, NEG_LARGE)

    half = rows // 2
    for start, stop in ((0, half), (half, rows)):
        mixed, log_totals = pair_forward(
            q_ref[start:stop, :], k_ref[:stop, :], v_ref[:stop, :], bias[start:stop, :stop]
        )
        mixed_ref[start:stop, :] = mixed.astype(BF16)
        log_ref[start:stop, :] = log_totals


def self_forward(order, meta, united):
    rows, width = united.shape[0], united.shape[1] // 3
    pairs = width // LANES
    spec = lambda third: pl.BlockSpec((rows, LANES), lambda i, _: (0, third * pairs + i))
    return order.launch(
        self_forward_kernel,
        "self_forward",
        [meta, united, united, united],
        [spec(0), spec(1), spec(2)],
        [spec(0), spec(0)],
        [jax.ShapeDtypeStruct((rows, width), kind) for kind in (BF16, F32)],
        [pltpu.VMEM((rows, rows), F32)],
        (pairs,),
        {},
    )


def self_backward_kernel(
    meta, q_ref, k_ref, v_ref, mixed_ref, up_ref, log_ref, grad_ref, bias
):
    rows = q_ref.shape[0]
    width = grad_ref.shape[1] // 3
    pair = pl.program_id(0)

    @pl.when(pair == 0)
    def _():
        key_ids = lax.broadcasted_iota(jnp.int32, (rows, rows), 0)
        query_ids = lax.broadcasted_iota(jnp.int32, (rows, rows), 1)
        seen = visible(query_ids, key_ids, meta[0], meta[1], meta[2])
        bias[...] = jnp.where(seen, 0.0, NEG_LARGE)

    log_rows, delta_rows = stat_rows(log_ref[...], mixed_ref[...], up_ref[...])
    half = rows // 2
    parts = []
    for start, stop in ((0, half), (half, rows)):
        parts.append(
            pair_backward(
                q_ref[start:stop, :],
                k_ref[:stop, :],
                v_ref[:stop, :],
                up_ref[start:stop, :],
                bias[:stop, start:stop],
                [row[:, start:stop] for row in log_rows],
                [row[:, start:stop] for row in delta_rows],
            )
        )
    low, high = parts
    columns = lambda third: pl.ds(pl.multiple_of(third * width + pair * LANES, LANES), LANES)
    grad_ref[:half, columns(0)] = low[0].astype(BF16)
    grad_ref[half:, columns(0)] = high[0].astype(BF16)
    for third in (1, 2):
        grad_ref[:half, columns(third)] = (low[third] + high[third][:half]).astype(BF16)
        grad_ref[half:, columns(third)] = high[third][half:].astype(BF16)


def self_backward(order, meta, united, mixed, upstream, log_totals, first, pairs):
    rows, width = mixed.shape
    third = width // LANES
    spec = lambda at: pl.BlockSpec((rows, LANES), lambda i, _: (0, at * third + first + i))
    shape = (rows, 3 * pairs * LANES)
    return order.launch(
        self_backward_kernel,
        "self_backward",
        [meta, united, united, united, mixed, upstream, log_totals],
        [spec(0), spec(1), spec(2), spec(0), spec(0), spec(0)],
        [whole_spec(shape)],
        [jax.ShapeDtypeStruct(shape, BF16)],
        [pltpu.VMEM((rows, rows), F32)],
        (pairs,),
        {},
    )[0]


def join_keys(near_ref, far_ref, joined):
    slots, piece = near_ref.shape[0], near_ref.shape[1]
    for slot in range(slots):
        joined[slot, :piece, :] = near_ref[slot]
        joined[slot, piece:, :] = far_ref[slot]


def cross_forward_kernel(
    meta, q_ref, kn_ref, vn_ref, kf_ref, vf_ref, bias_ref, mixed_ref, log_ref, keys, values
):
    half = q_ref.shape[0] // 2
    join_keys(kn_ref, kf_ref, keys)
    join_keys(vn_ref, vf_ref, values)
    for part in range(2):
        slot = part * meta[0]
        rows = slice(part * half, (part + 1) * half)
        mixed, log_totals = pair_forward(q_ref[rows, :], keys[slot], values[slot], bias_ref[slot])
        mixed_ref[rows, :] = mixed.astype(BF16)
        log_ref[rows, :] = log_totals


def cross_specs(rows, slots, piece, pairs):
    row_spec = pl.BlockSpec((rows, LANES), lambda i, _: (0, i))
    half = lambda at: pl.BlockSpec((slots, piece, LANES), lambda i, _: (0, 0, at * pairs + i))
    return row_spec, [row_spec, half(0), half(1), half(0), half(1)]


def cross_forward(order, meta, query, near, far, bias):
    rows, width = query.shape
    slots, piece = near.shape[0], near.shape[1]
    pairs = width // LANES
    row_spec, specs = cross_specs(rows, slots, piece, pairs)
    return order.launch(
        cross_forward_kernel,
        "cross_forward",
        [meta, query, near, near, far, far, bias],
        specs + [whole_spec(bias.shape)],
        [row_spec, row_spec],
        [jax.ShapeDtypeStruct((rows, width), kind) for kind in (BF16, F32)],
        [pltpu.VMEM((slots, 2 * piece, LANES), BF16)] * 2,
        (pairs,),
        {},
    )


def cross_backward_kernel(
    meta,
    q_ref,
    kn_ref,
    vn_ref,
    kf_ref,
    vf_ref,
    bias_ref,
    mixed_ref,
    up_ref,
    log_ref,
    grad_q_ref,
    grad_near_ref,
    grad_far_ref,
    keys,
    values,
):
    half = q_ref.shape[0] // 2
    slots, piece = kn_ref.shape[0], kn_ref.shape[1]
    width = grad_near_ref.shape[1] // 2
    join_keys(kn_ref, kf_ref, keys)
    join_keys(vn_ref, vf_ref, values)
    log_rows, delta_rows = stat_rows(log_ref[...], mixed_ref[...], up_ref[...])
    parts = []
    for part in range(2):
        slot = part * meta[0]
        rows = slice(part * half, (part + 1) * half)
        bias_column = bias_ref[slot]
        grads = pair_backward(
            q_ref[rows, :],
            keys[slot],
            values[slot],
            up_ref[rows, :],
            jnp.concatenate([bias_column] * (half // LANES), axis=1),
            [row[:, rows] for row in log_rows],
            [row[:, rows] for row in delta_rows],
        )
        grad_q_ref[rows, :] = grads[0].astype(BF16)
        parts.append(grads)
    split = meta[0].astype(F32)
    start = pl.program_id(0) * LANES
    for which in range(2):
        early, late = parts[0][1 + which], parts[1][1 + which]
        columns = pl.ds(pl.multiple_of(which * width + start, LANES), LANES)
        by_slot = (early + late * (1.0 - split), late * split)
        for slot in range(slots):
            for source, target in enumerate((grad_near_ref, grad_far_ref)):
                target[slot * piece : (slot + 1) * piece, columns] = by_slot[slot][
                    source * piece : (source + 1) * piece
                ].astype(BF16)


def cross_backward(order, meta, query, near, far, bias, mixed, upstream, log_totals):
    rows, width = query.shape
    slots, piece = near.shape[0], near.shape[1]
    pairs = width // LANES
    memory = (slots * piece, 2 * width)
    row_spec, specs = cross_specs(rows, slots, piece, pairs)
    return order.launch(
        cross_backward_kernel,
        "cross_backward",
        [meta, query, near, near, far, far, bias, mixed, upstream, log_totals],
        specs + [whole_spec(bias.shape)] + [row_spec] * 3,
        [row_spec, whole_spec(memory), whole_spec(memory)],
        [jax.ShapeDtypeStruct(shape, BF16) for shape in ((rows, width), memory, memory)],
        [pltpu.VMEM((slots, 2 * piece, LANES), BF16)] * 2,
        (pairs,),
        {},
    )


def swap_core(values):
    size = lax.axis_size("dp")
    return lax.ppermute(values, "dp", [(i, i ^ 1) for i in range(size)])


def swap_next(values):
    size = lax.axis_size("dp")
    return lax.ppermute(values, "dp", [(i, i ^ 2) for i in range(size)])


def swap_mem(values):
    return lax.ppermute(values, "mem", [(0, 1), (1, 0)])


def swap_outer(values, far):
    size = lax.axis_size("dp")
    return lax.ppermute(values, "dp", [(i, i ^ (4 * far)) for i in range(size)])


def outer_groups():
    size = lax.axis_size("dp")
    return [list(range(base, size, 4)) for base in range(4)]


def place_bits():
    dp, mem = lax.axis_index("dp"), lax.axis_index("mem")
    return jnp.stack([(dp >> 1) & 1, dp & 1, mem, dp >> 2]).astype(jnp.int32)


def outer_gather(shard):
    stacked = lax.all_gather(shard, "dp", axis_index_groups=outer_groups(), axis=0, tiled=True)
    return stacked.reshape(-1, *shard.shape)


def gate(order, bits, arrays):
    def kernel(*refs):
        pass

    return order.launch(
        kernel,
        "gate",
        [bits, *arrays],
        [pl.BlockSpec(memory_space=pltpu.HBM)] * len(arrays),
        [pl.BlockSpec(memory_space=pltpu.HBM)] * len(arrays),
        [jax.ShapeDtypeStruct(array.shape, array.dtype) for array in arrays],
        [],
        None,
        {1 + i: i for i in range(len(arrays))},
    )


class Moves:
    def __init__(self, order, bits):
        self.order, self.bits = order, bits
        self.sources, self.shapes, self.moves, self.aliases, self.then = [], [], [], {}, []

    def source(self, array):
        self.sources.append(array)
        return len(self.sources) - 1

    def target(self, shape, held=None):
        self.shapes.append(shape)
        if held is not None:
            self.aliases[1 + self.source(held)] = len(self.shapes) - 1
        return len(self.shapes) - 1

    def passed(self, array):
        return self.target(array.shape, array)

    def move(self, source, source_at, shape, *goals):
        self.moves.append((source, source_at, shape, goals))

    def run(self):
        moves, n_in, n_out = self.moves, len(self.sources), len(self.shapes)
        most = max([len(move[3]) for move in moves] + [0])

        def kernel(bits_ref, *refs):
            bits = [bits_ref[i] for i in range(4)]
            taken, given = refs[:n_in], refs[n_in : n_in + n_out]
            slots, sems = refs[n_in + n_out : -1], refs[-1]
            loads, stores = [], []
            for number, (source, source_at, _, goals) in enumerate(moves):
                slot = slots[number]
                loads.append(
                    pltpu.make_async_copy(
                        taken[source].at[source_at(bits) if callable(source_at) else source_at],
                        slot,
                        sems.at[0, number],
                    )
                )
                stores.append(
                    [
                        pltpu.make_async_copy(
                            slot, given[which].at[at(bits) if callable(at) else at], sems.at[1 + i, number]
                        )
                        for i, (which, at) in enumerate(goals)
                    ]
                )
            for load in loads:
                load.start()
            for load, group in zip(loads, stores):
                load.wait()
                for store in group:
                    store.start()
            for group in stores:
                for store in group:
                    store.wait()

        filled = self.order.launch(
            kernel,
            "move_blocks",
            [self.bits, *self.sources],
            [pl.BlockSpec(memory_space=pltpu.HBM)] * n_in,
            [pl.BlockSpec(memory_space=pltpu.HBM)] * n_out,
            [jax.ShapeDtypeStruct(shape, BF16) for shape in self.shapes],
            [pltpu.VMEM(shape, BF16) for _, _, shape, _ in moves]
            + [pltpu.SemaphoreType.DMA((1 + most, max(1, len(moves))))],
            None,
            self.aliases,
        )
        for step in self.then:
            step(filled)


def cast_shards(order, bits, groups):
    shapes = [(group[0].shape[0], sum(part.shape[1] for part in group)) for group in groups]
    parts = [part for group in groups for part in group]

    def kernel(bits_ref, *refs):
        number = 0
        for group, target in zip(groups, refs[len(parts) :]):
            start = 0
            for part in group:
                stop = start + part.shape[1]
                target[:, start:stop] = refs[number][...].astype(BF16)
                start, number = stop, number + 1

    return order.launch(
        kernel,
        "cast_shards",
        [bits, *parts],
        [pl.BlockSpec(memory_space=pltpu.VMEM)] * len(parts),
        [pl.BlockSpec(memory_space=pltpu.VMEM)] * len(shapes),
        [jax.ShapeDtypeStruct(shape, BF16) for shape in shapes],
        [],
        None,
        {},
    )


FIRST = (swap_next, swap_mem)
SECOND = (swap_mem, swap_next)


class Wave:
    def __init__(self, shard, windows, direct):
        self.windows = [(pl.ds(start, size), kind) for start, size, kind in windows]
        self.rows, self.columns = shard.shape
        self.outer = lax.axis_size("dp") // 4
        if direct:
            self.shards = [shard] + [swap_outer(shard, far) for far in range(1, self.outer)]
        else:
            self.stacked = outer_gather(shard)
        self.direct = direct

    def first(self, moves):
        def send(parts):
            self.pairs = [(part, FIRST[kind](part)) for part, (_, kind) in zip(parts, self.windows)]

        if not self.direct and len(self.windows) == 1:
            target = moves.passed(self.stacked)
            moves.then.append(lambda filled: send([filled[target]]))
            return
        targets = [moves.target((self.outer, self.rows, w.size)) for w, _ in self.windows]
        sources = [moves.source(part) for part in (self.shards if self.direct else [self.stacked])]
        for block in range(self.outer):
            for target, (window, _) in zip(targets, self.windows):
                shape = (self.rows, window.size)
                if self.direct:
                    goal = (target, lambda bits, block=block: (bits[3] ^ block,))
                    moves.move(sources[block], (slice(None), window), shape, goal)
                else:
                    goal = (target, (block,))
                    moves.move(sources[0], (block, slice(None), window), shape, goal)
        moves.then.append(lambda filled: send([filled[target] for target in targets]))

    def place(self, kind, second, first, block, window):
        near, mem = (first, second) if kind == 0 else (second, first)
        return lambda bits: (block, bits[0] ^ near, bits[2] ^ mem, slice(None), window)

    def second(self, moves):
        sources = [[moves.source(part) for part in pair] for pair in self.pairs]
        targets = [moves.target((2, *pair[0].shape)) for pair in self.pairs]
        own = moves.target((self.outer, 2, 2, self.rows, self.columns))
        for block in range(self.outer):
            for number, (window, kind) in enumerate(self.windows):
                for side in range(2):
                    goal = (targets[number], (side, block))
                    again = (own, self.place(kind, 0, side, block, window))
                    shape = (self.rows, window.size)
                    moves.move(sources[number][side], (block,), shape, goal, again)

        def send(filled):
            self.own = filled[own]
            self.far = [
                SECOND[kind](filled[target]) for target, (_, kind) in zip(targets, self.windows)
            ]

        moves.then.append(send)

    def third(self, moves):
        own = moves.target(self.own.shape, self.own)
        for number, (window, kind) in enumerate(self.windows):
            source = moves.source(self.far[number])
            for block in range(self.outer):
                for side in range(2):
                    goal = (own, self.place(kind, 1, side, block, window))
                    moves.move(source, (side, block), (self.rows, window.size), goal)

        def send(filled):
            shape = (2 * self.outer, 2 * self.rows, self.columns)
            self.own = filled[own].reshape(shape)
            self.other = swap_core(self.own)

        moves.then.append(send)


class Weight:
    def __init__(self, wave, start, width, whole=None):
        self.wave, self.start, self.width, self.whole = wave, start, width, whole
        if whole is not None:
            self.blocks, self.rows = whole.shape[0], whole.shape[2]
        else:
            self.blocks, self.rows = 2 * wave.outer, 2 * wave.rows
        self.features = self.blocks * 2 * self.rows

    def pieces(self):
        return [self.whole] if self.whole is not None else [self.wave.own, self.wave.other]

    def copies(self, kind, start, size, bits, find, target):
        if kind == "columns":
            blocks, columns = slice(None), pl.ds(self.start + start, size)
        else:
            blocks, columns = pl.ds(start, size), pl.ds(self.start, self.width)
        if self.whole is not None:
            return [(find(self.whole).at[blocks, :, :, columns], target)]
        return [
            (find(array).at[blocks, :, columns], target.at[:, bits[1] ^ core])
            for core, array in enumerate((self.wave.own, self.wave.other))
        ]


def weight_call(order, name, bits, weights, plan, inputs, outs, scratch, body):
    arrays = []
    for weight in weights:
        arrays += [a for a in weight.pieces() if not any(a is b for b in arrays)]
    kind, size = plan[0][1], plan[0][3]
    lead = weights[plan[0][0]]
    if kind == "columns":
        chunk = (lead.blocks, 2, lead.rows, size)
    else:
        chunk = (size, 2, lead.rows, lead.width)
    n_in, n_arrays, n_out = len(inputs), len(arrays), len(outs)

    def kernel(bits_ref, *refs):
        ins, refs = refs[:n_in], refs[n_in:]
        pieces, refs = refs[:n_arrays], refs[n_arrays:]
        out_refs, refs = refs[:n_out], refs[n_out:]
        held, sems = refs[-2:]
        bits_now = [bits_ref[i] for i in range(3)]

        def find(array):
            return next(ref for ref, known in zip(pieces, arrays) if known is array)

        def issue(number):
            which, kind, start, size = plan[number]
            slot = number % 2
            for source, target in weights[which].copies(
                kind, start, size, bits_now, find, held.at[slot]
            ):
                pltpu.make_async_copy(source, target, sems.at[slot]).start()

        taken = [0]

        def fetch():
            number = taken[0]
            taken[0] += 1
            if number + 1 < len(plan):
                issue(number + 1)
            slot = number % 2
            pltpu.make_async_copy(held.at[slot], held.at[slot], sems.at[slot]).wait()
            return held[slot].reshape(-1, chunk[-1])

        issue(0)
        body(fetch, ins, out_refs, refs[:-2])

    return order.launch(
        kernel,
        name,
        [bits, *inputs, *arrays],
        [pl.BlockSpec(memory_space=pltpu.VMEM)] * n_in
        + [pl.BlockSpec(memory_space=pltpu.HBM)] * n_arrays,
        [pl.BlockSpec(memory_space=pltpu.VMEM)] * n_out,
        [jax.ShapeDtypeStruct(shape, kind) for shape, kind in outs],
        [pltpu.VMEM(shape, kind) for shape, kind in scratch]
        + [pltpu.VMEM((2, *chunk), BF16), pltpu.SemaphoreType.DMA((2,))],
        None,
        {},
    )


def columns_plan(which, width, size):
    return [(which, "columns", start, size) for start in range(0, width, size)]


def row_blocks(rows, size, step):
    def run(i, carry):
        step(pl.ds(pl.multiple_of(i * size, size), size))
        return carry

    lax.fori_loop(0, rows // size, run, 0)


def normed_parts(values):
    centred = values - jnp.mean(values, axis=-1, keepdims=True)
    spread = jnp.mean(centred * centred, axis=-1, keepdims=True)
    rate = lax.rsqrt(spread + EPSILON)
    return centred * rate, rate


def norm_gradient(normed, rate, gain, cotangent):
    inner = cotangent * gain
    mean_inner = jnp.mean(inner, axis=-1, keepdims=True)
    mean_both = jnp.mean(inner * normed, axis=-1, keepdims=True)
    return rate * (inner - mean_inner - normed * mean_both)


def add_stats(stats, normed, cotangent):
    fold = lambda values: jnp.sum(values.reshape(-1, 8, values.shape[-1]), axis=0)
    stats[:8, :] += fold(cotangent * normed)
    stats[8:, :] += fold(cotangent)


def norm_table(order, bits, weight):
    features = weight.features

    def body(fetch, ins, outs, scratch):
        outs[0][...] = fetch().astype(F32).T[:8]

    return weight_call(
        order, "norm_table", bits, [weight], [(0, "columns", 0, LANES)], [],
        [((8, features), F32)], [], body,
    )[0]


def project(order, name, bits, weight, sources, size):
    def body(fetch, ins, outs, scratch):
        for start in range(0, weight.width, size):
            chunk = fetch()
            for source, target in zip(ins, outs):
                target[:, start : start + size] = plain_dot(source[...], chunk).astype(BF16)

    return weight_call(
        order, name, bits, [weight], columns_plan(0, weight.width, size), sources,
        [((source.shape[0], weight.width), BF16) for source in sources], [], body,
    )


def mix_norm(order, name, bits, weight, mixed, residual, table, index, query_weight=None):
    rows, width = mixed.shape
    size = min(1024, width)

    def body(fetch, ins, outs, scratch):
        mixed_ref, residual_ref, table_ref = ins
        summed, out, out_low = outs[:3]
        for start in range(0, width, size):
            part = plain_dot(mixed_ref[...], fetch())
            columns = slice(start, start + size)
            summed[:, columns] = ALPHA * residual_ref[:, columns].astype(F32) + part
        gain, shift = table_ref[index : index + 1, :], table_ref[3 + index : 4 + index, :]

        def step(block):
            normed, _ = normed_parts(summed[block, :])
            values = normed * gain + shift
            out[block, :] = values
            out_low[block, :] = values.astype(BF16)

        row_blocks(rows, 128, step)
        if query_weight is not None:
            for start in range(0, width, size):
                part = plain_dot(out_low[...], fetch())
                outs[3][:, start : start + size] = part.astype(BF16)

    weights = [weight] + ([query_weight] if query_weight is not None else [])
    plan = [entry for i in range(len(weights)) for entry in columns_plan(i, width, size)]
    outs = [((rows, width), F32), ((rows, width), F32), ((rows, width), BF16)]
    if query_weight is not None:
        outs.append(((rows, width), BF16))
    return weight_call(
        order, name, bits, weights, plan, [mixed, residual, table], outs, [], body
    )


def feed_in(order, bits, weight, source):
    rows, size = source.shape[0], 1024

    def body(fetch, ins, outs, scratch):
        held = scratch[0]
        for start in range(0, weight.width, size):
            held[...] = plain_dot(ins[0][...], fetch())

            def step(block):
                hidden = held[block, :]
                below = 0.5 + 0.5 * lax.erf(hidden * (0.5**0.5))
                density = jnp.exp(-0.5 * hidden * hidden) * (2.0 * jnp.pi) ** -0.5
                outs[0][block, start : start + size] = (hidden * below).astype(BF16)
                outs[1][block, start : start + size] = (below + hidden * density).astype(BF16)

            row_blocks(rows, 256, step)

    out = ((rows, weight.width), BF16)
    return weight_call(
        order, "feed_in", bits, [weight], columns_plan(0, weight.width, size), [source], [out, out],
        [((rows, size), F32)], body,
    )


def feed_out(order, bits, weight, activated, residual, table, cotangent):
    rows, width = residual.shape
    size = 512 if width % 512 == 0 else width

    def body(fetch, ins, outs, scratch):
        act_ref, residual_ref, table_ref, up_ref = ins
        layer_out, grad, grad_low, stats = outs
        summed = scratch[0]
        for start in range(0, width, size):
            columns = slice(start, start + size)
            part = plain_dot(act_ref[...], fetch())
            summed[:, columns] = ALPHA * residual_ref[:, columns] + part
        gain, shift = table_ref[2:3, :], table_ref[5:6, :]
        stats[...] = jnp.zeros_like(stats)

        def step(block):
            normed, rate = normed_parts(summed[block, :])
            layer_out[block, :] = (normed * gain + shift).astype(BF16)
            upstream = up_ref[block, :].astype(F32)
            values = norm_gradient(normed, rate, gain, upstream)
            grad[block, :] = values
            grad_low[block, :] = values.astype(BF16)
            add_stats(stats, normed, upstream)

        row_blocks(rows, 128, step)

    outs = [((rows, width), BF16), ((rows, width), F32), ((rows, width), BF16), ((16, width), F32)]
    return weight_call(
        order, "feed_out", bits, [weight], columns_plan(0, width, size),
        [activated, residual, table, cotangent], outs, [((rows, width), F32)], body,
    )


def feed_back(order, bits, weight, cotangent, slope):
    rows, features = slope.shape
    size = 1024 if features % 1024 == 0 else features
    steps = features // size

    def body(fetch, ins, outs, scratch):
        for number in range(steps):
            part = back_dot(ins[0][...], fetch())
            columns = slice(number * size, (number + 1) * size)
            outs[0][:, columns] = (part * ins[1][:, columns].astype(F32)).astype(BF16)

    blocks = weight.blocks // steps
    return weight_call(
        order, "feed_back", bits, [weight], [(0, "rows", i * blocks, blocks) for i in range(steps)],
        [cotangent, slope], [((rows, features), BF16)], [], body,
    )[0]


def norm_back(order, name, bits, weight, cotangent, carried, summed, table, index, mix_weight):
    rows, width = summed.shape
    size = min(1024, weight.width)

    def body(fetch, ins, outs, scratch):
        up_ref, carried_ref, summed_ref, table_ref = ins
        grad, grad_low, grad_mixed, stats = outs
        total = scratch[0]
        for start in range(0, weight.width, size):
            part = back_dot(up_ref[:, start : start + size], fetch())
            total[...] = part + (ALPHA * carried_ref[...] if start == 0 else total[...])
        gain = table_ref[index : index + 1, :]
        stats[...] = jnp.zeros_like(stats)

        def step(block):
            normed, rate = normed_parts(summed_ref[block, :])
            upstream = total[block, :]
            values = norm_gradient(normed, rate, gain, upstream)
            grad[block, :] = values
            grad_low[block, :] = values.astype(BF16)
            add_stats(stats, normed, upstream)

        row_blocks(rows, 128, step)
        grad_mixed[...] = back_dot(grad_low[...], fetch()).astype(BF16)

    outs = [((rows, width), F32), ((rows, width), BF16), ((rows, width), BF16), ((16, width), F32)]
    return weight_call(
        order, name, bits, [weight, mix_weight],
        columns_plan(0, weight.width, size) + columns_plan(1, width, size),
        [cotangent, carried, summed, table], outs, [((rows, width), F32)], body,
    )


def input_back(order, name, bits, weight, cotangents, carried, spans):
    rows, features = cotangents[0].shape[0], weight.features
    step = 512 if rows % 512 == 0 else rows // 2
    count = len(cotangents)

    def body(fetch, ins, outs, scratch):
        for number, (which, first, _, size) in enumerate(spans):
            chunk = fetch()
            for row in range(0, rows, step):
                block = slice(row, row + step)
                part = back_dot(ins[which][block, first : first + size], chunk)
                if number == 0 and carried is not None:
                    part += ALPHA * ins[count][block, :]
                elif number > 0:
                    part += scratch[0][block, :]
                if number == len(spans) - 1:
                    outs[0][block, :] = part.astype(BF16)
                else:
                    scratch[0][block, :] = part

    return weight_call(
        order, name, bits, [weight], [(0, "columns", start, size) for _, _, start, size in spans],
        [*cotangents] + ([carried] if carried is not None else []),
        [((rows, features), BF16)], [((rows, features), F32)], body,
    )[0]


def turn_rows(order, bits, sources, outer):
    features = sources[0].shape[1]
    total_rows = sum(source.shape[0] for source in sources)
    shard_rows = features // (8 * outer)

    def kernel(bits_ref, *refs):
        targets, filled = refs[len(sources) :], 0
        for ref in refs[: len(sources)]:
            stop = filled + ref.shape[0]
            for block in range(features // LANES):
                turned_block = ref[:, block * LANES : (block + 1) * LANES].T
                for part in range(LANES // shard_rows):
                    device = block * (LANES // shard_rows) + part
                    mem, core, near = device & 1, (device >> 1) & 1, (device >> 2) & 1
                    place = (mem ^ bits_ref[2]) * 2 + (near ^ bits_ref[0])
                    place = place * outer + (device >> 3)
                    rows = pl.ds(pl.multiple_of(place * shard_rows, shard_rows), shard_rows)
                    values = turned_block[part * shard_rows : (part + 1) * shard_rows]
                    side = core ^ bits_ref[1]

                    @pl.when(side == 0)
                    def _():
                        targets[0][rows, filled:stop] = values

                    @pl.when(side == 1)
                    def _():
                        targets[1][rows, filled:stop] = values

            filled = stop

    return order.launch(
        kernel,
        "turn_rows",
        [bits, *sources],
        [pl.BlockSpec(memory_space=pltpu.VMEM)] * len(sources),
        [pl.BlockSpec(memory_space=pltpu.VMEM)] * 2,
        [jax.ShapeDtypeStruct((features // 2, total_rows), BF16)] * 2,
        [],
        None,
        {},
    )


def weight_grad(
    order, bits, turned, cotangents, outer, cut, extra=None, held=None, place=None
):
    half_features = turned[0][0].shape[0]
    each, width = cotangents[0].shape
    n_turned = len(turned)
    n_grads = len(cotangents)
    total_rows = n_grads // 2 * each
    shard_rows = half_features // (4 * outer)
    chunk = 512 if cut is None or cut % 512 == 0 else 256
    added = 0 if extra is None else LANES
    n_held = 2 if held is not None else 0
    if place is None:
        halves = [(0, 0, cut // chunk, cut), (1, 0, (width - cut) // chunk, width - cut)]
    else:
        halves = [(place[0], place[1] // chunk, width // chunk, place[2])]
    steps = [count for _, _, count, _ in halves]
    first_steps = [sum(steps[:i]) for i in range(len(steps))]

    def kernel(bits_ref, *refs):
        n_in = n_turned + n_grads
        targets = refs[n_in + n_held + (len(halves) if added else 0) :]
        step = pl.program_id(0)
        features = jnp.concatenate([ref[...] for ref in refs[:n_turned]], axis=1)
        grads = jnp.concatenate([ref[...] for ref in refs[n_turned:n_in]], axis=0)
        product = plain_dot(features, grads)
        blocks = product.astype(BF16).reshape(2, 2, outer, shard_rows, chunk)
        for number, (half, _, count, _) in enumerate(halves):

            @pl.when((step >= first_steps[number]) & (step < first_steps[number] + count))
            def _():
                for side in range(2):
                    target = targets[2 * number + side]
                    picked = blocks[1 - side] if half == 0 else blocks[:, 1 - side]
                    target[..., :chunk] = picked
                    if added:
                        beside = refs[n_in + number]
                        picked = beside[1 - side] if half == 0 else beside[:, 1 - side]
                        target[..., chunk:] = picked

    def out_spec(number):
        _, first, count, _ = halves[number]
        at = lambda i, _: (0, 0, 0, first + jnp.clip(i - first_steps[number], 0, count - 1))
        return pl.BlockSpec((2, outer, shard_rows, chunk + added), at)

    def turned_spec(start, size):
        return pl.BlockSpec((half_features, size), lambda i, _: (0, start // size))

    whole = (2, 2, outer, shard_rows, LANES)
    specs = [turned_spec(start, size) for _, start, size in turned]
    specs += [pl.BlockSpec((each, chunk), lambda i, _: (0, i))] * n_grads
    specs += [pl.BlockSpec(memory_space=pltpu.HBM)] * n_held
    specs += [whole_spec(whole)] * (len(halves) if added else 0)
    return order.launch(
        kernel,
        "weight_grad",
        [bits, *(part for part, _, _ in turned), *cotangents, *(held or ()), *(extra or ())],
        specs,
        [out_spec(number) for number in range(len(halves)) for _ in range(2)],
        [
            jax.ShapeDtypeStruct((2, outer, shard_rows, columns + added), BF16)
            for _, _, _, columns in halves
            for _ in range(2)
        ],
        [],
        (sum(steps),),
        {1 + n_turned + n_grads: 0, 2 + n_turned + n_grads: 1} if n_held else {},
    )


def relative_rows(bits, values, outer):
    rows = values.shape[0] // (8 * outer)
    blocks = values.reshape(outer, 2, 2, 2, rows, -1)
    for axis, bit in ((1, bits[0]), (2, bits[1]), (3, bits[2])):
        blocks = jnp.where(bit == 1, jnp.flip(blocks, axis), blocks)
    blocks = blocks.transpose(2, 3, 1, 0, 4, 5)
    return blocks[0], blocks[1]


def add_blocks(order, bits, sums, shapes):
    arrays = []
    for group, _, _ in sums:
        arrays += [a for a, _ in group if not any(a is b for b in arrays)]
    blocks = [group[0][0].shape[-3:] for group, _, _ in sums]
    find = lambda array: next(i for i, known in enumerate(arrays) if known is array)
    chunks = [(number, place) for place in range(blocks[0][0]) for number in range(len(sums))]

    def kernel(bits_ref, *refs):
        sources, refs = refs[: len(arrays)], refs[len(arrays) :]
        targets, refs = refs[: len(shapes)], refs[len(shapes) :]
        held, summed, (load_sems, store_sems) = refs[: len(sums)], refs[len(sums) : -2], refs[-2:]
        loads, stores = [], []
        for index, (number, place) in enumerate(chunks):
            loads.append([])
            for term, (array, at) in enumerate(sums[number][0]):
                load = pltpu.make_async_copy(
                    sources[find(array)].at[(*at, place)],
                    held[number].at[term, place],
                    load_sems.at[index, term],
                )
                load.start()
                loads[-1].append(load)
        for index, (number, place) in enumerate(chunks):
            group, which, column = sums[number]
            for load in loads[index]:
                load.wait()
            values = [held[number][term, place].astype(F32) for term in range(len(group))]
            summed[number][place] = sum(values[1:], values[0]).astype(BF16)
            store = pltpu.make_async_copy(
                summed[number].at[place],
                targets[which].at[place, :, pl.ds(column, blocks[number][2])],
                store_sems.at[index],
            )
            store.start()
            stores.append(store)
        for store in stores:
            store.wait()

    most = max(len(group) for group, _, _ in sums)
    return order.launch(
        kernel,
        "add_blocks",
        [bits, *arrays],
        [pl.BlockSpec(memory_space=pltpu.HBM)] * len(arrays),
        [pl.BlockSpec(memory_space=pltpu.HBM)] * len(shapes),
        [jax.ShapeDtypeStruct(shape, BF16) for shape in shapes],
        [pltpu.VMEM((len(group), *block), BF16) for (group, _, _), block in zip(sums, blocks)]
        + [pltpu.VMEM(block, BF16) for block in blocks]
        + [
            pltpu.SemaphoreType.DMA((len(chunks), most)),
            pltpu.SemaphoreType.DMA((len(chunks),)),
        ],
        None,
        {},
    )


class Spread:
    def __init__(self, parts, kinds):
        self.kinds, self.kept = kinds, parts[1::2]
        self.once = [FIRST_BACK[kind](part) for part, kind in zip(parts[0::2], kinds)]

    def second(self):
        return [[(kept, (1,)), (once, (1,))] for kept, once in zip(self.kept, self.once)]

    def send(self, sent):
        self.twice = [SECOND_BACK[kind](part) for part, kind in zip(sent, self.kinds)]

    def third(self):
        return [
            [(kept, (0,)), (once, (0,)), (twice, ())]
            for kept, once, twice in zip(self.kept, self.once, self.twice)
        ]


def block_shape(group):
    return group[0][0].shape[-3:]


def spread_steps(order, bits, seconds, thirds, together=False):
    sums, shapes = [], []
    for wave in seconds:
        for group in wave.second():
            sums.append((group, len(shapes), 0))
            shapes.append(block_shape(group))
    joined = len(shapes)
    for number, wave in enumerate(thirds):
        if number == 0 or not together:
            shapes.append((*block_shape(wave.third()[0])[:2], 0))
        for group in wave.third():
            outer, rows, columns = shapes[-1]
            sums.append((group, len(shapes) - 1, columns))
            shapes[-1] = (outer, rows, columns + block_shape(group)[2])
    filled = add_blocks(order, bits, sums, shapes)
    start = 0
    for wave in seconds:
        wave.send(filled[start : start + len(wave.kinds)])
        start += len(wave.kinds)
    return filled[joined:]


def outer_sum(joined):
    joined = joined.reshape(-1, joined.shape[-1])
    return lax.psum_scatter(
        joined, "dp", axis_index_groups=outer_groups(), scatter_dimension=0, tiled=True
    )


def outer_swaps(joined):
    place = lax.axis_index("dp") >> 2
    block = lambda far: lax.dynamic_index_in_dim(joined, place ^ far, 0, False)
    return [swap_outer(block(far), far) for far in range(1, joined.shape[0])]


def last_shards(order, bits, joined, others, summed, spans):
    outer, rows, columns = joined.shape
    widths = [sum(size for _, _, size in span) for span in spans]

    def kernel(bits_ref, joined_ref, *refs):
        parts, refs = refs[: len(others)], refs[len(others) :]
        summed_ref, refs = refs[0], refs[1:]
        targets, (held, sem) = refs[:-2], refs[-2:]
        load = pltpu.make_async_copy(joined_ref.at[bits_ref[3]], held, sem)
        load.start()
        load.wait()
        total = held[...].astype(F32)
        for ref in parts:
            total += ref[...].astype(F32)
        for target, span in zip(targets, spans):
            at = 0
            for wave, start, size in span:
                if wave == 0:
                    values = total[:, start : start + size]
                else:
                    values = summed_ref[:, start : start + size].astype(F32)
                target[:, at : at + size] = values
                at += size

    return order.launch(
        kernel,
        "last_shards",
        [bits, joined, *others, summed],
        [pl.BlockSpec(memory_space=pltpu.HBM)]
        + [pl.BlockSpec(memory_space=pltpu.VMEM)] * (len(others) + 1),
        [pl.BlockSpec(memory_space=pltpu.VMEM)] * len(spans),
        [jax.ShapeDtypeStruct((rows, width), F32) for width in widths],
        [pltpu.VMEM((rows, columns), BF16), pltpu.SemaphoreType.DMA],
        None,
        {},
    )


FIRST_BACK = (swap_mem, swap_next)
SECOND_BACK = (swap_next, swap_mem)


def per_device(
    target_in,
    memory_in,
    bucket_ids,
    target_lengths,
    memory_mask,
    self_qkv,
    self_out,
    cross_q,
    cross_kv,
    cross_out,
    ffn_in,
    ffn_out,
    norm_gains,
    norm_biases,
    grad_out,
):
    both = ("dp", "mem")
    row_count, model_width = target_in.shape
    shard_rows = self_qkv.shape[0]
    outer = lax.axis_size("dp") // 4
    staged = shard_rows % 16 == 0 and shard_rows <= LANES and model_width % LANES == 0
    bits = place_bits()
    order = Order()
    own_index, pieces = lax.axis_index("mem"), lax.axis_size("mem")
    slot_count, mem_piece = memory_in.shape[3], memory_in.shape[4]

    norm_shard = jnp.concatenate((norm_gains, norm_biases), axis=1)
    norm_columns = norm_shard.shape[1]
    norm_shard = jnp.pad(norm_shard, ((0, 0), (0, LANES - norm_columns)))

    groups = [
        (self_qkv,),
        (cross_q, cross_out, norm_shard, cross_kv, self_out),
        (ffn_in,),
        (ffn_out,),
    ]
    if staged:
        shards = list(cast_shards(order, bits, groups))
    else:
        shards = [jnp.concatenate([part.astype(BF16) for part in group], axis=1) for group in groups]

    def gather(index, windows, direct=False):
        shard = shards[index]
        widths = [part.shape[1] for part in groups[index]]
        starts = [sum(widths[:i]) for i in range(len(widths))]
        if staged:
            wave = Wave(shard, windows, direct)
            return [Weight(wave, at, size) for at, size in zip(starts, widths)]
        full = lax.all_gather(shard, both, axis=0, tiled=True)
        rows = full.shape[0] // 16
        return [
            Weight(None, 0, size, full[:, at : at + size].reshape(8, 2, rows, size))
            for at, size in zip(starts, widths)
        ]

    def whole_sum(gradient):
        return lax.psum_scatter(gradient, both, scatter_dimension=0, tiled=True).astype(F32)

    class Turned:
        def __init__(self, *sources):
            self.sources = sources
            own, other = turn_rows(order, bits, sources, outer) if staged else (None, None)
            self.both = (own, swap_core(other)) if staged else ()

        def due(self):
            order.before(*self.both[1:])

    class Grad:
        def __init__(self, *places):
            self.sources = [source for _, source in places]
            self.turned = []
            for side in range(2 if staged else 0):
                for turned, source in places:
                    start = 0
                    for other in turned.sources:
                        if other is source:
                            break
                        start += other.shape[0]
                    stop = start + source.shape[0]
                    size = math.gcd(start, stop)
                    for at in range(start, stop, size):
                        self.turned.append((turned.both[side], at, size))

        def take(self, *cotangents):
            self.cotangents = cotangents
            if staged:
                self.cotangents += tuple(swap_core(part) for part in cotangents)

        def make(self, cut=None, **options):
            if staged:
                return weight_grad(
                    order, bits, self.turned, self.cotangents, outer, cut, **options
                )
            rows = [jnp.concatenate(part, axis=0) for part in (self.sources, self.cotangents)]
            return lead_dot(*rows).astype(BF16)

    def at_mem(values, index):
        return lax.dynamic_index_in_dim(values, index, 0, False)

    mem_rows = memory_in[0, :, 0]
    mem_live = memory_mask[0, :, 0]
    near_live = at_mem(mem_live, own_index)
    far_live = swap_mem(at_mem(mem_live, 1 - own_index))
    piece_shape = (mem_piece, model_width)
    if staged:
        moves = Moves(order, bits)
        source, near = moves.source(mem_rows), moves.target((slot_count, *piece_shape))
        sent = [moves.target(piece_shape) for _ in range(slot_count)]
        for slot in range(slot_count):
            at_far = lambda bits, slot=slot: (1 - bits[2], slot)
            at_near = lambda bits, slot=slot: (bits[2], slot)
            moves.move(source, at_far, piece_shape, (sent[slot], (slice(None),)))
            moves.move(source, at_near, piece_shape, (near, (slot,)))
        given = {}
        moves.then.append(lambda filled: given.update(near=filled[near], sent=[filled[t] for t in sent]))
        moves.run()
        near_rows, sent_rows = given["near"], given["sent"]
    else:
        near_rows = at_mem(mem_rows, own_index)
        sent_rows = [at_mem(mem_rows[:, slot], 1 - own_index) for slot in range(slot_count)]

    qkv_half = 3 * model_width // 2
    (w_qkv,) = gather(0, [(0, qkv_half, 0), (qkv_half, qkv_half, 1)], True)
    far_parts = [swap_mem(sent_rows[0])]
    if staged:
        order.before(far_parts[0], far_live)
        moves = Moves(order, bits)
        w_qkv.wave.first(moves)
        places = [moves.passed(shard) for shard in shards[1:]]
        moves.then.append(lambda filled: shards.__setitem__(slice(1, None), [filled[i] for i in places]))
        moves.run()
    lead = 5 * model_width // 2
    w_cq, w_co, w_norm, w_ckv, w_so = gather(
        1, [(0, lead, 0), (lead, 5 * model_width + LANES - lead, 1)]
    )
    (w_in,) = gather(2, [(0, ffn_in.shape[1], 0)])
    (w_out,) = gather(3, [(0, model_width, 1)])

    bucket = pick_entry(bucket_ids[0], own_index)
    lengths = target_lengths[0, 0]
    self_meta = jnp.stack([jnp.right_shift(jnp.int32(row_count), bucket), lengths[0], lengths[1]])
    cross_meta = bucket[None]
    live = jnp.concatenate((near_live, far_live), axis=1)
    key_bias = jnp.where(live == 1, 0.0, NEG_LARGE).astype(F32)
    key_columns = jnp.broadcast_to(key_bias[:, :, None], (*key_bias.shape, LANES))
    near_flat = near_rows.reshape(-1, model_width)
    slotted = (slot_count, mem_piece, 2 * model_width)

    def steps(*wanted):
        if staged:
            moves = Moves(order, bits)
            for weight, name in wanted:
                getattr(weight.wave, name)(moves)
            moves.run()

    steps((w_qkv, "second"))
    order.part()
    first_turned = Turned(target_in, near_flat)
    steps((w_ckv, "first"))
    order.part()
    steps((w_qkv, "third"))
    first_turned.due()
    order.part()
    steps((w_ckv, "second"))
    (united,) = project(order, "self_project", bits, w_qkv, [target_in], 1024)
    far_parts += [swap_mem(part) for part in gate(order, bits, sent_rows[1:])]
    steps((w_in, "first"))
    self_mixed, self_log = self_forward(order, self_meta, united)
    far_flat = jnp.concatenate(far_parts, axis=0)
    order.part()
    steps((w_ckv, "third"))
    order.before(*far_parts[1:])
    order.part()
    steps((w_out, "first"))
    table = norm_table(order, bits, w_norm)
    near_kv, far_kv = project(order, "cross_project", bits, w_ckv, [near_flat, far_flat], 1024)
    near_kv, far_kv = near_kv.reshape(slotted), far_kv.reshape(slotted)
    order.part()
    steps((w_in, "second"), (w_out, "second"))
    sum_one, first_out, first_low, cross_query = mix_norm(
        order, "self_mix", bits, w_so, self_mixed, target_in, table, 0, w_cq
    )
    cross_mixed, cross_log = cross_forward(
        order, cross_meta, cross_query, near_kv, far_kv, key_bias[:, None, :]
    )
    sum_two, second_out, second_low = mix_norm(
        order, "cross_mix", bits, w_co, cross_mixed, first_out, table, 1
    )
    order.part()
    steps((w_in, "third"))
    later = Turned(self_mixed, first_low, cross_mixed, second_low, far_flat)
    order.part()
    steps((w_out, "third"))
    activated, slope = feed_in(order, bits, w_in, second_low)
    later.due()
    hidden = Turned(activated)
    layer_out, grad_three, grad_ffn, stats_three = feed_out(
        order, bits, w_out, activated, second_out, table, grad_out
    )
    qkv_grad = Grad((first_turned, target_in))
    so_grad = Grad((later, self_mixed))
    ckv_grad = Grad((first_turned, near_flat), (later, far_flat))
    cq_grad = Grad((later, first_low))
    co_grad = Grad((later, cross_mixed))
    in_grad = Grad((later, second_low))
    out_grad = Grad((hidden, activated))

    shards = {}

    def spread(name, parts, kinds):
        if staged:
            return Spread(parts, kinds)
        shards[name] = whole_sum(parts)
        return None

    def advance(seconds=(), thirds=()):
        if staged:
            waves = [wave for _, wave in thirds]
            joined = spread_steps(order, bits, seconds, waves)
            for (name, _), part in zip(thirds, joined):
                shards[name] = outer_sum(part)

    out_grad.take(grad_ffn)
    out_wave = spread("out", out_grad.make(model_width // 2), (0, 1))
    grad_hidden = feed_back(order, bits, w_out, grad_ffn, slope)
    in_grad.take(grad_hidden)
    grad_two, grad_cross_out, grad_cross_mixed, stats_two = norm_back(
        order, "cross_back", bits, w_in, grad_hidden, grad_three, sum_two, table, 1, w_co
    )
    co_grad.take(grad_cross_out)
    order.part()
    advance([out_wave])
    in_wave = spread("in", in_grad.make(2 * model_width), (0, 1))
    pair_width = 2 * model_width
    near_parts = co_grad.make(place=(0, 0, pair_width))
    grad_query_low, grad_near_kv, grad_far_kv = cross_backward(
        order,
        cross_meta,
        cross_query,
        near_kv,
        far_kv,
        key_columns,
        cross_mixed,
        grad_cross_mixed,
        cross_log,
    )
    cq_grad.take(grad_query_low)
    ckv_grad.take(grad_near_kv, grad_far_kv)
    order.part()
    advance([in_wave], [("out", out_wave)])

    def memory_back(cotangent):
        spans = [(0, start, start, model_width) for start in (0, model_width)]
        return input_back(order, "memory_back", bits, w_ckv, [cotangent], None, spans)

    grad_one, grad_self_out, grad_self_mixed, stats_one = norm_back(
        order, "self_back", bits, w_cq, grad_query_low, grad_two, sum_one, table, 0, w_so
    )
    so_grad.take(grad_self_out)
    stats = [jnp.sum(s.reshape(2, 8, model_width), axis=1) for s in (stats_one, stats_two, stats_three)]
    norm_grads = [
        jnp.pad(jnp.stack([s[i] for s in stats], axis=1), ((0, 0), (0, LANES - len(stats))))
        for i in range(2)
    ]
    norm_grads = jnp.concatenate(norm_grads, axis=1).astype(BF16)
    if staged:
        own, other = relative_rows(bits, norm_grads, outer)
        own = (own.astype(F32) + swap_core(other).astype(F32)).astype(BF16)
        norm_grads = (own[..., :LANES], own[..., LANES:])
        near_parts = cq_grad.make(place=(0, model_width, pair_width), held=near_parts)
        mid_parts = [*near_parts, *ckv_grad.make(place=(1, 0, pair_width))]
    else:
        mid_parts = jnp.concatenate([near_parts, cq_grad.make(), ckv_grad.make()], axis=1)
    mid_wave = spread("mid", mid_parts, (0, 1))
    order.part()
    advance([], [("in", in_wave)])
    grad_united = self_backward(
        order,
        self_meta,
        united,
        self_mixed,
        grad_self_mixed,
        self_log,
        0,
        model_width // LANES,
    )
    qkv_grad.take(grad_united)
    order.part()
    advance([mid_wave])
    qkv_wave = spread("qkv", qkv_grad.make(qkv_half), (0, 1))
    if staged:
        order.before(shards["out"], shards["in"])
        order.part()
        advance([], [("mid", mid_wave)])
    half_width = model_width // 2
    if staged:
        so_wave = spread("so", so_grad.make(half_width, extra=norm_grads), (0, 1))
    else:
        part = so_grad.make()
        columns = [part[:, :half_width], norm_grads[:, :LANES], part[:, half_width:], norm_grads[:, LANES:]]
        so_wave = spread("so", jnp.concatenate(columns, axis=1), (0, 1))
    split = half_width + LANES
    grad_far = memory_back(grad_far_kv)
    if staged:
        order.part()
        advance([qkv_wave, so_wave])
        (grad_far,) = gate(order, bits, [grad_far])
    grad_far = swap_mem(grad_far)
    grad_near = memory_back(grad_near_kv)
    if staged:
        order.before(shards["mid"])
        order.part()
        (joined,) = spread_steps(order, bits, [], [so_wave, qkv_wave], True)
        others = outer_swaps(joined)
    target_grad = input_back(
        order,
        "target_back",
        bits,
        w_qkv,
        [grad_united],
        grad_one,
        [(0, start, start, model_width) for start in range(0, w_qkv.width, model_width)],
    )
    so_spans = [(0, 0, half_width), (0, split, half_width)]
    norm_spans = [[(0, half_width, 3)], [(0, split + half_width, 3)]]
    mid_spans = [[(1, i * model_width, model_width)] for i in range(2)]
    mid_spans.append([(1, 2 * model_width, 2 * model_width)])
    spans = [[(0, 2 * split, 2 * qkv_half)], so_spans, *norm_spans, *mid_spans]
    if staged:
        last = last_shards(order, bits, joined, others, shards["mid"], spans)
        moves = Moves(order, bits)
        target = moves.target((2, *near_flat.shape))
        for number, part in enumerate((grad_near, grad_far)):
            place = lambda bits, number=number: (bits[2] ^ number,)
            moves.move(moves.source(part), (slice(None),), near_flat.shape, (target, place))
        moves.then.append(lambda filled: shards.update(memory=filled[target]))
        moves.run()
        grad_pair = shards["memory"]
    else:
        grad_pair = jnp.stack((grad_near, grad_far))
        grad_pair = jnp.where(own_index == 0, grad_pair, grad_pair[::-1])
        sources = (jnp.concatenate((shards["so"], shards["qkv"]), axis=1), shards["mid"])
        last = [
            jnp.concatenate([sources[w][:, at : at + size] for w, at, size in span], axis=1)
            for span in spans
        ]
    qkv_shard, so_shard, gains, biases, co_shard, cq_shard, ckv_shard = last

    return (
        layer_out,
        target_grad,
        grad_pair.reshape(1, pieces, 1, *near_rows.shape),
        qkv_shard,
        so_shard,
        cq_shard,
        ckv_shard,
        co_shard,
        shards["in"].astype(F32),
        shards["out"].astype(F32),
        gains,
        biases,
    )


def solution(mesh):
    rows = P(("dp", "mem"), None)
    memory = P("dp", None, "mem", None, None, None)
    return jax.shard_map(
        per_device,
        mesh=mesh,
        in_specs=(
            rows,
            memory,
            P("dp", None),
            P("dp", "mem", None),
            P("dp", None, "mem", None, None),
        )
        + (rows,) * 10,
        out_specs=(rows, rows, memory) + (rows,) * 9,
        check_vma=False,
    )
```

```python
import math

import jax
import jax.numpy as jnp
from jax import lax
from jax.experimental import pallas as pl
from jax.experimental.pallas import tpu as pltpu
from jax.sharding import PartitionSpec as P

HD = 64
LANES = 128
PAIRS = 2
WIDE = PAIRS * LANES
ALPHA = 300.0**0.25
NEG_LARGE = -1e30
EPSILON = 1e-05
VMEM_BYTES = 64 * 1024 * 1024 - 128 * 1024
SCALE = HD**-0.5
BF16 = jnp.bfloat16
F32 = jnp.float32


def plain_dot(first_op, second_op):
    return jnp.dot(first_op, second_op, preferred_element_type=F32)


def lead_dot(first_op, second_op):
    return lax.dot_general(
        first_op, second_op, (((0,), (0,)), ((), ())), preferred_element_type=F32
    )


def back_dot(first_op, second_op):
    return lax.dot_general(
        first_op, second_op, (((1,), (1,)), ((), ())), preferred_element_type=F32
    )


def pick_entry(values, wanted):
    return jnp.sum(jnp.where(jnp.arange(values.shape[0]) == wanted, values, 0))


def kernel_params():
    return pltpu.CompilerParams(vmem_limit_bytes=VMEM_BYTES)


class Order:
    def __init__(self):
        self.last, self.due, self.parted = None, [], False

    def before(self, *arrays):
        self.due += arrays

    def part(self):
        self.parted = True

    def launch(self, kernel, name, operands, in_specs, out_specs, out_shape, scratch, grid, aliases):
        ties = self.due + ([self.last] if self.last is not None else [])
        ties = [tie for tie in ties if not any(tie is operand for operand in operands)]
        self.due = []
        count, n_ties = len(operands), len(ties)

        def tied(*refs):
            kernel(*refs[:count], *refs[count + n_ties :])

        specs = list(in_specs) + [pl.BlockSpec(memory_space=pltpu.HBM)] * n_ties
        cost = pl.CostEstimate(
            flops=10**12 if self.parted else 10**6, bytes_accessed=1, transcendentals=0
        )
        self.parted = False
        if grid is None:
            run = pl.pallas_call(
                tied,
                in_specs=[pl.BlockSpec(memory_space=pltpu.SMEM)] + specs,
                out_specs=out_specs,
                out_shape=out_shape,
                scratch_shapes=scratch,
                input_output_aliases=aliases,
                compiler_params=kernel_params(),
                cost_estimate=cost,
                name=name,
            )
        else:
            run = pl.pallas_call(
                tied,
                grid_spec=pltpu.PrefetchScalarGridSpec(
                    num_scalar_prefetch=1,
                    grid=grid,
                    in_specs=specs,
                    out_specs=out_specs,
                    scratch_shapes=scratch,
                ),
                out_shape=out_shape,
                input_output_aliases=aliases,
                compiler_params=kernel_params(),
                cost_estimate=cost,
                name=name,
            )
        results = run(*operands, *ties)
        self.last = results[0]
        return results


def whole_spec(shape):
    return pl.BlockSpec(shape, lambda *_: (0,) * len(shape))


def head_lanes(rows, head):
    lane = lax.broadcasted_iota(jnp.int32, (rows, LANES), 1)
    return (lane < HD) if head == 0 else (lane >= HD)


def visible(query_ids, key_ids, slot_len, first_len, second_len):
    query_slot = (query_ids >= slot_len).astype(jnp.int32)
    key_slot = (key_ids >= slot_len).astype(jnp.int32)
    place = key_ids - key_slot * slot_len
    limit = jnp.where(key_slot == 0, first_len, second_len)
    return (query_slot == key_slot) & (key_ids <= query_ids) & (place < limit)


def pair_forward(query, keys, values, bias):
    rows, key_rows = query.shape[0], keys.shape[0]
    mixed, peaks = [], []
    for head in range(2):
        mine = head_lanes(rows, head)
        masked = jnp.where(mine, query * BF16(SCALE), BF16(0))
        scores = back_dot(masked, keys) + bias
        peak = jnp.max(scores, axis=1, keepdims=True)
        raised = jnp.exp(scores - peak).astype(BF16)
        widened = jnp.where(head_lanes(key_rows, head), values, BF16(1))
        mixed.append(plain_dot(raised, widened))
        peaks.append(peak)
    first = head_lanes(rows, 0)
    totals = pltpu.roll(jnp.where(first, mixed[1], mixed[0]), HD, 1)
    joined = jnp.where(first, mixed[0], mixed[1])
    log_totals = jnp.where(first, peaks[0], peaks[1]) + jnp.log(totals)
    return joined / totals, log_totals


def pair_backward(query, keys, values, upstream, bias, log_rows, delta_rows):
    rows, key_rows = query.shape[0], keys.shape[0]
    grad_q, grad_k, grad_v = None, None, None
    for head in range(2):
        mine = head_lanes(rows, head)
        masked = jnp.where(mine, query * BF16(SCALE), BF16(0))
        masked_up = jnp.where(mine, upstream, BF16(0))
        scores = back_dot(keys, masked) + bias
        probs = jnp.exp(scores - log_rows[head])
        grad_probs = back_dot(values, masked_up)
        grad_scores = (probs * (grad_probs - delta_rows[head])).astype(BF16)
        part_v = plain_dot(probs.astype(BF16), masked_up)
        part_k = plain_dot(grad_scores, masked)
        masked_keys = jnp.where(head_lanes(key_rows, head), keys, BF16(0))
        part_q = lead_dot(grad_scores, masked_keys)
        grad_q = part_q if grad_q is None else grad_q + part_q
        grad_k = part_k if grad_k is None else grad_k + part_k
        grad_v = part_v if grad_v is None else grad_v + part_v
    return grad_q * SCALE, grad_k, grad_v


def stat_rows(log_block, mixed, upstream):
    log_turned = log_block.T
    products = (mixed.astype(F32) * upstream.astype(F32)).T
    log_rows = [log_turned[:1], log_turned[HD : HD + 1]]
    delta_rows = [jnp.sum(products[h * HD : (h + 1) * HD], axis=0, keepdims=True) for h in range(2)]
    return log_rows, delta_rows


def pair_lanes(pair):
    return slice(pair * LANES, (pair + 1) * LANES)


def self_forward_kernel(meta, q_ref, k_ref, v_ref, mixed_ref, log_ref, bias):
    rows = q_ref.shape[0]

    @pl.when(pl.program_id(0) == 0)
    def _():
        query_ids = lax.broadcasted_iota(jnp.int32, (rows, rows), 0)
        key_ids = lax.broadcasted_iota(jnp.int32, (rows, rows), 1)
        seen = visible(query_ids, key_ids, meta[0], meta[1], meta[2])
        bias[...] = jnp.where(seen, 0.0, NEG_LARGE)

    half = rows // 2
    for pair in range(PAIRS):
        lanes = pair_lanes(pair)
        for start, stop in ((0, half), (half, rows)):
            mixed, log_totals = pair_forward(
                q_ref[start:stop, lanes],
                k_ref[:stop, lanes],
                v_ref[:stop, lanes],
                bias[start:stop, :stop],
            )
            mixed_ref[start:stop, lanes] = mixed.astype(BF16)
            log_ref[start:stop, lanes] = log_totals


def self_forward(order, meta, united):
    rows, width = united.shape[0], united.shape[1] // 3
    steps = width // WIDE
    spec = lambda third: pl.BlockSpec((rows, WIDE), lambda i, _: (0, third * steps + i))
    return order.launch(
        self_forward_kernel,
        "self_forward",
        [meta, united, united, united],
        [spec(0), spec(1), spec(2)],
        [spec(0), spec(0)],
        [jax.ShapeDtypeStruct((rows, width), kind) for kind in (BF16, F32)],
        [pltpu.VMEM((rows, rows), F32)],
        (steps,),
        {},
    )


def self_backward_kernel(
    meta, q_ref, k_ref, v_ref, mixed_ref, up_ref, log_ref, grad_ref, bias
):
    rows = q_ref.shape[0]
    width = grad_ref.shape[1] // 3
    step = pl.program_id(0)

    @pl.when(step == 0)
    def _():
        key_ids = lax.broadcasted_iota(jnp.int32, (rows, rows), 0)
        query_ids = lax.broadcasted_iota(jnp.int32, (rows, rows), 1)
        seen = visible(query_ids, key_ids, meta[0], meta[1], meta[2])
        bias[...] = jnp.where(seen, 0.0, NEG_LARGE)

    half = rows // 2
    for pair in range(PAIRS):
        lanes = pair_lanes(pair)
        log_rows, delta_rows = stat_rows(log_ref[:, lanes], mixed_ref[:, lanes], up_ref[:, lanes])
        parts = []
        for start, stop in ((0, half), (half, rows)):
            parts.append(
                pair_backward(
                    q_ref[start:stop, lanes],
                    k_ref[:stop, lanes],
                    v_ref[:stop, lanes],
                    up_ref[start:stop, lanes],
                    bias[:stop, start:stop],
                    [row[:, start:stop] for row in log_rows],
                    [row[:, start:stop] for row in delta_rows],
                )
            )
        low, high = parts
        at = step * WIDE + pair * LANES
        columns = lambda third: pl.ds(pl.multiple_of(third * width + at, LANES), LANES)
        grad_ref[:half, columns(0)] = low[0].astype(BF16)
        grad_ref[half:, columns(0)] = high[0].astype(BF16)
        for third in (1, 2):
            grad_ref[:half, columns(third)] = (low[third] + high[third][:half]).astype(BF16)
            grad_ref[half:, columns(third)] = high[third][half:].astype(BF16)


def self_backward(order, meta, united, mixed, upstream, log_totals):
    rows, width = mixed.shape
    steps = width // WIDE
    spec = lambda third: pl.BlockSpec((rows, WIDE), lambda i, _: (0, third * steps + i))
    shape = (rows, 3 * width)
    return order.launch(
        self_backward_kernel,
        "self_backward",
        [meta, united, united, united, mixed, upstream, log_totals],
        [spec(0), spec(1), spec(2), spec(0), spec(0), spec(0)],
        [whole_spec(shape)],
        [jax.ShapeDtypeStruct(shape, BF16)],
        [pltpu.VMEM((rows, rows), F32)],
        (steps,),
        {},
    )[0]


def join_keys(near_ref, far_ref, joined):
    slots, piece = near_ref.shape[0], near_ref.shape[1]
    for slot in range(slots):
        joined[slot, :piece, :] = near_ref[slot]
        joined[slot, piece:, :] = far_ref[slot]


def cross_forward_kernel(
    meta, q_ref, kn_ref, vn_ref, kf_ref, vf_ref, bias_ref, mixed_ref, log_ref, keys, values
):
    half = q_ref.shape[0] // 2
    join_keys(kn_ref, kf_ref, keys)
    join_keys(vn_ref, vf_ref, values)
    for pair in range(PAIRS):
        lanes = pair_lanes(pair)
        for part in range(2):
            slot = part * meta[0]
            rows = slice(part * half, (part + 1) * half)
            mixed, log_totals = pair_forward(
                q_ref[rows, lanes], keys[slot, :, lanes], values[slot, :, lanes], bias_ref[slot]
            )
            mixed_ref[rows, lanes] = mixed.astype(BF16)
            log_ref[rows, lanes] = log_totals


def cross_specs(rows, slots, piece, steps):
    row_spec = pl.BlockSpec((rows, WIDE), lambda i, _: (0, i))
    half = lambda at: pl.BlockSpec((slots, piece, WIDE), lambda i, _: (0, 0, at * steps + i))
    return row_spec, [row_spec, half(0), half(1), half(0), half(1)]


def cross_forward(order, meta, query, near, far, bias):
    rows, width = query.shape
    slots, piece = near.shape[0], near.shape[1]
    steps = width // WIDE
    row_spec, specs = cross_specs(rows, slots, piece, steps)
    return order.launch(
        cross_forward_kernel,
        "cross_forward",
        [meta, query, near, near, far, far, bias],
        specs + [whole_spec(bias.shape)],
        [row_spec, row_spec],
        [jax.ShapeDtypeStruct((rows, width), kind) for kind in (BF16, F32)],
        [pltpu.VMEM((slots, 2 * piece, WIDE), BF16)] * 2,
        (steps,),
        {},
    )


def cross_backward_kernel(
    meta,
    q_ref,
    kn_ref,
    vn_ref,
    kf_ref,
    vf_ref,
    bias_ref,
    mixed_ref,
    up_ref,
    log_ref,
    grad_q_ref,
    grad_near_ref,
    grad_far_ref,
    keys,
    values,
):
    half = q_ref.shape[0] // 2
    slots, piece = kn_ref.shape[0], kn_ref.shape[1]
    width = grad_near_ref.shape[1] // 2
    join_keys(kn_ref, kf_ref, keys)
    join_keys(vn_ref, vf_ref, values)
    split = meta[0].astype(F32)
    for pair in range(PAIRS):
        lanes = pair_lanes(pair)
        log_rows, delta_rows = stat_rows(log_ref[:, lanes], mixed_ref[:, lanes], up_ref[:, lanes])
        parts = []
        for part in range(2):
            slot = part * meta[0]
            rows = slice(part * half, (part + 1) * half)
            bias_column = bias_ref[slot]
            grads = pair_backward(
                q_ref[rows, lanes],
                keys[slot, :, lanes],
                values[slot, :, lanes],
                up_ref[rows, lanes],
                jnp.concatenate([bias_column] * (half // LANES), axis=1),
                [row[:, rows] for row in log_rows],
                [row[:, rows] for row in delta_rows],
            )
            grad_q_ref[rows, lanes] = grads[0].astype(BF16)
            parts.append(grads)
        start = pl.program_id(0) * WIDE + pair * LANES
        for which in range(2):
            early, late = parts[0][1 + which], parts[1][1 + which]
            columns = pl.ds(pl.multiple_of(which * width + start, LANES), LANES)
            by_slot = (early + late * (1.0 - split), late * split)
            for slot in range(slots):
                for source, target in enumerate((grad_near_ref, grad_far_ref)):
                    target[slot * piece : (slot + 1) * piece, columns] = by_slot[slot][
                        source * piece : (source + 1) * piece
                    ].astype(BF16)


def cross_backward(order, meta, query, near, far, bias, mixed, upstream, log_totals):
    rows, width = query.shape
    slots, piece = near.shape[0], near.shape[1]
    steps = width // WIDE
    memory = (slots * piece, 2 * width)
    row_spec, specs = cross_specs(rows, slots, piece, steps)
    return order.launch(
        cross_backward_kernel,
        "cross_backward",
        [meta, query, near, near, far, far, bias, mixed, upstream, log_totals],
        specs + [whole_spec(bias.shape)] + [row_spec] * 3,
        [row_spec, whole_spec(memory), whole_spec(memory)],
        [jax.ShapeDtypeStruct(shape, BF16) for shape in ((rows, width), memory, memory)],
        [pltpu.VMEM((slots, 2 * piece, WIDE), BF16)] * 2,
        (steps,),
        {},
    )


def swap_core(values):
    size = lax.axis_size("dp")
    return lax.ppermute(values, "dp", [(i, i ^ 1) for i in range(size)])


def swap_next(values):
    size = lax.axis_size("dp")
    return lax.ppermute(values, "dp", [(i, i ^ 2) for i in range(size)])


def swap_mem(values):
    return lax.ppermute(values, "mem", [(0, 1), (1, 0)])


def swap_outer(values, far):
    size = lax.axis_size("dp")
    return lax.ppermute(values, "dp", [(i, i ^ (4 * far)) for i in range(size)])


def outer_groups():
    size = lax.axis_size("dp")
    return [list(range(base, size, 4)) for base in range(4)]


def place_bits():
    dp, mem = lax.axis_index("dp"), lax.axis_index("mem")
    return jnp.stack([(dp >> 1) & 1, dp & 1, mem, dp >> 2]).astype(jnp.int32)


def outer_gather(shard):
    stacked = lax.all_gather(shard, "dp", axis_index_groups=outer_groups(), axis=0, tiled=True)
    return stacked.reshape(-1, *shard.shape)


def gate(order, bits, arrays):
    def kernel(*refs):
        pass

    return order.launch(
        kernel,
        "gate",
        [bits, *arrays],
        [pl.BlockSpec(memory_space=pltpu.HBM)] * len(arrays),
        [pl.BlockSpec(memory_space=pltpu.HBM)] * len(arrays),
        [jax.ShapeDtypeStruct(array.shape, array.dtype) for array in arrays],
        [],
        None,
        {1 + i: i for i in range(len(arrays))},
    )


class Moves:
    def __init__(self, order, bits):
        self.order, self.bits = order, bits
        self.sources, self.shapes, self.moves, self.aliases, self.then = [], [], [], {}, []

    def source(self, array):
        self.sources.append(array)
        return len(self.sources) - 1

    def target(self, shape, held=None):
        self.shapes.append(shape)
        if held is not None:
            self.aliases[1 + self.source(held)] = len(self.shapes) - 1
        return len(self.shapes) - 1

    def passed(self, array):
        return self.target(array.shape, array)

    def move(self, source, source_at, shape, *goals):
        self.moves.append((source, source_at, shape, goals))

    def run(self):
        moves, n_in, n_out = self.moves, len(self.sources), len(self.shapes)
        most = max([len(move[3]) for move in moves] + [0])

        def kernel(bits_ref, *refs):
            bits = [bits_ref[i] for i in range(4)]
            taken, given = refs[:n_in], refs[n_in : n_in + n_out]
            slots, sems = refs[n_in + n_out : -1], refs[-1]
            loads, stores = [], []
            for number, (source, source_at, _, goals) in enumerate(moves):
                slot = slots[number]
                loads.append(
                    pltpu.make_async_copy(
                        taken[source].at[source_at(bits) if callable(source_at) else source_at],
                        slot,
                        sems.at[0, number],
                    )
                )
                stores.append(
                    [
                        pltpu.make_async_copy(
                            slot, given[which].at[at(bits) if callable(at) else at], sems.at[1 + i, number]
                        )
                        for i, (which, at) in enumerate(goals)
                    ]
                )
            for load in loads:
                load.start()
            for load, group in zip(loads, stores):
                load.wait()
                for store in group:
                    store.start()
            for group in stores:
                for store in group:
                    store.wait()

        filled = self.order.launch(
            kernel,
            "move_blocks",
            [self.bits, *self.sources],
            [pl.BlockSpec(memory_space=pltpu.HBM)] * n_in,
            [pl.BlockSpec(memory_space=pltpu.HBM)] * n_out,
            [jax.ShapeDtypeStruct(shape, BF16) for shape in self.shapes],
            [pltpu.VMEM(shape, BF16) for _, _, shape, _ in moves]
            + [pltpu.SemaphoreType.DMA((1 + most, max(1, len(moves))))],
            None,
            self.aliases,
        )
        for step in self.then:
            step(filled)


def cast_shards(order, bits, groups):
    shapes = [(group[0].shape[0], sum(part.shape[1] for part in group)) for group in groups]
    parts = [part for group in groups for part in group]

    def kernel(bits_ref, *refs):
        number = 0
        for group, target in zip(groups, refs[len(parts) :]):
            start = 0
            for part in group:
                stop = start + part.shape[1]
                target[:, start:stop] = refs[number][...].astype(BF16)
                start, number = stop, number + 1

    return order.launch(
        kernel,
        "cast_shards",
        [bits, *parts],
        [pl.BlockSpec(memory_space=pltpu.VMEM)] * len(parts),
        [pl.BlockSpec(memory_space=pltpu.VMEM)] * len(shapes),
        [jax.ShapeDtypeStruct(shape, BF16) for shape in shapes],
        [],
        None,
        {},
    )


FIRST = (swap_next, swap_mem)
SECOND = (swap_mem, swap_next)


class Wave:
    def __init__(self, shard, windows, direct):
        self.windows = [(pl.ds(start, size), kind) for start, size, kind in windows]
        self.rows, self.columns = shard.shape
        self.outer = lax.axis_size("dp") // 4
        if direct:
            self.shards = [shard] + [swap_outer(shard, far) for far in range(1, self.outer)]
        else:
            self.stacked = outer_gather(shard)
        self.direct = direct

    def first(self, moves):
        def send(parts):
            self.pairs = [(part, FIRST[kind](part)) for part, (_, kind) in zip(parts, self.windows)]

        if not self.direct and len(self.windows) == 1:
            target = moves.passed(self.stacked)
            moves.then.append(lambda filled: send([filled[target]]))
            return
        targets = [moves.target((self.outer, self.rows, w.size)) for w, _ in self.windows]
        sources = [moves.source(part) for part in (self.shards if self.direct else [self.stacked])]
        for block in range(self.outer):
            for target, (window, _) in zip(targets, self.windows):
                shape = (self.rows, window.size)
                if self.direct:
                    goal = (target, lambda bits, block=block: (bits[3] ^ block,))
                    moves.move(sources[block], (slice(None), window), shape, goal)
                else:
                    goal = (target, (block,))
                    moves.move(sources[0], (block, slice(None), window), shape, goal)
        moves.then.append(lambda filled: send([filled[target] for target in targets]))

    def place(self, kind, second, first, block, window):
        near, mem = (first, second) if kind == 0 else (second, first)
        return lambda bits: (block, bits[0] ^ near, bits[2] ^ mem, slice(None), window)

    def second(self, moves):
        sources = [[moves.source(part) for part in pair] for pair in self.pairs]
        targets = [moves.target((2, *pair[0].shape)) for pair in self.pairs]
        own = moves.target((self.outer, 2, 2, self.rows, self.columns))
        for block in range(self.outer):
            for number, (window, kind) in enumerate(self.windows):
                for side in range(2):
                    goal = (targets[number], (side, block))
                    again = (own, self.place(kind, 0, side, block, window))
                    shape = (self.rows, window.size)
                    moves.move(sources[number][side], (block,), shape, goal, again)

        def send(filled):
            self.own = filled[own]
            self.far = [
                SECOND[kind](filled[target]) for target, (_, kind) in zip(targets, self.windows)
            ]

        moves.then.append(send)

    def third(self, moves):
        own = moves.target(self.own.shape, self.own)
        for number, (window, kind) in enumerate(self.windows):
            source = moves.source(self.far[number])
            for block in range(self.outer):
                for side in range(2):
                    goal = (own, self.place(kind, 1, side, block, window))
                    moves.move(source, (side, block), (self.rows, window.size), goal)

        def send(filled):
            shape = (2 * self.outer, 2 * self.rows, self.columns)
            self.own = filled[own].reshape(shape)
            self.other = swap_core(self.own)

        moves.then.append(send)


class Weight:
    def __init__(self, wave, start, width, whole=None):
        self.wave, self.start, self.width, self.whole = wave, start, width, whole
        if whole is not None:
            self.blocks, self.rows = whole.shape[0], whole.shape[2]
        else:
            self.blocks, self.rows = 2 * wave.outer, 2 * wave.rows
        self.features = self.blocks * 2 * self.rows

    def pieces(self):
        return [self.whole] if self.whole is not None else [self.wave.own, self.wave.other]

    def copies(self, kind, start, size, bits, find, target):
        if kind == "columns":
            blocks, columns = slice(None), pl.ds(self.start + start, size)
        else:
            blocks, columns = pl.ds(start, size), pl.ds(self.start, self.width)
        if self.whole is not None:
            return [(find(self.whole).at[blocks, :, :, columns], target)]
        return [
            (find(array).at[blocks, :, columns], target.at[:, bits[1] ^ core])
            for core, array in enumerate((self.wave.own, self.wave.other))
        ]


def weight_call(order, name, bits, weights, plan, inputs, outs, scratch, body, streams=None, sends=0):
    streams = streams or {}
    arrays = []
    for weight in weights:
        arrays += [a for a in weight.pieces() if not any(a is b for b in arrays)]
    kind, size = plan[0][1], plan[0][3]
    lead = weights[plan[0][0]]
    if kind == "columns":
        chunk = (lead.blocks, 2, lead.rows, size)
    else:
        chunk = (size, 2, lead.rows, lead.width)
    n_in, n_arrays, n_out = len(inputs), len(arrays), len(outs)
    streamed = sorted(streams)
    most = max([1] + [inputs[i].shape[1] // streams[i] for i in streamed])

    def kernel(bits_ref, *refs):
        ins, refs = list(refs[:n_in]), refs[n_in:]
        pieces, refs = refs[:n_arrays], refs[n_arrays:]
        out_refs, refs = refs[:n_out], refs[n_out:]
        held, sems, stream_sems, send_sems = refs[-4:]
        staged = refs[: n_out if sends else 0]
        stream_refs = refs[len(staged) : len(staged) + len(streamed)]
        rest = refs[len(staged) + len(streamed) : -4]
        bits_now = [bits_ref[i] for i in range(3)]

        def find(array):
            return next(ref for ref, known in zip(pieces, arrays) if known is array)

        def issue(number):
            which, kind, start, size = plan[number]
            slot = number % 2
            for source, target in weights[which].copies(
                kind, start, size, bits_now, find, held.at[slot]
            ):
                pltpu.make_async_copy(source, target, sems.at[slot]).start()

        taken, coming, sent = [0], {}, []

        def fetch():
            number = taken[0]
            taken[0] += 1
            if number + 1 < len(plan):
                issue(number + 1)
            slot = number % 2
            pltpu.make_async_copy(held.at[slot], held.at[slot], sems.at[slot]).wait()
            return held[slot].reshape(-1, chunk[-1])

        def need(which, part=0):
            coming.pop((which, part)).wait()

        def send(which, columns=None):
            columns = slice(None) if columns is None else columns
            copy = pltpu.make_async_copy(
                staged[which].at[:, columns], out_refs[which].at[:, columns], send_sems.at[len(sent)]
            )
            copy.start()
            sent.append(copy)

        fetch.need, fetch.send = need, send
        issue(0)
        for number, which in enumerate(streamed):
            count = streams[which]
            for part in range(inputs[which].shape[1] // count):
                columns = pl.ds(part * count, count)
                copy = pltpu.make_async_copy(
                    ins[which].at[:, columns],
                    stream_refs[number].at[:, columns],
                    stream_sems.at[number, part],
                )
                copy.start()
                coming[which, part] = copy
            ins[which] = stream_refs[number]
        body(fetch, ins, staged if sends else out_refs, rest)
        for copy in sent + list(coming.values()):
            copy.wait()

    hbm, vmem = pl.BlockSpec(memory_space=pltpu.HBM), pl.BlockSpec(memory_space=pltpu.VMEM)
    return order.launch(
        kernel,
        name,
        [bits, *inputs, *arrays],
        [hbm if i in streams else vmem for i in range(n_in)] + [hbm] * n_arrays,
        [hbm if sends else vmem] * n_out,
        [jax.ShapeDtypeStruct(shape, kind) for shape, kind in outs],
        ([pltpu.VMEM(shape, kind) for shape, kind in outs] if sends else [])
        + [pltpu.VMEM(inputs[i].shape, inputs[i].dtype) for i in streamed]
        + [pltpu.VMEM(shape, kind) for shape, kind in scratch]
        + [
            pltpu.VMEM((2, *chunk), BF16),
            pltpu.SemaphoreType.DMA((2,)),
            pltpu.SemaphoreType.DMA((max(1, len(streamed)), most)),
            pltpu.SemaphoreType.DMA((max(1, sends),)),
        ],
        None,
        {},
    )


def columns_plan(which, width, size):
    return [(which, "columns", start, size) for start in range(0, width, size)]


def row_blocks(rows, size, step):
    def run(i, carry):
        step(pl.ds(pl.multiple_of(i * size, size), size))
        return carry

    lax.fori_loop(0, rows // size, run, 0)


def normed_parts(values):
    centred = values - jnp.mean(values, axis=-1, keepdims=True)
    spread = jnp.mean(centred * centred, axis=-1, keepdims=True)
    rate = lax.rsqrt(spread + EPSILON)
    return centred * rate, rate


def norm_gradient(normed, rate, gain, cotangent):
    inner = cotangent * gain
    mean_inner = jnp.mean(inner, axis=-1, keepdims=True)
    mean_both = jnp.mean(inner * normed, axis=-1, keepdims=True)
    return rate * (inner - mean_inner - normed * mean_both)


def add_stats(stats, normed, cotangent):
    fold = lambda values: jnp.sum(values.reshape(-1, 8, values.shape[-1]), axis=0)
    stats[:8, :] += fold(cotangent * normed)
    stats[8:, :] += fold(cotangent)


def norm_table(order, bits, weight):
    features = weight.features

    def body(fetch, ins, outs, scratch):
        outs[0][...] = fetch().astype(F32).T[:8]

    return weight_call(
        order, "norm_table", bits, [weight], [(0, "columns", 0, LANES)], [],
        [((8, features), F32)], [], body,
    )[0]


def project(order, name, bits, weight, sources, size, groups=None):
    groups = groups or [1] * len(sources)
    goals = []
    for number, count in enumerate(groups):
        row = 0
        for _ in range(count):
            goals.append((number, row))
            row += sources[len(goals) - 1].shape[0]
    rows = [
        sum(source.shape[0] for source, (which, _) in zip(sources, goals) if which == number)
        for number in range(len(groups))
    ]

    def body(fetch, ins, outs, scratch):
        for start in range(0, weight.width, size):
            chunk, columns = fetch(), slice(start, start + size)
            for number, (source, (which, row)) in enumerate(zip(ins, goals)):
                if start == 0:
                    fetch.need(number)
                block = slice(row, row + source.shape[0])
                outs[which][block, columns] = plain_dot(source[...], chunk).astype(BF16)
            for which in range(len(groups)):
                fetch.send(which, columns)

    return weight_call(
        order, name, bits, [weight], columns_plan(0, weight.width, size), sources,
        [((count, weight.width), BF16) for count in rows], [], body,
        {i: source.shape[1] for i, source in enumerate(sources)},
        weight.width // size * len(groups),
    )


def mix_norm(order, name, bits, weight, mixed, residual, table, index, query_weight=None):
    rows, width = mixed.shape
    size = min(1024, width)

    def body(fetch, ins, outs, scratch):
        mixed_ref, residual_ref, table_ref = ins
        summed, out, out_low = outs[:3]
        fetch.need(0)
        for start in range(0, width, size):
            part = plain_dot(mixed_ref[...], fetch())
            if start == 0:
                fetch.need(1)
            columns = slice(start, start + size)
            summed[:, columns] = ALPHA * residual_ref[:, columns].astype(F32) + part
        fetch.send(0)
        gain, shift = table_ref[index : index + 1, :], table_ref[3 + index : 4 + index, :]

        def step(block):
            normed, _ = normed_parts(summed[block, :])
            values = normed * gain + shift
            out[block, :] = values
            out_low[block, :] = values.astype(BF16)

        row_blocks(rows, 128, step)
        fetch.send(1)
        fetch.send(2)
        if query_weight is not None:
            for start in range(0, width, size):
                part = plain_dot(out_low[...], fetch())
                outs[3][:, start : start + size] = part.astype(BF16)
            fetch.send(3)

    weights = [weight] + ([query_weight] if query_weight is not None else [])
    plan = [entry for i in range(len(weights)) for entry in columns_plan(i, width, size)]
    outs = [((rows, width), F32), ((rows, width), F32), ((rows, width), BF16)]
    if query_weight is not None:
        outs.append(((rows, width), BF16))
    return weight_call(
        order, name, bits, weights, plan, [mixed, residual, table], outs, [], body,
        {0: width, 1: width}, len(outs),
    )


def feed_in(order, bits, weight, source):
    rows, size = source.shape[0], 1024

    def body(fetch, ins, outs, scratch):
        held = scratch[0]
        fetch.need(0)
        for start in range(0, weight.width, size):
            held[...] = plain_dot(ins[0][...], fetch())

            def step(block):
                hidden = held[block, :]
                below = 0.5 + 0.5 * lax.erf(hidden * (0.5**0.5))
                density = jnp.exp(-0.5 * hidden * hidden) * (2.0 * jnp.pi) ** -0.5
                outs[0][block, start : start + size] = (hidden * below).astype(BF16)
                outs[1][block, start : start + size] = (below + hidden * density).astype(BF16)

            row_blocks(rows, 256, step)
            for which in range(2):
                fetch.send(which, slice(start, start + size))

    out = ((rows, weight.width), BF16)
    return weight_call(
        order, "feed_in", bits, [weight], columns_plan(0, weight.width, size), [source], [out, out],
        [((rows, size), F32)], body, {0: source.shape[1]}, 2 * weight.width // size,
    )


def feed_out(order, bits, weight, activated, residual, table, cotangent):
    rows, width = residual.shape
    size = 512 if width % 512 == 0 else width

    def body(fetch, ins, outs, scratch):
        act_ref, residual_ref, table_ref, up_ref = ins
        layer_out, grad, grad_low, stats = outs
        summed = scratch[0]
        fetch.need(0)
        for start in range(0, width, size):
            columns = slice(start, start + size)
            part = plain_dot(act_ref[...], fetch())
            if start == 0:
                fetch.need(1)
            summed[:, columns] = ALPHA * residual_ref[:, columns] + part
        fetch.need(3)
        gain, shift = table_ref[2:3, :], table_ref[5:6, :]
        stats[...] = jnp.zeros_like(stats)

        def step(block):
            normed, rate = normed_parts(summed[block, :])
            layer_out[block, :] = (normed * gain + shift).astype(BF16)
            upstream = up_ref[block, :].astype(F32)
            values = norm_gradient(normed, rate, gain, upstream)
            grad[block, :] = values
            grad_low[block, :] = values.astype(BF16)
            add_stats(stats, normed, upstream)

        row_blocks(rows, 128, step)

    outs = [((rows, width), BF16), ((rows, width), F32), ((rows, width), BF16), ((16, width), F32)]
    return weight_call(
        order, "feed_out", bits, [weight], columns_plan(0, width, size),
        [activated, residual, table, cotangent], outs, [((rows, width), F32)], body,
        {0: activated.shape[1], 1: width, 3: width},
    )


def feed_back(order, bits, weight, cotangent, slope):
    rows, features = slope.shape
    size = 1024 if features % 1024 == 0 else features
    steps = features // size

    def body(fetch, ins, outs, scratch):
        fetch.need(0)
        for number in range(steps):
            part = back_dot(ins[0][...], fetch())
            fetch.need(1, number)
            columns = slice(number * size, (number + 1) * size)
            outs[0][:, columns] = (part * ins[1][:, columns].astype(F32)).astype(BF16)
            fetch.send(0, columns)

    blocks = weight.blocks // steps
    return weight_call(
        order, "feed_back", bits, [weight], [(0, "rows", i * blocks, blocks) for i in range(steps)],
        [cotangent, slope], [((rows, features), BF16)], [], body,
        {0: cotangent.shape[1], 1: size}, steps,
    )[0]


def norm_back(order, name, bits, weight, cotangent, carried, summed, table, index, mix_weight):
    rows, width = summed.shape
    size = min(1024, weight.width)

    def body(fetch, ins, outs, scratch):
        up_ref, carried_ref, summed_ref, table_ref = ins
        grad, grad_low, grad_mixed, stats = outs
        total = scratch[0]
        for number, start in enumerate(range(0, weight.width, size)):
            fetch.need(0, number)
            part = back_dot(up_ref[:, start : start + size], fetch())
            if start == 0:
                fetch.need(1)
            total[...] = part + (ALPHA * carried_ref[...] if start == 0 else total[...])
        fetch.need(2)
        gain = table_ref[index : index + 1, :]
        stats[...] = jnp.zeros_like(stats)

        def step(block):
            normed, rate = normed_parts(summed_ref[block, :])
            upstream = total[block, :]
            values = norm_gradient(normed, rate, gain, upstream)
            grad[block, :] = values
            grad_low[block, :] = values.astype(BF16)
            add_stats(stats, normed, upstream)

        row_blocks(rows, 128, step)
        for which in (0, 1, 3):
            fetch.send(which)
        grad_mixed[...] = back_dot(grad_low[...], fetch()).astype(BF16)
        fetch.send(2)

    outs = [((rows, width), F32), ((rows, width), BF16), ((rows, width), BF16), ((16, width), F32)]
    return weight_call(
        order, name, bits, [weight, mix_weight],
        columns_plan(0, weight.width, size) + columns_plan(1, width, size),
        [cotangent, carried, summed, table], outs, [((rows, width), F32)], body,
        {0: size, 1: width, 2: width}, len(outs),
    )


def input_back(order, name, bits, weight, cotangents, carried, spans):
    rows, features = cotangents[0].shape[0], weight.features
    step = 512 if rows % 512 == 0 else rows // 2
    count = len(cotangents)
    streams = {which: size for which, _, _, size in spans}
    if carried is not None:
        streams[count] = carried.shape[1]

    def body(fetch, ins, outs, scratch):
        for number, (which, first, _, size) in enumerate(spans):
            chunk = fetch()
            fetch.need(which, first // size)
            if number == 0 and carried is not None:
                fetch.need(count)
            for row in range(0, rows, step):
                block = slice(row, row + step)
                part = back_dot(ins[which][block, first : first + size], chunk)
                if number == 0 and carried is not None:
                    part += ALPHA * ins[count][block, :]
                elif number > 0:
                    part += scratch[0][block, :]
                if number == len(spans) - 1:
                    outs[0][block, :] = part.astype(BF16)
                else:
                    scratch[0][block, :] = part

    return weight_call(
        order, name, bits, [weight], [(0, "columns", start, size) for _, _, start, size in spans],
        [*cotangents] + ([carried] if carried is not None else []),
        [((rows, features), BF16)], [((rows, features), F32)], body, streams,
    )[0]


def turn_rows(order, bits, sources, outer):
    features = sources[0].shape[1]
    total_rows = sum(source.shape[0] for source in sources)
    shard_rows = features // (8 * outer)

    def kernel(bits_ref, *refs):
        targets, filled = refs[len(sources) :], 0
        for ref in refs[: len(sources)]:
            stop = filled + ref.shape[0]
            for block in range(features // LANES):
                turned_block = ref[:, block * LANES : (block + 1) * LANES].T
                for part in range(LANES // shard_rows):
                    device = block * (LANES // shard_rows) + part
                    mem, core, near = device & 1, (device >> 1) & 1, (device >> 2) & 1
                    place = (mem ^ bits_ref[2]) * 2 + (near ^ bits_ref[0])
                    place = place * outer + (device >> 3)
                    rows = pl.ds(pl.multiple_of(place * shard_rows, shard_rows), shard_rows)
                    values = turned_block[part * shard_rows : (part + 1) * shard_rows]
                    side = core ^ bits_ref[1]

                    @pl.when(side == 0)
                    def _():
                        targets[0][rows, filled:stop] = values

                    @pl.when(side == 1)
                    def _():
                        targets[1][rows, filled:stop] = values

            filled = stop

    return order.launch(
        kernel,
        "turn_rows",
        [bits, *sources],
        [pl.BlockSpec(memory_space=pltpu.VMEM)] * len(sources),
        [pl.BlockSpec(memory_space=pltpu.VMEM)] * 2,
        [jax.ShapeDtypeStruct((features // 2, total_rows), BF16)] * 2,
        [],
        None,
        {},
    )


def weight_grad(
    order, bits, turned, cotangents, outer, cut, extra=None, held=None, place=None
):
    half_features = turned[0][0].shape[0]
    each, width = cotangents[0].shape
    n_turned = len(turned)
    n_grads = len(cotangents)
    total_rows = n_grads // 2 * each
    shard_rows = half_features // (4 * outer)
    parts = [width] + ([cut, width - cut] if place is None else [place[1], place[2]])
    chunk = 1024 if all(part % 1024 == 0 for part in parts) else 512
    added = 0 if extra is None else LANES
    n_held = 2 if held is not None else 0
    if place is None:
        halves = [(0, 0, cut // chunk, cut), (1, 0, (width - cut) // chunk, width - cut)]
    else:
        halves = [(place[0], place[1] // chunk, width // chunk, place[2])]
    steps = [count for _, _, count, _ in halves]
    first_steps = [sum(steps[:i]) for i in range(len(steps))]

    def kernel(bits_ref, *refs):
        n_in = n_turned + n_grads
        targets = refs[n_in + n_held + (len(halves) if added else 0) :]
        step = pl.program_id(0)
        features = jnp.concatenate([ref[...] for ref in refs[:n_turned]], axis=1)
        grads = jnp.concatenate([ref[...] for ref in refs[n_turned:n_in]], axis=0)
        product = plain_dot(features, grads)
        blocks = product.astype(BF16).reshape(2, 2, outer, shard_rows, chunk)
        for number, (half, _, count, _) in enumerate(halves):

            @pl.when((step >= first_steps[number]) & (step < first_steps[number] + count))
            def _():
                for side in range(2):
                    target = targets[2 * number + side]
                    picked = blocks[1 - side] if half == 0 else blocks[:, 1 - side]
                    target[..., :chunk] = picked
                    if added:
                        beside = refs[n_in + number]
                        picked = beside[1 - side] if half == 0 else beside[:, 1 - side]
                        target[..., chunk:] = picked

    def out_spec(number):
        _, first, count, _ = halves[number]
        at = lambda i, _: (0, 0, 0, first + jnp.clip(i - first_steps[number], 0, count - 1))
        return pl.BlockSpec((2, outer, shard_rows, chunk + added), at)

    def turned_spec(start, size):
        return pl.BlockSpec((half_features, size), lambda i, _: (0, start // size))

    whole = (2, 2, outer, shard_rows, LANES)
    specs = [turned_spec(start, size) for _, start, size in turned]
    specs += [pl.BlockSpec((each, chunk), lambda i, _: (0, i))] * n_grads
    specs += [pl.BlockSpec(memory_space=pltpu.HBM)] * n_held
    specs += [whole_spec(whole)] * (len(halves) if added else 0)
    return order.launch(
        kernel,
        "weight_grad",
        [bits, *(part for part, _, _ in turned), *cotangents, *(held or ()), *(extra or ())],
        specs,
        [out_spec(number) for number in range(len(halves)) for _ in range(2)],
        [
            jax.ShapeDtypeStruct((2, outer, shard_rows, columns + added), BF16)
            for _, _, _, columns in halves
            for _ in range(2)
        ],
        [],
        (sum(steps),),
        {1 + n_turned + n_grads: 0, 2 + n_turned + n_grads: 1} if n_held else {},
    )


def relative_rows(bits, values, outer):
    rows = values.shape[0] // (8 * outer)
    blocks = values.reshape(outer, 2, 2, 2, rows, -1)
    for axis, bit in ((1, bits[0]), (2, bits[1]), (3, bits[2])):
        blocks = jnp.where(bit == 1, jnp.flip(blocks, axis), blocks)
    blocks = blocks.transpose(2, 3, 1, 0, 4, 5)
    return blocks[0], blocks[1]


def add_blocks(order, bits, sums, shapes, apart=False):
    if apart:
        shapes = [shapes[0][1:]] * shapes[0][0]
    arrays = []
    for group, _, _ in sums:
        arrays += [a for a, _ in group if not any(a is b for b in arrays)]
    blocks = [group[0][0].shape[-3:] for group, _, _ in sums]
    find = lambda array: next(i for i, known in enumerate(arrays) if known is array)
    chunks = [(number, place) for place in range(blocks[0][0]) for number in range(len(sums))]

    def kernel(bits_ref, *refs):
        sources, refs = refs[: len(arrays)], refs[len(arrays) :]
        targets, refs = refs[: len(shapes)], refs[len(shapes) :]
        held, summed, (load_sems, store_sems) = refs[: len(sums)], refs[len(sums) : -2], refs[-2:]
        loads, stores = [], []
        for index, (number, place) in enumerate(chunks):
            loads.append([])
            block = place ^ bits_ref[3] if apart else place
            for term, (array, at) in enumerate(sums[number][0]):
                load = pltpu.make_async_copy(
                    sources[find(array)].at[(*at, block)],
                    held[number].at[term, place],
                    load_sems.at[index, term],
                )
                load.start()
                loads[-1].append(load)
        for index, (number, place) in enumerate(chunks):
            group, which, column = sums[number]
            for load in loads[index]:
                load.wait()
            values = [held[number][term, place].astype(F32) for term in range(len(group))]
            summed[number][place] = sum(values[1:], values[0]).astype(BF16)
            columns = pl.ds(column, blocks[number][2])
            goal = targets[place].at[:, columns] if apart else targets[which].at[place, :, columns]
            store = pltpu.make_async_copy(summed[number].at[place], goal, store_sems.at[index])
            store.start()
            stores.append(store)
        for store in stores:
            store.wait()

    most = max(len(group) for group, _, _ in sums)
    return order.launch(
        kernel,
        "add_blocks",
        [bits, *arrays],
        [pl.BlockSpec(memory_space=pltpu.HBM)] * len(arrays),
        [pl.BlockSpec(memory_space=pltpu.HBM)] * len(shapes),
        [jax.ShapeDtypeStruct(shape, BF16) for shape in shapes],
        [pltpu.VMEM((len(group), *block), BF16) for (group, _, _), block in zip(sums, blocks)]
        + [pltpu.VMEM(block, BF16) for block in blocks]
        + [
            pltpu.SemaphoreType.DMA((len(chunks), most)),
            pltpu.SemaphoreType.DMA((len(chunks),)),
        ],
        None,
        {},
    )


class Spread:
    def __init__(self, parts, kinds):
        self.kinds, self.kept = kinds, parts[1::2]
        self.once = [FIRST_BACK[kind](part) for part, kind in zip(parts[0::2], kinds)]

    def second(self):
        return [[(kept, (1,)), (once, (1,))] for kept, once in zip(self.kept, self.once)]

    def send(self, sent):
        self.twice = [SECOND_BACK[kind](part) for part, kind in zip(sent, self.kinds)]

    def third(self):
        return [
            [(kept, (0,)), (once, (0,)), (twice, ())]
            for kept, once, twice in zip(self.kept, self.once, self.twice)
        ]


def block_shape(group):
    return group[0][0].shape[-3:]


def spread_steps(order, bits, seconds, thirds, together=False):
    sums, shapes = [], []
    for wave in seconds:
        for group in wave.second():
            sums.append((group, len(shapes), 0))
            shapes.append(block_shape(group))
    joined = len(shapes)
    for number, wave in enumerate(thirds):
        if number == 0 or not together:
            shapes.append((*block_shape(wave.third()[0])[:2], 0))
        for group in wave.third():
            outer, rows, columns = shapes[-1]
            sums.append((group, len(shapes) - 1, columns))
            shapes[-1] = (outer, rows, columns + block_shape(group)[2])
    filled = add_blocks(order, bits, sums, shapes, together)
    start = 0
    for wave in seconds:
        wave.send(filled[start : start + len(wave.kinds)])
        start += len(wave.kinds)
    return filled[joined:]


def outer_sum(joined):
    joined = joined.reshape(-1, joined.shape[-1])
    return lax.psum_scatter(
        joined, "dp", axis_index_groups=outer_groups(), scatter_dimension=0, tiled=True
    )


def last_shards(order, bits, parts, summed, spans):
    rows, columns = parts[0].shape
    widths = [sum(size for _, _, size in span) for span in spans]

    def kernel(bits_ref, *refs):
        refs, summed_ref, targets = refs[: len(parts)], refs[len(parts)], refs[len(parts) + 1 :]
        total = refs[0][...].astype(F32)
        for ref in refs[1:]:
            total += ref[...].astype(F32)
        for target, span in zip(targets, spans):
            at = 0
            for wave, start, size in span:
                if wave == 0:
                    values = total[:, start : start + size]
                else:
                    values = summed_ref[:, start : start + size].astype(F32)
                target[:, at : at + size] = values
                at += size

    return order.launch(
        kernel,
        "last_shards",
        [bits, *parts, summed],
        [pl.BlockSpec(memory_space=pltpu.VMEM)] * (len(parts) + 1),
        [pl.BlockSpec(memory_space=pltpu.VMEM)] * len(spans),
        [jax.ShapeDtypeStruct((rows, width), F32) for width in widths],
        [],
        None,
        {},
    )


FIRST_BACK = (swap_mem, swap_next)
SECOND_BACK = (swap_next, swap_mem)


def per_device(
    target_in,
    memory_in,
    bucket_ids,
    target_lengths,
    memory_mask,
    self_qkv,
    self_out,
    cross_q,
    cross_kv,
    cross_out,
    ffn_in,
    ffn_out,
    norm_gains,
    norm_biases,
    grad_out,
):
    both = ("dp", "mem")
    row_count, model_width = target_in.shape
    shard_rows = self_qkv.shape[0]
    outer = lax.axis_size("dp") // 4
    staged = shard_rows % 16 == 0 and shard_rows <= LANES and model_width % LANES == 0
    bits = place_bits()
    order = Order()
    own_index, pieces = lax.axis_index("mem"), lax.axis_size("mem")
    slot_count, mem_piece = memory_in.shape[3], memory_in.shape[4]

    norm_shard = jnp.concatenate((norm_gains, norm_biases), axis=1)
    norm_columns = norm_shard.shape[1]
    norm_shard = jnp.pad(norm_shard, ((0, 0), (0, LANES - norm_columns)))

    groups = [
        (self_qkv,),
        (cross_q, cross_out, norm_shard, cross_kv, self_out),
        (ffn_in,),
        (ffn_out,),
    ]
    if staged:
        shards = list(cast_shards(order, bits, groups))
    else:
        shards = [jnp.concatenate([part.astype(BF16) for part in group], axis=1) for group in groups]

    def gather(index, windows, direct=False):
        shard = shards[index]
        widths = [part.shape[1] for part in groups[index]]
        starts = [sum(widths[:i]) for i in range(len(widths))]
        if staged:
            wave = Wave(shard, windows, direct)
            return [Weight(wave, at, size) for at, size in zip(starts, widths)]
        full = lax.all_gather(shard, both, axis=0, tiled=True)
        rows = full.shape[0] // 16
        return [
            Weight(None, 0, size, full[:, at : at + size].reshape(8, 2, rows, size))
            for at, size in zip(starts, widths)
        ]

    def whole_sum(gradient):
        return lax.psum_scatter(gradient, both, scatter_dimension=0, tiled=True).astype(F32)

    class Turned:
        def __init__(self, *sources):
            self.sources = sources
            own, other = turn_rows(order, bits, sources, outer) if staged else (None, None)
            self.both = (own, swap_core(other)) if staged else ()

        def due(self):
            order.before(*self.both[1:])

    class Grad:
        def __init__(self, *places):
            self.sources = [source for _, *sources in places for source in sources]
            self.turned = []
            for side in range(2 if staged else 0):
                for turned, *sources in places:
                    start = 0
                    for other in turned.sources:
                        if other is sources[0]:
                            break
                        start += other.shape[0]
                    stop = start + sum(source.shape[0] for source in sources)
                    size = math.gcd(start, stop)
                    for at in range(start, stop, size):
                        self.turned.append((turned.both[side], at, size))

        def take(self, *cotangents):
            self.cotangents = cotangents
            if staged:
                self.cotangents += tuple(swap_core(part) for part in cotangents)

        def make(self, cut=None, **options):
            if staged:
                return weight_grad(
                    order, bits, self.turned, self.cotangents, outer, cut, **options
                )
            rows = [jnp.concatenate(part, axis=0) for part in (self.sources, self.cotangents)]
            return lead_dot(*rows).astype(BF16)

    def at_mem(values, index):
        return lax.dynamic_index_in_dim(values, index, 0, False)

    mem_rows = memory_in[0, :, 0]
    mem_live = memory_mask[0, :, 0]
    near_live = at_mem(mem_live, own_index)
    far_live = swap_mem(at_mem(mem_live, 1 - own_index))
    piece_shape = (mem_piece, model_width)
    if staged:
        moves = Moves(order, bits)
        source, near = moves.source(mem_rows), moves.target((slot_count, *piece_shape))
        sent = [moves.target(piece_shape) for _ in range(slot_count)]
        for slot in range(slot_count):
            at_far = lambda bits, slot=slot: (1 - bits[2], slot)
            at_near = lambda bits, slot=slot: (bits[2], slot)
            moves.move(source, at_far, piece_shape, (sent[slot], (slice(None),)))
            moves.move(source, at_near, piece_shape, (near, (slot,)))
        given = {}
        moves.then.append(lambda filled: given.update(near=filled[near], sent=[filled[t] for t in sent]))
        moves.run()
        near_rows, sent_rows = given["near"], given["sent"]
    else:
        near_rows = at_mem(mem_rows, own_index)
        sent_rows = [at_mem(mem_rows[:, slot], 1 - own_index) for slot in range(slot_count)]

    qkv_half = 3 * model_width // 2
    (w_qkv,) = gather(0, [(0, qkv_half, 0), (qkv_half, qkv_half, 1)], True)
    far_parts = [swap_mem(sent_rows[0])]
    if staged:
        order.before(far_parts[0], far_live)
        moves = Moves(order, bits)
        w_qkv.wave.first(moves)
        places = [moves.passed(shard) for shard in shards[1:]]
        moves.then.append(lambda filled: shards.__setitem__(slice(1, None), [filled[i] for i in places]))
        moves.run()
    lead = 2 * model_width + LANES
    w_cq, w_co, w_norm, w_ckv, w_so = gather(
        1, [(0, lead, 0), (lead, 5 * model_width + LANES - lead, 1)]
    )
    (w_in,) = gather(2, [(0, ffn_in.shape[1], 0)])
    (w_out,) = gather(3, [(0, model_width, 1)])

    bucket = pick_entry(bucket_ids[0], own_index)
    lengths = target_lengths[0, 0]
    self_meta = jnp.stack([jnp.right_shift(jnp.int32(row_count), bucket), lengths[0], lengths[1]])
    cross_meta = bucket[None]
    live = jnp.concatenate((near_live, far_live), axis=1)
    key_bias = jnp.where(live == 1, 0.0, NEG_LARGE).astype(F32)
    key_columns = jnp.broadcast_to(key_bias[:, :, None], (*key_bias.shape, LANES))
    near_flat = near_rows.reshape(-1, model_width)
    slotted = (slot_count, mem_piece, 2 * model_width)

    def steps(*wanted):
        if staged:
            moves = Moves(order, bits)
            for weight, name in wanted:
                getattr(weight.wave, name)(moves)
            moves.run()

    steps((w_qkv, "second"))
    order.part()
    first_turned = Turned(target_in, near_flat)
    steps((w_ckv, "first"))
    order.part()
    steps((w_qkv, "third"))
    first_turned.due()
    order.part()
    steps((w_ckv, "second"))
    (united,) = project(order, "self_project", bits, w_qkv, [target_in], 1024)
    far_parts += [swap_mem(part) for part in gate(order, bits, sent_rows[1:])]
    steps((w_in, "first"))
    order.before(key_columns)
    self_mixed, self_log = self_forward(order, self_meta, united)
    order.part()
    steps((w_ckv, "third"))
    order.before(*far_parts[1:])
    order.part()
    steps((w_out, "first"))
    table = norm_table(order, bits, w_norm)
    near_kv, far_kv = project(
        order, "cross_project", bits, w_ckv, [near_flat, *far_parts], 1024, [1, len(far_parts)]
    )
    near_kv, far_kv = near_kv.reshape(slotted), far_kv.reshape(slotted)
    order.part()
    steps((w_in, "second"), (w_out, "second"))
    sum_one, first_out, first_low, cross_query = mix_norm(
        order, "self_mix", bits, w_so, self_mixed, target_in, table, 0, w_cq
    )
    cross_mixed, cross_log = cross_forward(
        order, cross_meta, cross_query, near_kv, far_kv, key_bias[:, None, :]
    )
    sum_two, second_out, second_low = mix_norm(
        order, "cross_mix", bits, w_co, cross_mixed, first_out, table, 1
    )
    later = Turned(self_mixed, first_low, cross_mixed, second_low, *far_parts)
    order.part()
    steps((w_in, "third"), (w_out, "third"))
    activated, slope = feed_in(order, bits, w_in, second_low)
    later.due()
    hidden = Turned(activated)
    layer_out, grad_three, grad_ffn, stats_three = feed_out(
        order, bits, w_out, activated, second_out, table, grad_out
    )
    qkv_grad = Grad((first_turned, target_in))
    so_grad = Grad((later, self_mixed))
    ckv_grad = Grad((first_turned, near_flat), (later, *far_parts))
    cq_grad = Grad((later, first_low))
    co_grad = Grad((later, cross_mixed))
    in_grad = Grad((later, second_low))
    out_grad = Grad((hidden, activated))

    shards = {}

    def spread(name, parts, kinds):
        if staged:
            return Spread(parts, kinds)
        shards[name] = whole_sum(parts)
        return None

    def advance(seconds=(), thirds=()):
        if staged:
            waves = [wave for _, wave in thirds]
            joined = spread_steps(order, bits, seconds, waves)
            for (name, _), part in zip(thirds, joined):
                shards[name] = outer_sum(part)

    out_grad.take(grad_ffn)
    out_wave = spread("out", out_grad.make(model_width // 2), (0, 1))
    grad_hidden = feed_back(order, bits, w_out, grad_ffn, slope)
    in_grad.take(grad_hidden)
    grad_two, grad_cross_out, grad_cross_mixed, stats_two = norm_back(
        order, "cross_back", bits, w_in, grad_hidden, grad_three, sum_two, table, 1, w_co
    )
    co_grad.take(grad_cross_out)
    order.part()
    advance([out_wave])
    in_wave = spread("in", in_grad.make(2 * model_width), (0, 1))
    pair_width = 2 * model_width
    near_parts = co_grad.make(place=(0, 0, pair_width))
    grad_query_low, grad_near_kv, grad_far_kv = cross_backward(
        order,
        cross_meta,
        cross_query,
        near_kv,
        far_kv,
        key_columns,
        cross_mixed,
        grad_cross_mixed,
        cross_log,
    )
    cq_grad.take(grad_query_low)
    ckv_grad.take(grad_near_kv, grad_far_kv)
    order.part()
    advance([in_wave], [("out", out_wave)])

    def memory_back(cotangent):
        spans = [(0, start, start, model_width) for start in (0, model_width)]
        return input_back(order, "memory_back", bits, w_ckv, [cotangent], None, spans)

    grad_one, grad_self_out, grad_self_mixed, stats_one = norm_back(
        order, "self_back", bits, w_cq, grad_query_low, grad_two, sum_one, table, 0, w_so
    )
    so_grad.take(grad_self_out)
    stats = [jnp.sum(s.reshape(2, 8, model_width), axis=1) for s in (stats_one, stats_two, stats_three)]
    norm_grads = [
        jnp.pad(jnp.stack([s[i] for s in stats], axis=1), ((0, 0), (0, LANES - len(stats))))
        for i in range(2)
    ]
    norm_grads = jnp.concatenate(norm_grads, axis=1).astype(BF16)
    if staged:
        own, other = relative_rows(bits, norm_grads, outer)
        own = (own.astype(F32) + swap_core(other).astype(F32)).astype(BF16)
        norm_grads = (own[..., :LANES], own[..., LANES:])
        far_parts = ckv_grad.make(place=(1, 0, pair_width))
        near_parts = cq_grad.make(place=(0, model_width, pair_width), held=near_parts)
        mid_parts = [*near_parts, *far_parts]
    else:
        mid_parts = jnp.concatenate([near_parts, cq_grad.make(), ckv_grad.make()], axis=1)
    mid_wave = spread("mid", mid_parts, (0, 1))
    order.part()
    advance([], [("in", in_wave)])
    grad_united = self_backward(
        order,
        self_meta,
        united,
        self_mixed,
        grad_self_mixed,
        self_log,
    )
    qkv_grad.take(grad_united)
    half_width = model_width // 2
    if staged:
        so_wave = spread("so", so_grad.make(half_width, extra=norm_grads), (0, 1))
    else:
        part = so_grad.make()
        columns = [part[:, :half_width], norm_grads[:, :LANES], part[:, half_width:], norm_grads[:, LANES:]]
        so_wave = spread("so", jnp.concatenate(columns, axis=1), (0, 1))
    order.part()
    advance([mid_wave])
    qkv_wave = spread("qkv", qkv_grad.make(qkv_half), (0, 1))
    if staged:
        order.before(shards["out"], shards["in"])
        order.part()
        advance([], [("mid", mid_wave)])
    split = half_width + LANES
    grad_far = memory_back(grad_far_kv)
    if staged:
        order.part()
        advance([qkv_wave, so_wave])
        (grad_far,) = gate(order, bits, [grad_far])
    grad_far = swap_mem(grad_far)
    if staged:
        order.before(shards["mid"])
        order.part()
        blocks = spread_steps(order, bits, [], [so_wave, qkv_wave], True)
        blocks = [blocks[0]] + [swap_outer(blocks[far], far) for far in range(1, outer)]
    grad_near = memory_back(grad_near_kv)
    target_grad = input_back(
        order,
        "target_back",
        bits,
        w_qkv,
        [grad_united],
        grad_one,
        [(0, start, start, model_width) for start in range(0, w_qkv.width, model_width)],
    )
    so_spans = [(0, 0, half_width), (0, split, half_width)]
    norm_spans = [[(0, half_width, 3)], [(0, split + half_width, 3)]]
    mid_spans = [[(1, i * model_width, model_width)] for i in range(2)]
    mid_spans.append([(1, 2 * model_width, 2 * model_width)])
    spans = [[(0, 2 * split, 2 * qkv_half)], so_spans, *norm_spans, *mid_spans]
    if staged:
        last = last_shards(order, bits, blocks, shards["mid"], spans)
        moves = Moves(order, bits)
        target = moves.target((2, *near_flat.shape))
        for number, part in enumerate((grad_near, grad_far)):
            place = lambda bits, number=number: (bits[2] ^ number,)
            moves.move(moves.source(part), (slice(None),), near_flat.shape, (target, place))
        moves.then.append(lambda filled: shards.update(memory=filled[target]))
        moves.run()
        grad_pair = shards["memory"]
    else:
        grad_pair = jnp.stack((grad_near, grad_far))
        grad_pair = jnp.where(own_index == 0, grad_pair, grad_pair[::-1])
        sources = (jnp.concatenate((shards["so"], shards["qkv"]), axis=1), shards["mid"])
        last = [
            jnp.concatenate([sources[w][:, at : at + size] for w, at, size in span], axis=1)
            for span in spans
        ]
    qkv_shard, so_shard, gains, biases, co_shard, cq_shard, ckv_shard = last

    return (
        layer_out,
        target_grad,
        grad_pair.reshape(1, pieces, 1, *near_rows.shape),
        qkv_shard,
        so_shard,
        cq_shard,
        ckv_shard,
        co_shard,
        shards["in"].astype(F32),
        shards["out"].astype(F32),
        gains,
        biases,
    )


def solution(mesh):
    rows = P(("dp", "mem"), None)
    memory = P("dp", None, "mem", None, None, None)
    return jax.shard_map(
        per_device,
        mesh=mesh,
        in_specs=(
            rows,
            memory,
            P("dp", None),
            P("dp", "mem", None),
            P("dp", None, "mem", None, None),
        )
        + (rows,) * 10,
        out_specs=(rows, rows, memory) + (rows,) * 9,
        check_vma=False,
    )
```

```python
import math

import jax
import jax.numpy as jnp
from jax import lax
from jax.experimental import pallas as pl
from jax.experimental.pallas import tpu as pltpu
from jax.sharding import PartitionSpec as P

HD = 64
LANES = 128
PAIRS = 2
WIDE = PAIRS * LANES
ALPHA = 300.0**0.25
NEG_LARGE = -1e30
EPSILON = 1e-05
VMEM_BYTES = 64 * 1024 * 1024 - 128 * 1024
SCALE = HD**-0.5
BF16 = jnp.bfloat16
F32 = jnp.float32


def plain_dot(first_op, second_op):
    return jnp.dot(first_op, second_op, preferred_element_type=F32)


def lead_dot(first_op, second_op):
    return lax.dot_general(
        first_op, second_op, (((0,), (0,)), ((), ())), preferred_element_type=F32
    )


def back_dot(first_op, second_op):
    return lax.dot_general(
        first_op, second_op, (((1,), (1,)), ((), ())), preferred_element_type=F32
    )


def pick_entry(values, wanted):
    return jnp.sum(jnp.where(jnp.arange(values.shape[0]) == wanted, values, 0))


def kernel_params():
    return pltpu.CompilerParams(vmem_limit_bytes=VMEM_BYTES)


class Order:
    def __init__(self):
        self.last, self.due, self.parted = None, [], False

    def before(self, *arrays):
        self.due += arrays

    def part(self):
        self.parted = True

    def launch(self, kernel, name, operands, in_specs, out_specs, out_shape, scratch, grid, aliases):
        ties = self.due + ([self.last] if self.last is not None else [])
        ties = [tie for tie in ties if not any(tie is operand for operand in operands)]
        self.due = []
        count, n_ties = len(operands), len(ties)

        def tied(*refs):
            kernel(*refs[:count], *refs[count + n_ties :])

        specs = list(in_specs) + [pl.BlockSpec(memory_space=pltpu.HBM)] * n_ties
        cost = pl.CostEstimate(
            flops=10**12 if self.parted else 10**6, bytes_accessed=1, transcendentals=0
        )
        self.parted = False
        if grid is None:
            run = pl.pallas_call(
                tied,
                in_specs=[pl.BlockSpec(memory_space=pltpu.SMEM)] + specs,
                out_specs=out_specs,
                out_shape=out_shape,
                scratch_shapes=scratch,
                input_output_aliases=aliases,
                compiler_params=kernel_params(),
                cost_estimate=cost,
                name=name,
            )
        else:
            run = pl.pallas_call(
                tied,
                grid_spec=pltpu.PrefetchScalarGridSpec(
                    num_scalar_prefetch=1,
                    grid=grid,
                    in_specs=specs,
                    out_specs=out_specs,
                    scratch_shapes=scratch,
                ),
                out_shape=out_shape,
                input_output_aliases=aliases,
                compiler_params=kernel_params(),
                cost_estimate=cost,
                name=name,
            )
        results = run(*operands, *ties)
        self.last = results[0]
        return results


def whole_spec(shape):
    return pl.BlockSpec(shape, lambda *_: (0,) * len(shape))


def head_lanes(rows, head):
    lane = lax.broadcasted_iota(jnp.int32, (rows, LANES), 1)
    return (lane < HD) if head == 0 else (lane >= HD)


def visible(query_ids, key_ids, slot_len, first_len, second_len):
    query_slot = (query_ids >= slot_len).astype(jnp.int32)
    key_slot = (key_ids >= slot_len).astype(jnp.int32)
    place = key_ids - key_slot * slot_len
    limit = jnp.where(key_slot == 0, first_len, second_len)
    return (query_slot == key_slot) & (key_ids <= query_ids) & (place < limit)


def pair_forward(query, keys, values, bias):
    rows, key_rows = query.shape[0], keys.shape[0]
    mixed, peaks = [], []
    for head in range(2):
        mine = head_lanes(rows, head)
        masked = jnp.where(mine, query * BF16(SCALE), BF16(0))
        scores = back_dot(masked, keys) + bias
        peak = jnp.max(scores, axis=1, keepdims=True)
        raised = jnp.exp(scores - peak).astype(BF16)
        widened = jnp.where(head_lanes(key_rows, head), values, BF16(1))
        mixed.append(plain_dot(raised, widened))
        peaks.append(peak)
    first = head_lanes(rows, 0)
    totals = pltpu.roll(jnp.where(first, mixed[1], mixed[0]), HD, 1)
    joined = jnp.where(first, mixed[0], mixed[1])
    log_totals = jnp.where(first, peaks[0], peaks[1]) + jnp.log(totals)
    return joined / totals, log_totals


def pair_backward(query, keys, values, upstream, bias, log_rows, delta_rows):
    rows, key_rows = query.shape[0], keys.shape[0]
    grad_q, grad_k, grad_v = None, None, None
    for head in range(2):
        mine = head_lanes(rows, head)
        masked = jnp.where(mine, query * BF16(SCALE), BF16(0))
        masked_up = jnp.where(mine, upstream, BF16(0))
        scores = back_dot(keys, masked) + bias
        probs = jnp.exp(scores - log_rows[head])
        grad_probs = back_dot(values, masked_up)
        grad_scores = (probs * (grad_probs - delta_rows[head])).astype(BF16)
        part_v = plain_dot(probs.astype(BF16), masked_up)
        part_k = plain_dot(grad_scores, masked)
        masked_keys = jnp.where(head_lanes(key_rows, head), keys, BF16(0))
        part_q = lead_dot(grad_scores, masked_keys)
        grad_q = part_q if grad_q is None else grad_q + part_q
        grad_k = part_k if grad_k is None else grad_k + part_k
        grad_v = part_v if grad_v is None else grad_v + part_v
    return grad_q * SCALE, grad_k, grad_v


def stat_rows(log_block, mixed, upstream):
    log_turned = log_block.T
    products = (mixed.astype(F32) * upstream.astype(F32)).T
    log_rows = [log_turned[:1], log_turned[HD : HD + 1]]
    delta_rows = [jnp.sum(products[h * HD : (h + 1) * HD], axis=0, keepdims=True) for h in range(2)]
    return log_rows, delta_rows


def pair_lanes(pair):
    return slice(pair * LANES, (pair + 1) * LANES)


def self_forward_kernel(meta, q_ref, k_ref, v_ref, mixed_ref, log_ref, bias):
    rows = q_ref.shape[0]

    @pl.when(pl.program_id(0) == 0)
    def _():
        query_ids = lax.broadcasted_iota(jnp.int32, (rows, rows), 0)
        key_ids = lax.broadcasted_iota(jnp.int32, (rows, rows), 1)
        seen = visible(query_ids, key_ids, meta[0], meta[1], meta[2])
        bias[...] = jnp.where(seen, 0.0, NEG_LARGE)

    half = rows // 2
    for pair in range(PAIRS):
        lanes = pair_lanes(pair)
        for start, stop in ((0, half), (half, rows)):
            mixed, log_totals = pair_forward(
                q_ref[start:stop, lanes],
                k_ref[:stop, lanes],
                v_ref[:stop, lanes],
                bias[start:stop, :stop],
            )
            mixed_ref[start:stop, lanes] = mixed.astype(BF16)
            log_ref[start:stop, lanes] = log_totals


def self_forward(order, meta, united):
    rows, width = united.shape[0], united.shape[1] // 3
    steps = width // WIDE
    spec = lambda third: pl.BlockSpec((rows, WIDE), lambda i, _: (0, third * steps + i))
    return order.launch(
        self_forward_kernel,
        "self_forward",
        [meta, united, united, united],
        [spec(0), spec(1), spec(2)],
        [spec(0), spec(0)],
        [jax.ShapeDtypeStruct((rows, width), kind) for kind in (BF16, F32)],
        [pltpu.VMEM((rows, rows), F32)],
        (steps,),
        {},
    )


def self_backward_kernel(
    meta, q_ref, k_ref, v_ref, mixed_ref, up_ref, log_ref, grad_ref, bias
):
    rows = q_ref.shape[0]
    width = grad_ref.shape[1] // 3
    step = pl.program_id(0)

    @pl.when(step == 0)
    def _():
        key_ids = lax.broadcasted_iota(jnp.int32, (rows, rows), 0)
        query_ids = lax.broadcasted_iota(jnp.int32, (rows, rows), 1)
        seen = visible(query_ids, key_ids, meta[0], meta[1], meta[2])
        bias[...] = jnp.where(seen, 0.0, NEG_LARGE)

    half = rows // 2
    for pair in range(PAIRS):
        lanes = pair_lanes(pair)
        log_rows, delta_rows = stat_rows(log_ref[:, lanes], mixed_ref[:, lanes], up_ref[:, lanes])
        parts = []
        for start, stop in ((0, half), (half, rows)):
            parts.append(
                pair_backward(
                    q_ref[start:stop, lanes],
                    k_ref[:stop, lanes],
                    v_ref[:stop, lanes],
                    up_ref[start:stop, lanes],
                    bias[:stop, start:stop],
                    [row[:, start:stop] for row in log_rows],
                    [row[:, start:stop] for row in delta_rows],
                )
            )
        low, high = parts
        at = step * WIDE + pair * LANES
        columns = lambda third: pl.ds(pl.multiple_of(third * width + at, LANES), LANES)
        grad_ref[:half, columns(0)] = low[0].astype(BF16)
        grad_ref[half:, columns(0)] = high[0].astype(BF16)
        for third in (1, 2):
            grad_ref[:half, columns(third)] = (low[third] + high[third][:half]).astype(BF16)
            grad_ref[half:, columns(third)] = high[third][half:].astype(BF16)


def self_backward(order, meta, united, mixed, upstream, log_totals):
    rows, width = mixed.shape
    steps = width // WIDE
    spec = lambda third: pl.BlockSpec((rows, WIDE), lambda i, _: (0, third * steps + i))
    shape = (rows, 3 * width)
    return order.launch(
        self_backward_kernel,
        "self_backward",
        [meta, united, united, united, mixed, upstream, log_totals],
        [spec(0), spec(1), spec(2), spec(0), spec(0), spec(0)],
        [whole_spec(shape)],
        [jax.ShapeDtypeStruct(shape, BF16)],
        [pltpu.VMEM((rows, rows), F32)],
        (steps,),
        {},
    )[0]


def join_keys(near_ref, far_ref, joined):
    slots, piece = near_ref.shape[0], near_ref.shape[1]
    for slot in range(slots):
        joined[slot, :piece, :] = near_ref[slot]
        joined[slot, piece:, :] = far_ref[slot]


def cross_forward_kernel(
    meta, q_ref, kn_ref, vn_ref, kf_ref, vf_ref, bias_ref, mixed_ref, log_ref, keys, values
):
    half = q_ref.shape[0] // 2
    join_keys(kn_ref, kf_ref, keys)
    join_keys(vn_ref, vf_ref, values)
    for pair in range(PAIRS):
        lanes = pair_lanes(pair)
        for part in range(2):
            slot = part * meta[0]
            rows = slice(part * half, (part + 1) * half)
            mixed, log_totals = pair_forward(
                q_ref[rows, lanes], keys[slot, :, lanes], values[slot, :, lanes], bias_ref[slot]
            )
            mixed_ref[rows, lanes] = mixed.astype(BF16)
            log_ref[rows, lanes] = log_totals


def cross_specs(rows, slots, piece, steps):
    row_spec = pl.BlockSpec((rows, WIDE), lambda i, _: (0, i))
    half = lambda at: pl.BlockSpec((slots, piece, WIDE), lambda i, _: (0, 0, at * steps + i))
    return row_spec, [row_spec, half(0), half(1), half(0), half(1)]


def cross_forward(order, meta, query, near, far, bias):
    rows, width = query.shape
    slots, piece = near.shape[0], near.shape[1]
    steps = width // WIDE
    row_spec, specs = cross_specs(rows, slots, piece, steps)
    return order.launch(
        cross_forward_kernel,
        "cross_forward",
        [meta, query, near, near, far, far, bias],
        specs + [whole_spec(bias.shape)],
        [row_spec, row_spec],
        [jax.ShapeDtypeStruct((rows, width), kind) for kind in (BF16, F32)],
        [pltpu.VMEM((slots, 2 * piece, WIDE), BF16)] * 2,
        (steps,),
        {},
    )


def cross_backward_kernel(
    meta,
    q_ref,
    kn_ref,
    vn_ref,
    kf_ref,
    vf_ref,
    bias_ref,
    mixed_ref,
    up_ref,
    log_ref,
    grad_q_ref,
    grad_near_ref,
    grad_far_ref,
    keys,
    values,
):
    half = q_ref.shape[0] // 2
    slots, piece = kn_ref.shape[0], kn_ref.shape[1]
    width = grad_near_ref.shape[1] // 2
    join_keys(kn_ref, kf_ref, keys)
    join_keys(vn_ref, vf_ref, values)
    split = meta[0].astype(F32)
    for pair in range(PAIRS):
        lanes = pair_lanes(pair)
        log_rows, delta_rows = stat_rows(log_ref[:, lanes], mixed_ref[:, lanes], up_ref[:, lanes])
        parts = []
        for part in range(2):
            slot = part * meta[0]
            rows = slice(part * half, (part + 1) * half)
            bias_column = bias_ref[slot]
            grads = pair_backward(
                q_ref[rows, lanes],
                keys[slot, :, lanes],
                values[slot, :, lanes],
                up_ref[rows, lanes],
                jnp.concatenate([bias_column] * (half // LANES), axis=1),
                [row[:, rows] for row in log_rows],
                [row[:, rows] for row in delta_rows],
            )
            grad_q_ref[rows, lanes] = grads[0].astype(BF16)
            parts.append(grads)
        start = pl.program_id(0) * WIDE + pair * LANES
        for which in range(2):
            early, late = parts[0][1 + which], parts[1][1 + which]
            columns = pl.ds(pl.multiple_of(which * width + start, LANES), LANES)
            by_slot = (early + late * (1.0 - split), late * split)
            for slot in range(slots):
                for source, target in enumerate((grad_near_ref, grad_far_ref)):
                    target[slot * piece : (slot + 1) * piece, columns] = by_slot[slot][
                        source * piece : (source + 1) * piece
                    ].astype(BF16)


def cross_backward(order, meta, query, near, far, bias, mixed, upstream, log_totals):
    rows, width = query.shape
    slots, piece = near.shape[0], near.shape[1]
    steps = width // WIDE
    memory = (slots * piece, 2 * width)
    row_spec, specs = cross_specs(rows, slots, piece, steps)
    return order.launch(
        cross_backward_kernel,
        "cross_backward",
        [meta, query, near, near, far, far, bias, mixed, upstream, log_totals],
        specs + [whole_spec(bias.shape)] + [row_spec] * 3,
        [row_spec, whole_spec(memory), whole_spec(memory)],
        [jax.ShapeDtypeStruct(shape, BF16) for shape in ((rows, width), memory, memory)],
        [pltpu.VMEM((slots, 2 * piece, WIDE), BF16)] * 2,
        (steps,),
        {},
    )


def swap_core(values):
    size = lax.axis_size("dp")
    return lax.ppermute(values, "dp", [(i, i ^ 1) for i in range(size)])


def swap_next(values):
    size = lax.axis_size("dp")
    return lax.ppermute(values, "dp", [(i, i ^ 2) for i in range(size)])


def swap_mem(values):
    return lax.ppermute(values, "mem", [(0, 1), (1, 0)])


def swap_outer(values, far):
    size = lax.axis_size("dp")
    return lax.ppermute(values, "dp", [(i, i ^ (4 * far)) for i in range(size)])


def outer_groups():
    size = lax.axis_size("dp")
    return [list(range(base, size, 4)) for base in range(4)]


def place_bits():
    dp, mem = lax.axis_index("dp"), lax.axis_index("mem")
    return jnp.stack([(dp >> 1) & 1, dp & 1, mem, dp >> 2]).astype(jnp.int32)


def outer_gather(shard):
    stacked = lax.all_gather(shard, "dp", axis_index_groups=outer_groups(), axis=0, tiled=True)
    return stacked.reshape(-1, *shard.shape)


def gate(order, bits, arrays):
    def kernel(*refs):
        pass

    return order.launch(
        kernel,
        "gate",
        [bits, *arrays],
        [pl.BlockSpec(memory_space=pltpu.HBM)] * len(arrays),
        [pl.BlockSpec(memory_space=pltpu.HBM)] * len(arrays),
        [jax.ShapeDtypeStruct(array.shape, array.dtype) for array in arrays],
        [],
        None,
        {1 + i: i for i in range(len(arrays))},
    )


class Moves:
    def __init__(self, order, bits):
        self.order, self.bits = order, bits
        self.sources, self.shapes, self.moves, self.aliases, self.then = [], [], [], {}, []

    def source(self, array):
        self.sources.append(array)
        return len(self.sources) - 1

    def target(self, shape, held=None):
        self.shapes.append(shape)
        if held is not None:
            self.aliases[1 + self.source(held)] = len(self.shapes) - 1
        return len(self.shapes) - 1

    def passed(self, array):
        return self.target(array.shape, array)

    def move(self, source, source_at, shape, *goals):
        self.moves.append((source, source_at, shape, goals))

    def run(self):
        moves, n_in, n_out = self.moves, len(self.sources), len(self.shapes)
        most = max([len(move[3]) for move in moves] + [0])

        def kernel(bits_ref, *refs):
            bits = [bits_ref[i] for i in range(4)]
            taken, given = refs[:n_in], refs[n_in : n_in + n_out]
            slots, sems = refs[n_in + n_out : -1], refs[-1]
            loads, stores = [], []
            for number, (source, source_at, _, goals) in enumerate(moves):
                slot = slots[number]
                loads.append(
                    pltpu.make_async_copy(
                        taken[source].at[source_at(bits) if callable(source_at) else source_at],
                        slot,
                        sems.at[0, number],
                    )
                )
                stores.append(
                    [
                        pltpu.make_async_copy(
                            slot, given[which].at[at(bits) if callable(at) else at], sems.at[1 + i, number]
                        )
                        for i, (which, at) in enumerate(goals)
                    ]
                )
            for load in loads:
                load.start()
            for load, group in zip(loads, stores):
                load.wait()
                for store in group:
                    store.start()
            for group in stores:
                for store in group:
                    store.wait()

        filled = self.order.launch(
            kernel,
            "move_blocks",
            [self.bits, *self.sources],
            [pl.BlockSpec(memory_space=pltpu.HBM)] * n_in,
            [pl.BlockSpec(memory_space=pltpu.HBM)] * n_out,
            [jax.ShapeDtypeStruct(shape, BF16) for shape in self.shapes],
            [pltpu.VMEM(shape, BF16) for _, _, shape, _ in moves]
            + [pltpu.SemaphoreType.DMA((1 + most, max(1, len(moves))))],
            None,
            self.aliases,
        )
        for step in self.then:
            step(filled)


def cast_shards(order, bits, groups):
    shapes = [(group[0].shape[0], sum(part.shape[1] for part in group)) for group in groups]
    parts = [part for group in groups for part in group]

    def kernel(bits_ref, *refs):
        number = 0
        for group, target in zip(groups, refs[len(parts) :]):
            start = 0
            for part in group:
                stop = start + part.shape[1]
                target[:, start:stop] = refs[number][...].astype(BF16)
                start, number = stop, number + 1

    return order.launch(
        kernel,
        "cast_shards",
        [bits, *parts],
        [pl.BlockSpec(memory_space=pltpu.VMEM)] * len(parts),
        [pl.BlockSpec(memory_space=pltpu.VMEM)] * len(shapes),
        [jax.ShapeDtypeStruct(shape, BF16) for shape in shapes],
        [],
        None,
        {},
    )


FIRST = (swap_next, swap_mem)
SECOND = (swap_mem, swap_next)


class Wave:
    def __init__(self, shard, windows, direct):
        self.windows = [(pl.ds(start, size), kind) for start, size, kind in windows]
        self.rows, self.columns = shard.shape
        self.outer = lax.axis_size("dp") // 4
        if direct:
            self.shards = [shard] + [swap_outer(shard, far) for far in range(1, self.outer)]
        else:
            self.stacked = outer_gather(shard)
        self.direct = direct

    def first(self, moves):
        def send(parts):
            self.pairs = [(part, FIRST[kind](part)) for part, (_, kind) in zip(parts, self.windows)]

        if not self.direct and len(self.windows) == 1:
            target = moves.passed(self.stacked)
            moves.then.append(lambda filled: send([filled[target]]))
            return
        targets = [moves.target((self.outer, self.rows, w.size)) for w, _ in self.windows]
        sources = [moves.source(part) for part in (self.shards if self.direct else [self.stacked])]
        for block in range(self.outer):
            for target, (window, _) in zip(targets, self.windows):
                shape = (self.rows, window.size)
                if self.direct:
                    goal = (target, lambda bits, block=block: (bits[3] ^ block,))
                    moves.move(sources[block], (slice(None), window), shape, goal)
                else:
                    goal = (target, (block,))
                    moves.move(sources[0], (block, slice(None), window), shape, goal)
        moves.then.append(lambda filled: send([filled[target] for target in targets]))

    def place(self, kind, second, first, block, window):
        near, mem = (first, second) if kind == 0 else (second, first)
        return lambda bits: (block, bits[0] ^ near, bits[2] ^ mem, slice(None), window)

    def second(self, moves):
        sources = [[moves.source(part) for part in pair] for pair in self.pairs]
        targets = [moves.target((2, *pair[0].shape)) for pair in self.pairs]
        own = moves.target((self.outer, 2, 2, self.rows, self.columns))
        for block in range(self.outer):
            for number, (window, kind) in enumerate(self.windows):
                for side in range(2):
                    goal = (targets[number], (side, block))
                    again = (own, self.place(kind, 0, side, block, window))
                    shape = (self.rows, window.size)
                    moves.move(sources[number][side], (block,), shape, goal, again)

        def send(filled):
            self.own = filled[own]
            self.far = [
                SECOND[kind](filled[target]) for target, (_, kind) in zip(targets, self.windows)
            ]

        moves.then.append(send)

    def third(self, moves):
        own = moves.target(self.own.shape, self.own)
        for number, (window, kind) in enumerate(self.windows):
            source = moves.source(self.far[number])
            for block in range(self.outer):
                for side in range(2):
                    goal = (own, self.place(kind, 1, side, block, window))
                    moves.move(source, (side, block), (self.rows, window.size), goal)

        def send(filled):
            shape = (2 * self.outer, 2 * self.rows, self.columns)
            self.own = filled[own].reshape(shape)
            self.other = swap_core(self.own)

        moves.then.append(send)


class Weight:
    def __init__(self, wave, start, width, whole=None):
        self.wave, self.start, self.width, self.whole = wave, start, width, whole
        if whole is not None:
            self.blocks, self.rows = whole.shape[0], whole.shape[2]
        else:
            self.blocks, self.rows = 2 * wave.outer, 2 * wave.rows
        self.features = self.blocks * 2 * self.rows

    def pieces(self):
        return [self.whole] if self.whole is not None else [self.wave.own, self.wave.other]

    def copies(self, kind, start, size, bits, find, target):
        if kind == "columns":
            blocks, columns = slice(None), pl.ds(self.start + start, size)
        else:
            blocks, columns = pl.ds(start, size), pl.ds(self.start, self.width)
        if self.whole is not None:
            return [(find(self.whole).at[blocks, :, :, columns], target)]
        return [
            (find(array).at[blocks, :, columns], target.at[:, bits[1] ^ core])
            for core, array in enumerate((self.wave.own, self.wave.other))
        ]


def weight_call(order, name, bits, weights, plan, inputs, outs, scratch, body, streams=None, sends=0):
    streams = streams or {}
    arrays = []
    for weight in weights:
        arrays += [a for a in weight.pieces() if not any(a is b for b in arrays)]
    kind, size = plan[0][1], plan[0][3]
    lead = weights[plan[0][0]]
    if kind == "columns":
        chunk = (lead.blocks, 2, lead.rows, size)
    else:
        chunk = (size, 2, lead.rows, lead.width)
    n_in, n_arrays, n_out = len(inputs), len(arrays), len(outs)
    streamed = sorted(streams)
    most = max([1] + [inputs[i].shape[1] // streams[i] for i in streamed])

    def kernel(bits_ref, *refs):
        ins, refs = list(refs[:n_in]), refs[n_in:]
        pieces, refs = refs[:n_arrays], refs[n_arrays:]
        out_refs, refs = refs[:n_out], refs[n_out:]
        held, sems, stream_sems, send_sems = refs[-4:]
        staged = refs[: n_out if sends else 0]
        stream_refs = refs[len(staged) : len(staged) + len(streamed)]
        rest = refs[len(staged) + len(streamed) : -4]
        bits_now = [bits_ref[i] for i in range(3)]

        def find(array):
            return next(ref for ref, known in zip(pieces, arrays) if known is array)

        def issue(number):
            which, kind, start, size = plan[number]
            slot = number % 2
            for source, target in weights[which].copies(
                kind, start, size, bits_now, find, held.at[slot]
            ):
                pltpu.make_async_copy(source, target, sems.at[slot]).start()

        taken, coming, sent = [0], {}, []

        def fetch():
            number = taken[0]
            taken[0] += 1
            if number + 1 < len(plan):
                issue(number + 1)
            slot = number % 2
            pltpu.make_async_copy(held.at[slot], held.at[slot], sems.at[slot]).wait()
            return held[slot].reshape(-1, chunk[-1])

        def need(which, part=0):
            coming.pop((which, part)).wait()

        def send(which, columns=None):
            columns = slice(None) if columns is None else columns
            copy = pltpu.make_async_copy(
                staged[which].at[:, columns], out_refs[which].at[:, columns], send_sems.at[len(sent)]
            )
            copy.start()
            sent.append(copy)

        fetch.need, fetch.send, fetch.bits = need, send, bits_now
        issue(0)
        for number, which in enumerate(streamed):
            count = streams[which]
            for part in range(inputs[which].shape[1] // count):
                columns = pl.ds(part * count, count)
                copy = pltpu.make_async_copy(
                    ins[which].at[:, columns],
                    stream_refs[number].at[:, columns],
                    stream_sems.at[number, part],
                )
                copy.start()
                coming[which, part] = copy
            ins[which] = stream_refs[number]
        body(fetch, ins, staged if sends else out_refs, rest)
        for copy in sent + list(coming.values()):
            copy.wait()

    hbm, vmem = pl.BlockSpec(memory_space=pltpu.HBM), pl.BlockSpec(memory_space=pltpu.VMEM)
    return order.launch(
        kernel,
        name,
        [bits, *inputs, *arrays],
        [hbm if i in streams else vmem for i in range(n_in)] + [hbm] * n_arrays,
        [hbm if sends else vmem] * n_out,
        [jax.ShapeDtypeStruct(shape, kind) for shape, kind in outs],
        ([pltpu.VMEM(shape, kind) for shape, kind in outs] if sends else [])
        + [pltpu.VMEM(inputs[i].shape, inputs[i].dtype) for i in streamed]
        + [pltpu.VMEM(shape, kind) for shape, kind in scratch]
        + [
            pltpu.VMEM((2, *chunk), BF16),
            pltpu.SemaphoreType.DMA((2,)),
            pltpu.SemaphoreType.DMA((max(1, len(streamed)), most)),
            pltpu.SemaphoreType.DMA((max(1, sends),)),
        ],
        None,
        {},
    )


def columns_plan(which, width, size):
    return [(which, "columns", start, size) for start in range(0, width, size)]


def row_blocks(rows, size, step):
    def run(i, carry):
        step(pl.ds(pl.multiple_of(i * size, size), size))
        return carry

    lax.fori_loop(0, rows // size, run, 0)


def normed_parts(values):
    centred = values - jnp.mean(values, axis=-1, keepdims=True)
    spread = jnp.mean(centred * centred, axis=-1, keepdims=True)
    rate = lax.rsqrt(spread + EPSILON)
    return centred * rate, rate


def norm_gradient(normed, rate, gain, cotangent):
    inner = cotangent * gain
    mean_inner = jnp.mean(inner, axis=-1, keepdims=True)
    mean_both = jnp.mean(inner * normed, axis=-1, keepdims=True)
    return rate * (inner - mean_inner - normed * mean_both)


def add_stats(stats, normed, cotangent):
    fold = lambda values: jnp.sum(values.reshape(-1, 8, values.shape[-1]), axis=0)
    stats[:8, :] += fold(cotangent * normed)
    stats[8:, :] += fold(cotangent)


def norm_table(order, bits, weight):
    features = weight.features

    def body(fetch, ins, outs, scratch):
        outs[0][...] = fetch().astype(F32).T[:8]

    return weight_call(
        order, "norm_table", bits, [weight], [(0, "columns", 0, LANES)], [],
        [((8, features), F32)], [], body,
    )[0]


def project(order, name, bits, weight, sources, size, groups=None):
    groups = groups or [1] * len(sources)
    goals = []
    for number, count in enumerate(groups):
        row = 0
        for _ in range(count):
            goals.append((number, row))
            row += sources[len(goals) - 1].shape[0]
    rows = [
        sum(source.shape[0] for source, (which, _) in zip(sources, goals) if which == number)
        for number in range(len(groups))
    ]

    def body(fetch, ins, outs, scratch):
        for start in range(0, weight.width, size):
            chunk, columns = fetch(), slice(start, start + size)
            for number, (source, (which, row)) in enumerate(zip(ins, goals)):
                if start == 0:
                    fetch.need(number)
                block = slice(row, row + source.shape[0])
                outs[which][block, columns] = plain_dot(source[...], chunk).astype(BF16)
            for which in range(len(groups)):
                fetch.send(which, columns)

    return weight_call(
        order, name, bits, [weight], columns_plan(0, weight.width, size), sources,
        [((count, weight.width), BF16) for count in rows], [], body,
        {i: source.shape[1] for i, source in enumerate(sources)},
        weight.width // size * len(groups),
    )


def mix_norm(order, name, bits, weight, mixed, residual, table, index, query_weight=None):
    rows, width = mixed.shape
    size = min(1024, width)

    def body(fetch, ins, outs, scratch):
        mixed_ref, residual_ref, table_ref = ins
        summed, out, out_low = outs[:3]
        fetch.need(0)
        for start in range(0, width, size):
            part = plain_dot(mixed_ref[...], fetch())
            if start == 0:
                fetch.need(1)
            columns = slice(start, start + size)
            summed[:, columns] = ALPHA * residual_ref[:, columns].astype(F32) + part
        fetch.send(0)
        gain, shift = table_ref[index : index + 1, :], table_ref[3 + index : 4 + index, :]

        def step(block):
            normed, _ = normed_parts(summed[block, :])
            values = normed * gain + shift
            out[block, :] = values
            out_low[block, :] = values.astype(BF16)

        row_blocks(rows, 128, step)
        fetch.send(1)
        fetch.send(2)
        if query_weight is not None:
            for start in range(0, width, size):
                part = plain_dot(out_low[...], fetch())
                outs[3][:, start : start + size] = part.astype(BF16)
            fetch.send(3)

    weights = [weight] + ([query_weight] if query_weight is not None else [])
    plan = [entry for i in range(len(weights)) for entry in columns_plan(i, width, size)]
    outs = [((rows, width), F32), ((rows, width), F32), ((rows, width), BF16)]
    if query_weight is not None:
        outs.append(((rows, width), BF16))
    return weight_call(
        order, name, bits, weights, plan, [mixed, residual, table], outs, [], body,
        {0: width, 1: width}, len(outs),
    )


def feed_in(order, bits, weight, source, outer):
    rows, size = source.shape[0], 1024
    shard_rows = weight.width // (8 * outer) if outer else 0
    turning = shard_rows > 0 and LANES % shard_rows == 0

    def turn_chunk(bits_now, values, start, targets):
        for block in range(size // LANES):
            turned = values[:, block * LANES : (block + 1) * LANES].T
            for part in range(LANES // shard_rows):
                device = (start + block * LANES) // shard_rows + part
                mem, core, near = device & 1, (device >> 1) & 1, (device >> 2) & 1
                place = (mem ^ bits_now[2]) * 2 + (near ^ bits_now[0])
                place = (place * outer + (device >> 3)) * shard_rows
                block_rows = pl.ds(pl.multiple_of(place, shard_rows), shard_rows)
                piece = turned[part * shard_rows : (part + 1) * shard_rows]
                for side, target in enumerate(targets):

                    @pl.when((core ^ bits_now[1]) == side)
                    def _():
                        target[block_rows, :] = piece

    def body(fetch, ins, outs, scratch):
        held = scratch[0]
        fetch.need(0)
        for start in range(0, weight.width, size):
            held[...] = plain_dot(ins[0][...], fetch())

            def step(block):
                hidden = held[block, :]
                below = 0.5 + 0.5 * lax.erf(hidden * (0.5**0.5))
                density = jnp.exp(-0.5 * hidden * hidden) * (2.0 * jnp.pi) ** -0.5
                outs[0][block, start : start + size] = (hidden * below).astype(BF16)
                outs[1][block, start : start + size] = (below + hidden * density).astype(BF16)

            row_blocks(rows, 256, step)
            columns = slice(start, start + size)
            for which in range(2):
                fetch.send(which, columns)
            if turning:
                turn_chunk(fetch.bits, outs[0][:, columns], start, outs[2:])
        for which in range(2, len(outs)):
            fetch.send(which)

    out, turned = ((rows, weight.width), BF16), ((weight.width // 2, rows), BF16)
    outs = [out, out] + ([turned, turned] if turning else [])
    return weight_call(
        order, "feed_in", bits, [weight], columns_plan(0, weight.width, size), [source], outs,
        [((rows, size), F32)], body, {0: source.shape[1]}, 2 * weight.width // size + len(outs) - 2,
    )


def feed_out(order, bits, weight, activated, residual, table, cotangent):
    rows, width = residual.shape
    size = 512 if width % 512 == 0 else width

    def body(fetch, ins, outs, scratch):
        act_ref, residual_ref, table_ref, up_ref = ins
        layer_out, grad, grad_low, stats = outs
        summed = scratch[0]
        fetch.need(0)
        for start in range(0, width, size):
            columns = slice(start, start + size)
            part = plain_dot(act_ref[...], fetch())
            if start == 0:
                fetch.need(1)
            summed[:, columns] = ALPHA * residual_ref[:, columns] + part
        fetch.need(3)
        gain, shift = table_ref[2:3, :], table_ref[5:6, :]
        stats[...] = jnp.zeros_like(stats)

        def step(block):
            normed, rate = normed_parts(summed[block, :])
            layer_out[block, :] = (normed * gain + shift).astype(BF16)
            upstream = up_ref[block, :].astype(F32)
            values = norm_gradient(normed, rate, gain, upstream)
            grad[block, :] = values
            grad_low[block, :] = values.astype(BF16)
            add_stats(stats, normed, upstream)

        row_blocks(rows, 128, step)

    outs = [((rows, width), BF16), ((rows, width), F32), ((rows, width), BF16), ((16, width), F32)]
    return weight_call(
        order, "feed_out", bits, [weight], columns_plan(0, width, size),
        [activated, residual, table, cotangent], outs, [((rows, width), F32)], body,
        {0: activated.shape[1], 1: width, 3: width},
    )


def feed_back(order, bits, weight, cotangent, slope):
    rows, features = slope.shape
    size = 1024 if features % 1024 == 0 else features
    steps = features // size

    def body(fetch, ins, outs, scratch):
        fetch.need(0)
        for number in range(steps):
            part = back_dot(ins[0][...], fetch())
            fetch.need(1, number)
            columns = slice(number * size, (number + 1) * size)
            outs[0][:, columns] = (part * ins[1][:, columns].astype(F32)).astype(BF16)
            fetch.send(0, columns)

    blocks = weight.blocks // steps
    return weight_call(
        order, "feed_back", bits, [weight], [(0, "rows", i * blocks, blocks) for i in range(steps)],
        [cotangent, slope], [((rows, features), BF16)], [], body,
        {0: cotangent.shape[1], 1: size}, steps,
    )[0]


def norm_back(order, name, bits, weight, cotangent, carried, summed, table, index, mix_weight):
    rows, width = summed.shape
    size = min(1024, weight.width)

    def body(fetch, ins, outs, scratch):
        up_ref, carried_ref, summed_ref, table_ref = ins
        grad, grad_low, grad_mixed, stats = outs
        total = scratch[0]
        for number, start in enumerate(range(0, weight.width, size)):
            fetch.need(0, number)
            part = back_dot(up_ref[:, start : start + size], fetch())
            if start == 0:
                fetch.need(1)
            total[...] = part + (ALPHA * carried_ref[...] if start == 0 else total[...])
        fetch.need(2)
        gain = table_ref[index : index + 1, :]
        stats[...] = jnp.zeros_like(stats)

        def step(block):
            normed, rate = normed_parts(summed_ref[block, :])
            upstream = total[block, :]
            values = norm_gradient(normed, rate, gain, upstream)
            grad[block, :] = values
            grad_low[block, :] = values.astype(BF16)
            add_stats(stats, normed, upstream)

        row_blocks(rows, 128, step)
        for which in (0, 1, 3):
            fetch.send(which)
        grad_mixed[...] = back_dot(grad_low[...], fetch()).astype(BF16)
        fetch.send(2)

    outs = [((rows, width), F32), ((rows, width), BF16), ((rows, width), BF16), ((16, width), F32)]
    return weight_call(
        order, name, bits, [weight, mix_weight],
        columns_plan(0, weight.width, size) + columns_plan(1, width, size),
        [cotangent, carried, summed, table], outs, [((rows, width), F32)], body,
        {0: size, 1: width, 2: width}, len(outs),
    )


def input_back(order, name, bits, weight, cotangents, carried, spans):
    rows, features = cotangents[0].shape[0], weight.features
    step = 512 if rows % 512 == 0 else rows // 2
    count = len(cotangents)
    streams = {which: size for which, _, _, size in spans}
    if carried is not None:
        streams[count] = carried.shape[1]

    def body(fetch, ins, outs, scratch):
        for number, (which, first, _, size) in enumerate(spans):
            chunk = fetch()
            fetch.need(which, first // size)
            if number == 0 and carried is not None:
                fetch.need(count)
            for row in range(0, rows, step):
                block = slice(row, row + step)
                part = back_dot(ins[which][block, first : first + size], chunk)
                if number == 0 and carried is not None:
                    part += ALPHA * ins[count][block, :]
                elif number > 0:
                    part += scratch[0][block, :]
                if number == len(spans) - 1:
                    outs[0][block, :] = part.astype(BF16)
                else:
                    scratch[0][block, :] = part

    return weight_call(
        order, name, bits, [weight], [(0, "columns", start, size) for _, _, start, size in spans],
        [*cotangents] + ([carried] if carried is not None else []),
        [((rows, features), BF16)], [((rows, features), F32)], body, streams,
    )[0]


def turn_rows(order, bits, sources, outer):
    features = sources[0].shape[1]
    total_rows = sum(source.shape[0] for source in sources)
    shard_rows = features // (8 * outer)

    def kernel(bits_ref, *refs):
        targets, filled = refs[len(sources) :], 0
        for ref in refs[: len(sources)]:
            stop = filled + ref.shape[0]
            for block in range(features // LANES):
                turned_block = ref[:, block * LANES : (block + 1) * LANES].T
                for part in range(LANES // shard_rows):
                    device = block * (LANES // shard_rows) + part
                    mem, core, near = device & 1, (device >> 1) & 1, (device >> 2) & 1
                    place = (mem ^ bits_ref[2]) * 2 + (near ^ bits_ref[0])
                    place = place * outer + (device >> 3)
                    rows = pl.ds(pl.multiple_of(place * shard_rows, shard_rows), shard_rows)
                    values = turned_block[part * shard_rows : (part + 1) * shard_rows]
                    side = core ^ bits_ref[1]

                    @pl.when(side == 0)
                    def _():
                        targets[0][rows, filled:stop] = values

                    @pl.when(side == 1)
                    def _():
                        targets[1][rows, filled:stop] = values

            filled = stop

    return order.launch(
        kernel,
        "turn_rows",
        [bits, *sources],
        [pl.BlockSpec(memory_space=pltpu.VMEM)] * len(sources),
        [pl.BlockSpec(memory_space=pltpu.VMEM)] * 2,
        [jax.ShapeDtypeStruct((features // 2, total_rows), BF16)] * 2,
        [],
        None,
        {},
    )


def weight_grad(
    order, bits, turned, cotangents, outer, cut, extra=None, held=None, place=None
):
    half_features = turned[0][0].shape[0]
    each, width = cotangents[0].shape
    n_turned = len(turned)
    n_grads = len(cotangents)
    total_rows = n_grads // 2 * each
    shard_rows = half_features // (4 * outer)
    parts = [width] + ([cut, width - cut] if place is None else [place[1], place[2]])
    chunk = 1024 if all(part % 1024 == 0 for part in parts) else 512
    added = 0 if extra is None else LANES
    n_held = 2 if held is not None else 0
    if place is None:
        halves = [(0, 0, cut // chunk, cut), (1, 0, (width - cut) // chunk, width - cut)]
    else:
        halves = [(place[0], place[1] // chunk, width // chunk, place[2])]
    steps = [count for _, _, count, _ in halves]
    first_steps = [sum(steps[:i]) for i in range(len(steps))]

    def kernel(bits_ref, *refs):
        n_in = n_turned + n_grads
        targets = refs[n_in + n_held + (len(halves) if added else 0) :]
        step = pl.program_id(0)
        features = jnp.concatenate([ref[...] for ref in refs[:n_turned]], axis=1)
        grads = jnp.concatenate([ref[...] for ref in refs[n_turned:n_in]], axis=0)
        product = plain_dot(features, grads)
        blocks = product.astype(BF16).reshape(2, 2, outer, shard_rows, chunk)
        for number, (half, _, count, _) in enumerate(halves):

            @pl.when((step >= first_steps[number]) & (step < first_steps[number] + count))
            def _():
                for side in range(2):
                    target = targets[2 * number + side]
                    picked = blocks[1 - side] if half == 0 else blocks[:, 1 - side]
                    target[..., :chunk] = picked
                    if added:
                        beside = refs[n_in + number]
                        picked = beside[1 - side] if half == 0 else beside[:, 1 - side]
                        target[..., chunk:] = picked

    def out_spec(number):
        _, first, count, _ = halves[number]
        at = lambda i, _: (0, 0, 0, first + jnp.clip(i - first_steps[number], 0, count - 1))
        return pl.BlockSpec((2, outer, shard_rows, chunk + added), at)

    def turned_spec(start, size):
        return pl.BlockSpec((half_features, size), lambda i, _: (0, start // size))

    whole = (2, 2, outer, shard_rows, LANES)
    specs = [turned_spec(start, size) for _, start, size in turned]
    specs += [pl.BlockSpec((each, chunk), lambda i, _: (0, i))] * n_grads
    specs += [pl.BlockSpec(memory_space=pltpu.HBM)] * n_held
    specs += [whole_spec(whole)] * (len(halves) if added else 0)
    return order.launch(
        kernel,
        "weight_grad",
        [bits, *(part for part, _, _ in turned), *cotangents, *(held or ()), *(extra or ())],
        specs,
        [out_spec(number) for number in range(len(halves)) for _ in range(2)],
        [
            jax.ShapeDtypeStruct((2, outer, shard_rows, columns + added), BF16)
            for _, _, _, columns in halves
            for _ in range(2)
        ],
        [],
        (sum(steps),),
        {1 + n_turned + n_grads: 0, 2 + n_turned + n_grads: 1} if n_held else {},
    )


def relative_rows(bits, values, outer):
    rows = values.shape[0] // (8 * outer)
    blocks = values.reshape(outer, 2, 2, 2, rows, -1)
    for axis, bit in ((1, bits[0]), (2, bits[1]), (3, bits[2])):
        blocks = jnp.where(bit == 1, jnp.flip(blocks, axis), blocks)
    blocks = blocks.transpose(2, 3, 1, 0, 4, 5)
    return blocks[0], blocks[1]


def add_blocks(order, bits, sums, shapes, apart=False):
    if apart:
        shapes = [shapes[0][1:]] * shapes[0][0]
    arrays = []
    for group, _, _ in sums:
        arrays += [a for a, _ in group if not any(a is b for b in arrays)]
    blocks = [group[0][0].shape[-3:] for group, _, _ in sums]
    find = lambda array: next(i for i, known in enumerate(arrays) if known is array)
    chunks = [(number, place) for place in range(blocks[0][0]) for number in range(len(sums))]

    def kernel(bits_ref, *refs):
        sources, refs = refs[: len(arrays)], refs[len(arrays) :]
        targets, refs = refs[: len(shapes)], refs[len(shapes) :]
        held, summed, (load_sems, store_sems) = refs[: len(sums)], refs[len(sums) : -2], refs[-2:]
        loads, stores = [], []
        for index, (number, place) in enumerate(chunks):
            loads.append([])
            block = place ^ bits_ref[3] if apart else place
            for term, (array, at) in enumerate(sums[number][0]):
                load = pltpu.make_async_copy(
                    sources[find(array)].at[(*at, block)],
                    held[number].at[term, place],
                    load_sems.at[index, term],
                )
                load.start()
                loads[-1].append(load)
        for index, (number, place) in enumerate(chunks):
            group, which, column = sums[number]
            for load in loads[index]:
                load.wait()
            values = [held[number][term, place].astype(F32) for term in range(len(group))]
            summed[number][place] = sum(values[1:], values[0]).astype(BF16)
            columns = pl.ds(column, blocks[number][2])
            goal = targets[place].at[:, columns] if apart else targets[which].at[place, :, columns]
            store = pltpu.make_async_copy(summed[number].at[place], goal, store_sems.at[index])
            store.start()
            stores.append(store)
        for store in stores:
            store.wait()

    most = max(len(group) for group, _, _ in sums)
    return order.launch(
        kernel,
        "add_blocks",
        [bits, *arrays],
        [pl.BlockSpec(memory_space=pltpu.HBM)] * len(arrays),
        [pl.BlockSpec(memory_space=pltpu.HBM)] * len(shapes),
        [jax.ShapeDtypeStruct(shape, BF16) for shape in shapes],
        [pltpu.VMEM((len(group), *block), BF16) for (group, _, _), block in zip(sums, blocks)]
        + [pltpu.VMEM(block, BF16) for block in blocks]
        + [
            pltpu.SemaphoreType.DMA((len(chunks), most)),
            pltpu.SemaphoreType.DMA((len(chunks),)),
        ],
        None,
        {},
    )


class Spread:
    def __init__(self, parts, kinds):
        self.kinds, self.kept = kinds, parts[1::2]
        self.once = [FIRST_BACK[kind](part) for part, kind in zip(parts[0::2], kinds)]

    def second(self):
        return [[(kept, (1,)), (once, (1,))] for kept, once in zip(self.kept, self.once)]

    def send(self, sent):
        self.twice = [SECOND_BACK[kind](part) for part, kind in zip(sent, self.kinds)]

    def third(self):
        return [
            [(kept, (0,)), (once, (0,)), (twice, ())]
            for kept, once, twice in zip(self.kept, self.once, self.twice)
        ]


def block_shape(group):
    return group[0][0].shape[-3:]


def spread_steps(order, bits, seconds, thirds, together=False):
    sums, shapes = [], []
    for wave in seconds:
        for group in wave.second():
            sums.append((group, len(shapes), 0))
            shapes.append(block_shape(group))
    joined = len(shapes)
    for number, wave in enumerate(thirds):
        if number == 0 or not together:
            shapes.append((*block_shape(wave.third()[0])[:2], 0))
        for group in wave.third():
            outer, rows, columns = shapes[-1]
            sums.append((group, len(shapes) - 1, columns))
            shapes[-1] = (outer, rows, columns + block_shape(group)[2])
    filled = add_blocks(order, bits, sums, shapes, together)
    start = 0
    for wave in seconds:
        wave.send(filled[start : start + len(wave.kinds)])
        start += len(wave.kinds)
    return filled[joined:]


def outer_sum(joined):
    joined = joined.reshape(-1, joined.shape[-1])
    return lax.psum_scatter(
        joined, "dp", axis_index_groups=outer_groups(), scatter_dimension=0, tiled=True
    )


def last_shards(order, bits, parts, summed, spans):
    rows, columns = parts[0].shape
    widths = [sum(size for _, _, size in span) for span in spans]

    def kernel(bits_ref, *refs):
        refs, summed_ref, targets = refs[: len(parts)], refs[len(parts)], refs[len(parts) + 1 :]
        total = refs[0][...].astype(F32)
        for ref in refs[1:]:
            total += ref[...].astype(F32)
        for target, span in zip(targets, spans):
            at = 0
            for wave, start, size in span:
                if wave == 0:
                    values = total[:, start : start + size]
                else:
                    values = summed_ref[:, start : start + size].astype(F32)
                target[:, at : at + size] = values
                at += size

    return order.launch(
        kernel,
        "last_shards",
        [bits, *parts, summed],
        [pl.BlockSpec(memory_space=pltpu.VMEM)] * (len(parts) + 1),
        [pl.BlockSpec(memory_space=pltpu.VMEM)] * len(spans),
        [jax.ShapeDtypeStruct((rows, width), F32) for width in widths],
        [],
        None,
        {},
    )


FIRST_BACK = (swap_mem, swap_next)
SECOND_BACK = (swap_next, swap_mem)


def per_device(
    target_in,
    memory_in,
    bucket_ids,
    target_lengths,
    memory_mask,
    self_qkv,
    self_out,
    cross_q,
    cross_kv,
    cross_out,
    ffn_in,
    ffn_out,
    norm_gains,
    norm_biases,
    grad_out,
):
    both = ("dp", "mem")
    row_count, model_width = target_in.shape
    shard_rows = self_qkv.shape[0]
    outer = lax.axis_size("dp") // 4
    staged = shard_rows % 16 == 0 and shard_rows <= LANES and model_width % LANES == 0
    bits = place_bits()
    order = Order()
    own_index, pieces = lax.axis_index("mem"), lax.axis_size("mem")
    slot_count, mem_piece = memory_in.shape[3], memory_in.shape[4]

    norm_shard = jnp.concatenate((norm_gains, norm_biases), axis=1)
    norm_columns = norm_shard.shape[1]
    norm_shard = jnp.pad(norm_shard, ((0, 0), (0, LANES - norm_columns)))

    groups = [
        (self_qkv,),
        (cross_q, cross_out, norm_shard, cross_kv, self_out),
        (ffn_in,),
        (ffn_out,),
    ]
    if staged:
        shards = list(cast_shards(order, bits, groups))
    else:
        shards = [jnp.concatenate([part.astype(BF16) for part in group], axis=1) for group in groups]

    def gather(index, windows, direct=False):
        shard = shards[index]
        widths = [part.shape[1] for part in groups[index]]
        starts = [sum(widths[:i]) for i in range(len(widths))]
        if staged:
            wave = Wave(shard, windows, direct)
            return [Weight(wave, at, size) for at, size in zip(starts, widths)]
        full = lax.all_gather(shard, both, axis=0, tiled=True)
        rows = full.shape[0] // 16
        return [
            Weight(None, 0, size, full[:, at : at + size].reshape(8, 2, rows, size))
            for at, size in zip(starts, widths)
        ]

    def whole_sum(gradient):
        return lax.psum_scatter(gradient, both, scatter_dimension=0, tiled=True).astype(F32)

    class Turned:
        def __init__(self, *sources, turned=()):
            self.sources = sources
            own, other = turned or (turn_rows(order, bits, sources, outer) if staged else (None, None))
            self.both = (own, swap_core(other)) if staged else ()

        def due(self):
            order.before(*self.both[1:])

    class Grad:
        def __init__(self, *places):
            self.sources = [source for _, *sources in places for source in sources]
            self.turned = []
            for side in range(2 if staged else 0):
                for turned, *sources in places:
                    start = 0
                    for other in turned.sources:
                        if other is sources[0]:
                            break
                        start += other.shape[0]
                    stop = start + sum(source.shape[0] for source in sources)
                    size = math.gcd(start, stop)
                    for at in range(start, stop, size):
                        self.turned.append((turned.both[side], at, size))

        def take(self, *cotangents):
            self.cotangents = cotangents
            if staged:
                self.cotangents += tuple(swap_core(part) for part in cotangents)

        def make(self, cut=None, **options):
            if staged:
                return weight_grad(
                    order, bits, self.turned, self.cotangents, outer, cut, **options
                )
            rows = [jnp.concatenate(part, axis=0) for part in (self.sources, self.cotangents)]
            return lead_dot(*rows).astype(BF16)

    def at_mem(values, index):
        return lax.dynamic_index_in_dim(values, index, 0, False)

    mem_rows = memory_in[0, :, 0]
    mem_live = memory_mask[0, :, 0]
    near_live = at_mem(mem_live, own_index)
    far_live = swap_mem(at_mem(mem_live, 1 - own_index))
    piece_shape = (mem_piece, model_width)
    if staged:
        moves = Moves(order, bits)
        source, near = moves.source(mem_rows), moves.target((slot_count, *piece_shape))
        sent = [moves.target(piece_shape) for _ in range(slot_count)]
        for slot in range(slot_count):
            at_far = lambda bits, slot=slot: (1 - bits[2], slot)
            at_near = lambda bits, slot=slot: (bits[2], slot)
            moves.move(source, at_far, piece_shape, (sent[slot], (slice(None),)))
            moves.move(source, at_near, piece_shape, (near, (slot,)))
        given = {}
        moves.then.append(lambda filled: given.update(near=filled[near], sent=[filled[t] for t in sent]))
        moves.run()
        near_rows, sent_rows = given["near"], given["sent"]
    else:
        near_rows = at_mem(mem_rows, own_index)
        sent_rows = [at_mem(mem_rows[:, slot], 1 - own_index) for slot in range(slot_count)]

    qkv_half = 3 * model_width // 2
    (w_qkv,) = gather(0, [(0, qkv_half, 0), (qkv_half, qkv_half, 1)], True)
    far_parts = [swap_mem(sent_rows[0])]
    if staged:
        order.before(far_parts[0], far_live)
        moves = Moves(order, bits)
        w_qkv.wave.first(moves)
        places = [moves.passed(shard) for shard in shards[1:]]
        moves.then.append(lambda filled: shards.__setitem__(slice(1, None), [filled[i] for i in places]))
        moves.run()
    lead = 2 * model_width + LANES
    w_cq, w_co, w_norm, w_ckv, w_so = gather(
        1, [(0, lead, 0), (lead, 5 * model_width + LANES - lead, 1)]
    )
    (w_in,) = gather(2, [(0, ffn_in.shape[1], 0)])
    (w_out,) = gather(3, [(0, model_width, 1)])

    bucket = pick_entry(bucket_ids[0], own_index)
    lengths = target_lengths[0, 0]
    self_meta = jnp.stack([jnp.right_shift(jnp.int32(row_count), bucket), lengths[0], lengths[1]])
    cross_meta = bucket[None]
    live = jnp.concatenate((near_live, far_live), axis=1)
    key_bias = jnp.where(live == 1, 0.0, NEG_LARGE).astype(F32)
    key_columns = jnp.broadcast_to(key_bias[:, :, None], (*key_bias.shape, LANES))
    near_flat = near_rows.reshape(-1, model_width)
    slotted = (slot_count, mem_piece, 2 * model_width)

    def steps(*wanted):
        if staged:
            moves = Moves(order, bits)
            for weight, name in wanted:
                getattr(weight.wave, name)(moves)
            moves.run()

    steps((w_qkv, "second"))
    order.part()
    first_turned = Turned(target_in, near_flat)
    steps((w_ckv, "first"))
    order.part()
    steps((w_qkv, "third"))
    first_turned.due()
    order.part()
    steps((w_ckv, "second"))
    (united,) = project(order, "self_project", bits, w_qkv, [target_in], 1024)
    far_parts += [swap_mem(part) for part in gate(order, bits, sent_rows[1:])]
    steps((w_in, "first"))
    order.before(key_columns)
    self_mixed, self_log = self_forward(order, self_meta, united)
    order.part()
    steps((w_ckv, "third"))
    order.before(*far_parts[1:])
    order.part()
    steps((w_out, "first"))
    middle = Turned(self_mixed, *far_parts)
    table = norm_table(order, bits, w_norm)
    near_kv, far_kv = project(
        order, "cross_project", bits, w_ckv, [near_flat, *far_parts], 1024, [1, len(far_parts)]
    )
    near_kv, far_kv = near_kv.reshape(slotted), far_kv.reshape(slotted)
    order.part()
    steps((w_in, "second"))
    order.part()
    steps((w_out, "second"))
    middle.due()
    sum_one, first_out, first_low, cross_query = mix_norm(
        order, "self_mix", bits, w_so, self_mixed, target_in, table, 0, w_cq
    )
    cross_mixed, cross_log = cross_forward(
        order, cross_meta, cross_query, near_kv, far_kv, key_bias[:, None, :]
    )
    sum_two, second_out, second_low = mix_norm(
        order, "cross_mix", bits, w_co, cross_mixed, first_out, table, 1
    )
    later = Turned(first_low, cross_mixed, second_low)
    order.part()
    steps((w_in, "third"))
    steps((w_out, "third"))
    activated, slope, *turned = feed_in(order, bits, w_in, second_low, outer if staged else 0)
    later.due()
    hidden = Turned(activated, turned=turned)
    layer_out, grad_three, grad_ffn, stats_three = feed_out(
        order, bits, w_out, activated, second_out, table, grad_out
    )
    qkv_grad = Grad((first_turned, target_in))
    so_grad = Grad((middle, self_mixed))
    ckv_grad = Grad((first_turned, near_flat), (middle, *far_parts))
    cq_grad = Grad((later, first_low))
    co_grad = Grad((later, cross_mixed))
    in_grad = Grad((later, second_low))
    out_grad = Grad((hidden, activated))

    shards = {}

    def spread(name, parts, kinds):
        if staged:
            return Spread(parts, kinds)
        shards[name] = whole_sum(parts)
        return None

    def advance(seconds=(), thirds=()):
        if staged:
            waves = [wave for _, wave in thirds]
            joined = spread_steps(order, bits, seconds, waves)
            for (name, _), part in zip(thirds, joined):
                shards[name] = outer_sum(part)

    out_grad.take(grad_ffn)
    out_wave = spread("out", out_grad.make(model_width // 2), (0, 1))
    grad_hidden = feed_back(order, bits, w_out, grad_ffn, slope)
    in_grad.take(grad_hidden)
    grad_two, grad_cross_out, grad_cross_mixed, stats_two = norm_back(
        order, "cross_back", bits, w_in, grad_hidden, grad_three, sum_two, table, 1, w_co
    )
    co_grad.take(grad_cross_out)
    order.part()
    advance([out_wave])
    in_wave = spread("in", in_grad.make(2 * model_width), (0, 1))
    pair_width = 2 * model_width
    near_parts = co_grad.make(place=(0, 0, pair_width))
    grad_query_low, grad_near_kv, grad_far_kv = cross_backward(
        order,
        cross_meta,
        cross_query,
        near_kv,
        far_kv,
        key_columns,
        cross_mixed,
        grad_cross_mixed,
        cross_log,
    )
    cq_grad.take(grad_query_low)
    ckv_grad.take(grad_near_kv, grad_far_kv)
    order.part()
    advance([in_wave], [("out", out_wave)])

    def memory_back(cotangent):
        spans = [(0, start, start, model_width) for start in (0, model_width)]
        return input_back(order, "memory_back", bits, w_ckv, [cotangent], None, spans)

    grad_one, grad_self_out, grad_self_mixed, stats_one = norm_back(
        order, "self_back", bits, w_cq, grad_query_low, grad_two, sum_one, table, 0, w_so
    )
    so_grad.take(grad_self_out)
    stats = [jnp.sum(s.reshape(2, 8, model_width), axis=1) for s in (stats_one, stats_two, stats_three)]
    norm_grads = [
        jnp.pad(jnp.stack([s[i] for s in stats], axis=1), ((0, 0), (0, LANES - len(stats))))
        for i in range(2)
    ]
    norm_grads = jnp.concatenate(norm_grads, axis=1).astype(BF16)
    if staged:
        own, other = relative_rows(bits, norm_grads, outer)
        own = (own.astype(F32) + swap_core(other).astype(F32)).astype(BF16)
        norm_grads = (own[..., :LANES], own[..., LANES:])
        far_parts = ckv_grad.make(place=(1, 0, pair_width))
        near_parts = cq_grad.make(place=(0, model_width, pair_width), held=near_parts)
        mid_parts = [*near_parts, *far_parts]
    else:
        mid_parts = jnp.concatenate([near_parts, cq_grad.make(), ckv_grad.make()], axis=1)
    mid_wave = spread("mid", mid_parts, (0, 1))
    order.part()
    advance([], [("in", in_wave)])
    grad_united = self_backward(
        order,
        self_meta,
        united,
        self_mixed,
        grad_self_mixed,
        self_log,
    )
    qkv_grad.take(grad_united)
    half_width = model_width // 2
    if staged:
        so_wave = spread("so", so_grad.make(half_width, extra=norm_grads), (0, 1))
    else:
        part = so_grad.make()
        columns = [part[:, :half_width], norm_grads[:, :LANES], part[:, half_width:], norm_grads[:, LANES:]]
        so_wave = spread("so", jnp.concatenate(columns, axis=1), (0, 1))
    order.part()
    advance([mid_wave])
    qkv_wave = spread("qkv", qkv_grad.make(qkv_half), (0, 1))
    if staged:
        order.before(shards["out"], shards["in"])
        order.part()
        advance([], [("mid", mid_wave)])
    split = half_width + LANES
    grad_far = memory_back(grad_far_kv)
    if staged:
        order.part()
        advance([qkv_wave, so_wave])
        (grad_far,) = gate(order, bits, [grad_far])
    grad_far = swap_mem(grad_far)
    if staged:
        order.before(shards["mid"])
        order.part()
        blocks = spread_steps(order, bits, [], [so_wave, qkv_wave], True)
        blocks = [blocks[0]] + [swap_outer(blocks[far], far) for far in range(1, outer)]
    grad_near = memory_back(grad_near_kv)
    target_grad = input_back(
        order,
        "target_back",
        bits,
        w_qkv,
        [grad_united],
        grad_one,
        [(0, start, start, model_width) for start in range(0, w_qkv.width, model_width)],
    )
    so_spans = [(0, 0, half_width), (0, split, half_width)]
    norm_spans = [[(0, half_width, 3)], [(0, split + half_width, 3)]]
    mid_spans = [[(1, i * model_width, model_width)] for i in range(2)]
    mid_spans.append([(1, 2 * model_width, 2 * model_width)])
    spans = [[(0, 2 * split, 2 * qkv_half)], so_spans, *norm_spans, *mid_spans]
    if staged:
        last = last_shards(order, bits, blocks, shards["mid"], spans)
        moves = Moves(order, bits)
        target = moves.target((2, *near_flat.shape))
        for number, part in enumerate((grad_near, grad_far)):
            place = lambda bits, number=number: (bits[2] ^ number,)
            moves.move(moves.source(part), (slice(None),), near_flat.shape, (target, place))
        moves.then.append(lambda filled: shards.update(memory=filled[target]))
        moves.run()
        grad_pair = shards["memory"]
    else:
        grad_pair = jnp.stack((grad_near, grad_far))
        grad_pair = jnp.where(own_index == 0, grad_pair, grad_pair[::-1])
        sources = (jnp.concatenate((shards["so"], shards["qkv"]), axis=1), shards["mid"])
        last = [
            jnp.concatenate([sources[w][:, at : at + size] for w, at, size in span], axis=1)
            for span in spans
        ]
    qkv_shard, so_shard, gains, biases, co_shard, cq_shard, ckv_shard = last

    return (
        layer_out,
        target_grad,
        grad_pair.reshape(1, pieces, 1, *near_rows.shape),
        qkv_shard,
        so_shard,
        cq_shard,
        ckv_shard,
        co_shard,
        shards["in"].astype(F32),
        shards["out"].astype(F32),
        gains,
        biases,
    )


def solution(mesh):
    rows = P(("dp", "mem"), None)
    memory = P("dp", None, "mem", None, None, None)
    return jax.shard_map(
        per_device,
        mesh=mesh,
        in_specs=(
            rows,
            memory,
            P("dp", None),
            P("dp", "mem", None),
            P("dp", None, "mem", None, None),
        )
        + (rows,) * 10,
        out_specs=(rows, rows, memory) + (rows,) * 9,
        check_vma=False,
    )
```

```python
import math

import jax
import jax.numpy as jnp
from jax import lax
from jax.experimental import pallas as pl
from jax.experimental.pallas import tpu as pltpu
from jax.sharding import PartitionSpec as P

HD = 64
LANES = 128
PAIRS = 2
WIDE = PAIRS * LANES
ALPHA = 300.0**0.25
NEG_LARGE = -1e30
EPSILON = 1e-05
VMEM_BYTES = 64 * 1024 * 1024 - 128 * 1024
SCALE = HD**-0.5
BF16 = jnp.bfloat16
F32 = jnp.float32


def plain_dot(first_op, second_op):
    return jnp.dot(first_op, second_op, preferred_element_type=F32)


def lead_dot(first_op, second_op):
    return lax.dot_general(
        first_op, second_op, (((0,), (0,)), ((), ())), preferred_element_type=F32
    )


def back_dot(first_op, second_op):
    return lax.dot_general(
        first_op, second_op, (((1,), (1,)), ((), ())), preferred_element_type=F32
    )


def pick_entry(values, wanted):
    return jnp.sum(jnp.where(jnp.arange(values.shape[0]) == wanted, values, 0))


def kernel_params():
    return pltpu.CompilerParams(vmem_limit_bytes=VMEM_BYTES)


class Order:
    def __init__(self):
        self.last, self.due, self.parted = None, [], False

    def before(self, *arrays):
        self.due += arrays

    def part(self):
        self.parted = True

    def launch(self, kernel, name, operands, in_specs, out_specs, out_shape, scratch, grid, aliases):
        ties = self.due + ([self.last] if self.last is not None else [])
        ties = [tie for tie in ties if not any(tie is operand for operand in operands)]
        self.due = []
        count, n_ties = len(operands), len(ties)

        def tied(*refs):
            kernel(*refs[:count], *refs[count + n_ties :])

        specs = list(in_specs) + [pl.BlockSpec(memory_space=pltpu.HBM)] * n_ties
        cost = pl.CostEstimate(
            flops=10**12 if self.parted else 10**6, bytes_accessed=1, transcendentals=0
        )
        self.parted = False
        if grid is None:
            run = pl.pallas_call(
                tied,
                in_specs=[pl.BlockSpec(memory_space=pltpu.SMEM)] + specs,
                out_specs=out_specs,
                out_shape=out_shape,
                scratch_shapes=scratch,
                input_output_aliases=aliases,
                compiler_params=kernel_params(),
                cost_estimate=cost,
                name=name,
            )
        else:
            run = pl.pallas_call(
                tied,
                grid_spec=pltpu.PrefetchScalarGridSpec(
                    num_scalar_prefetch=1,
                    grid=grid,
                    in_specs=specs,
                    out_specs=out_specs,
                    scratch_shapes=scratch,
                ),
                out_shape=out_shape,
                input_output_aliases=aliases,
                compiler_params=kernel_params(),
                cost_estimate=cost,
                name=name,
            )
        results = run(*operands, *ties)
        self.last = results[0]
        return results


def whole_spec(shape):
    return pl.BlockSpec(shape, lambda *_: (0,) * len(shape))


def head_lanes(rows, head):
    lane = lax.broadcasted_iota(jnp.int32, (rows, LANES), 1)
    return (lane < HD) if head == 0 else (lane >= HD)


def visible(query_ids, key_ids, slot_len, first_len, second_len):
    query_slot = (query_ids >= slot_len).astype(jnp.int32)
    key_slot = (key_ids >= slot_len).astype(jnp.int32)
    place = key_ids - key_slot * slot_len
    limit = jnp.where(key_slot == 0, first_len, second_len)
    return (query_slot == key_slot) & (key_ids <= query_ids) & (place < limit)


def pair_forward(query, keys, values, bias):
    rows, key_rows = query.shape[0], keys.shape[0]
    mixed, peaks = [], []
    for head in range(2):
        mine = head_lanes(rows, head)
        masked = jnp.where(mine, query * BF16(SCALE), BF16(0))
        scores = back_dot(masked, keys) + bias
        peak = jnp.max(scores, axis=1, keepdims=True)
        raised = jnp.exp(scores - peak).astype(BF16)
        widened = jnp.where(head_lanes(key_rows, head), values, BF16(1))
        mixed.append(plain_dot(raised, widened))
        peaks.append(peak)
    first = head_lanes(rows, 0)
    totals = pltpu.roll(jnp.where(first, mixed[1], mixed[0]), HD, 1)
    joined = jnp.where(first, mixed[0], mixed[1])
    log_totals = jnp.where(first, peaks[0], peaks[1]) + jnp.log(totals)
    return joined / totals, log_totals


def pair_backward(query, keys, values, upstream, bias, log_rows, delta_rows):
    rows, key_rows = query.shape[0], keys.shape[0]
    grad_q, grad_k, grad_v = None, None, None
    for head in range(2):
        mine = head_lanes(rows, head)
        masked = jnp.where(mine, query * BF16(SCALE), BF16(0))
        masked_up = jnp.where(mine, upstream, BF16(0))
        scores = back_dot(keys, masked) + bias
        probs = jnp.exp(scores - log_rows[head])
        grad_probs = back_dot(values, masked_up)
        grad_scores = (probs * (grad_probs - delta_rows[head])).astype(BF16)
        part_v = plain_dot(probs.astype(BF16), masked_up)
        part_k = plain_dot(grad_scores, masked)
        masked_keys = jnp.where(head_lanes(key_rows, head), keys, BF16(0))
        part_q = lead_dot(grad_scores, masked_keys)
        grad_q = part_q if grad_q is None else grad_q + part_q
        grad_k = part_k if grad_k is None else grad_k + part_k
        grad_v = part_v if grad_v is None else grad_v + part_v
    return grad_q * SCALE, grad_k, grad_v


def stat_rows(log_block, mixed, upstream):
    log_turned = log_block.T
    products = (mixed.astype(F32) * upstream.astype(F32)).T
    log_rows = [log_turned[:1], log_turned[HD : HD + 1]]
    delta_rows = [jnp.sum(products[h * HD : (h + 1) * HD], axis=0, keepdims=True) for h in range(2)]
    return log_rows, delta_rows


def pair_lanes(pair):
    return slice(pair * LANES, (pair + 1) * LANES)


def self_forward_kernel(meta, q_ref, k_ref, v_ref, mixed_ref, log_ref, bias):
    rows = q_ref.shape[0]

    @pl.when(pl.program_id(0) == 0)
    def _():
        query_ids = lax.broadcasted_iota(jnp.int32, (rows, rows), 0)
        key_ids = lax.broadcasted_iota(jnp.int32, (rows, rows), 1)
        seen = visible(query_ids, key_ids, meta[0], meta[1], meta[2])
        bias[...] = jnp.where(seen, 0.0, NEG_LARGE)

    half = rows // 2
    for pair in range(PAIRS):
        lanes = pair_lanes(pair)
        for start, stop in ((0, half), (half, rows)):
            mixed, log_totals = pair_forward(
                q_ref[start:stop, lanes],
                k_ref[:stop, lanes],
                v_ref[:stop, lanes],
                bias[start:stop, :stop],
            )
            mixed_ref[start:stop, lanes] = mixed.astype(BF16)
            log_ref[start:stop, lanes] = log_totals


def self_forward(order, meta, united):
    rows, width = united.shape[0], united.shape[1] // 3
    steps = width // WIDE
    spec = lambda third: pl.BlockSpec((rows, WIDE), lambda i, _: (0, third * steps + i))
    return order.launch(
        self_forward_kernel,
        "self_forward",
        [meta, united, united, united],
        [spec(0), spec(1), spec(2)],
        [spec(0), spec(0)],
        [jax.ShapeDtypeStruct((rows, width), kind) for kind in (BF16, F32)],
        [pltpu.VMEM((rows, rows), F32)],
        (steps,),
        {},
    )


def self_backward_kernel(
    meta, q_ref, k_ref, v_ref, mixed_ref, up_ref, log_ref, grad_ref, bias
):
    rows = q_ref.shape[0]
    width = grad_ref.shape[1] // 3
    step = pl.program_id(0)

    @pl.when(step == 0)
    def _():
        key_ids = lax.broadcasted_iota(jnp.int32, (rows, rows), 0)
        query_ids = lax.broadcasted_iota(jnp.int32, (rows, rows), 1)
        seen = visible(query_ids, key_ids, meta[0], meta[1], meta[2])
        bias[...] = jnp.where(seen, 0.0, NEG_LARGE)

    half = rows // 2
    for pair in range(PAIRS):
        lanes = pair_lanes(pair)
        log_rows, delta_rows = stat_rows(log_ref[:, lanes], mixed_ref[:, lanes], up_ref[:, lanes])
        parts = []
        for start, stop in ((0, half), (half, rows)):
            parts.append(
                pair_backward(
                    q_ref[start:stop, lanes],
                    k_ref[:stop, lanes],
                    v_ref[:stop, lanes],
                    up_ref[start:stop, lanes],
                    bias[:stop, start:stop],
                    [row[:, start:stop] for row in log_rows],
                    [row[:, start:stop] for row in delta_rows],
                )
            )
        low, high = parts
        at = step * WIDE + pair * LANES
        columns = lambda third: pl.ds(pl.multiple_of(third * width + at, LANES), LANES)
        grad_ref[:half, columns(0)] = low[0].astype(BF16)
        grad_ref[half:, columns(0)] = high[0].astype(BF16)
        for third in (1, 2):
            grad_ref[:half, columns(third)] = (low[third] + high[third][:half]).astype(BF16)
            grad_ref[half:, columns(third)] = high[third][half:].astype(BF16)


def self_backward(order, meta, united, mixed, upstream, log_totals):
    rows, width = mixed.shape
    steps = width // WIDE
    spec = lambda third: pl.BlockSpec((rows, WIDE), lambda i, _: (0, third * steps + i))
    shape = (rows, 3 * width)
    return order.launch(
        self_backward_kernel,
        "self_backward",
        [meta, united, united, united, mixed, upstream, log_totals],
        [spec(0), spec(1), spec(2), spec(0), spec(0), spec(0)],
        [whole_spec(shape)],
        [jax.ShapeDtypeStruct(shape, BF16)],
        [pltpu.VMEM((rows, rows), F32)],
        (steps,),
        {},
    )[0]


def join_keys(near_ref, far_ref, joined):
    slots, piece = near_ref.shape[0], near_ref.shape[1]
    for slot in range(slots):
        joined[slot, :piece, :] = near_ref[slot]
        joined[slot, piece:, :] = far_ref[slot]


def cross_forward_kernel(
    meta, q_ref, kn_ref, vn_ref, kf_ref, vf_ref, bias_ref, mixed_ref, log_ref, keys, values
):
    half = q_ref.shape[0] // 2
    join_keys(kn_ref, kf_ref, keys)
    join_keys(vn_ref, vf_ref, values)
    for pair in range(PAIRS):
        lanes = pair_lanes(pair)
        for part in range(2):
            slot = part * meta[0]
            rows = slice(part * half, (part + 1) * half)
            mixed, log_totals = pair_forward(
                q_ref[rows, lanes], keys[slot, :, lanes], values[slot, :, lanes], bias_ref[slot]
            )
            mixed_ref[rows, lanes] = mixed.astype(BF16)
            log_ref[rows, lanes] = log_totals


def cross_specs(rows, slots, piece, steps):
    row_spec = pl.BlockSpec((rows, WIDE), lambda i, _: (0, i))
    half = lambda at: pl.BlockSpec((slots, piece, WIDE), lambda i, _: (0, 0, at * steps + i))
    return row_spec, [row_spec, half(0), half(1), half(0), half(1)]


def cross_forward(order, meta, query, near, far, bias):
    rows, width = query.shape
    slots, piece = near.shape[0], near.shape[1]
    steps = width // WIDE
    row_spec, specs = cross_specs(rows, slots, piece, steps)
    return order.launch(
        cross_forward_kernel,
        "cross_forward",
        [meta, query, near, near, far, far, bias],
        specs + [whole_spec(bias.shape)],
        [row_spec, row_spec],
        [jax.ShapeDtypeStruct((rows, width), kind) for kind in (BF16, F32)],
        [pltpu.VMEM((slots, 2 * piece, WIDE), BF16)] * 2,
        (steps,),
        {},
    )


def cross_backward_kernel(
    meta,
    q_ref,
    kn_ref,
    vn_ref,
    kf_ref,
    vf_ref,
    bias_ref,
    mixed_ref,
    up_ref,
    log_ref,
    grad_q_ref,
    grad_near_ref,
    grad_far_ref,
    keys,
    values,
):
    half = q_ref.shape[0] // 2
    slots, piece = kn_ref.shape[0], kn_ref.shape[1]
    width = grad_near_ref.shape[1] // 2
    join_keys(kn_ref, kf_ref, keys)
    join_keys(vn_ref, vf_ref, values)
    split = meta[0].astype(F32)
    for pair in range(PAIRS):
        lanes = pair_lanes(pair)
        log_rows, delta_rows = stat_rows(log_ref[:, lanes], mixed_ref[:, lanes], up_ref[:, lanes])
        parts = []
        for part in range(2):
            slot = part * meta[0]
            rows = slice(part * half, (part + 1) * half)
            bias_column = bias_ref[slot]
            grads = pair_backward(
                q_ref[rows, lanes],
                keys[slot, :, lanes],
                values[slot, :, lanes],
                up_ref[rows, lanes],
                jnp.concatenate([bias_column] * (half // LANES), axis=1),
                [row[:, rows] for row in log_rows],
                [row[:, rows] for row in delta_rows],
            )
            grad_q_ref[rows, lanes] = grads[0].astype(BF16)
            parts.append(grads)
        start = pl.program_id(0) * WIDE + pair * LANES
        for which in range(2):
            early, late = parts[0][1 + which], parts[1][1 + which]
            columns = pl.ds(pl.multiple_of(which * width + start, LANES), LANES)
            by_slot = (early + late * (1.0 - split), late * split)
            for slot in range(slots):
                for source, target in enumerate((grad_near_ref, grad_far_ref)):
                    target[slot * piece : (slot + 1) * piece, columns] = by_slot[slot][
                        source * piece : (source + 1) * piece
                    ].astype(BF16)


def cross_backward(order, meta, query, near, far, bias, mixed, upstream, log_totals):
    rows, width = query.shape
    slots, piece = near.shape[0], near.shape[1]
    steps = width // WIDE
    memory = (slots * piece, 2 * width)
    row_spec, specs = cross_specs(rows, slots, piece, steps)
    return order.launch(
        cross_backward_kernel,
        "cross_backward",
        [meta, query, near, near, far, far, bias, mixed, upstream, log_totals],
        specs + [whole_spec(bias.shape)] + [row_spec] * 3,
        [row_spec, whole_spec(memory), whole_spec(memory)],
        [jax.ShapeDtypeStruct(shape, BF16) for shape in ((rows, width), memory, memory)],
        [pltpu.VMEM((slots, 2 * piece, WIDE), BF16)] * 2,
        (steps,),
        {},
    )


def swap_core(values):
    size = lax.axis_size("dp")
    return lax.ppermute(values, "dp", [(i, i ^ 1) for i in range(size)])


def swap_next(values):
    size = lax.axis_size("dp")
    return lax.ppermute(values, "dp", [(i, i ^ 2) for i in range(size)])


def swap_mem(values):
    return lax.ppermute(values, "mem", [(0, 1), (1, 0)])


def swap_outer(values, far):
    size = lax.axis_size("dp")
    return lax.ppermute(values, "dp", [(i, i ^ (4 * far)) for i in range(size)])


def outer_groups():
    size = lax.axis_size("dp")
    return [list(range(base, size, 4)) for base in range(4)]


def place_bits():
    dp, mem = lax.axis_index("dp"), lax.axis_index("mem")
    return jnp.stack([(dp >> 1) & 1, dp & 1, mem, dp >> 2]).astype(jnp.int32)


def outer_gather(shard):
    stacked = lax.all_gather(shard, "dp", axis_index_groups=outer_groups(), axis=0, tiled=True)
    return stacked.reshape(-1, *shard.shape)


def gate(order, bits, arrays):
    def kernel(*refs):
        pass

    return order.launch(
        kernel,
        "gate",
        [bits, *arrays],
        [pl.BlockSpec(memory_space=pltpu.HBM)] * len(arrays),
        [pl.BlockSpec(memory_space=pltpu.HBM)] * len(arrays),
        [jax.ShapeDtypeStruct(array.shape, array.dtype) for array in arrays],
        [],
        None,
        {1 + i: i for i in range(len(arrays))},
    )


class Moves:
    def __init__(self, order, bits):
        self.order, self.bits = order, bits
        self.sources, self.shapes, self.moves, self.aliases, self.then = [], [], [], {}, []

    def source(self, array):
        self.sources.append(array)
        return len(self.sources) - 1

    def target(self, shape, held=None):
        self.shapes.append(shape)
        if held is not None:
            self.aliases[1 + self.source(held)] = len(self.shapes) - 1
        return len(self.shapes) - 1

    def passed(self, array):
        return self.target(array.shape, array)

    def move(self, source, source_at, shape, *goals):
        self.moves.append((source, source_at, shape, goals))

    def run(self):
        moves, n_in, n_out = self.moves, len(self.sources), len(self.shapes)
        most = max([len(move[3]) for move in moves] + [0])

        def kernel(bits_ref, *refs):
            bits = [bits_ref[i] for i in range(4)]
            taken, given = refs[:n_in], refs[n_in : n_in + n_out]
            slots, sems = refs[n_in + n_out : -1], refs[-1]
            loads, stores = [], []
            for number, (source, source_at, _, goals) in enumerate(moves):
                slot = slots[number]
                loads.append(
                    pltpu.make_async_copy(
                        taken[source].at[source_at(bits) if callable(source_at) else source_at],
                        slot,
                        sems.at[0, number],
                    )
                )
                stores.append(
                    [
                        pltpu.make_async_copy(
                            slot, given[which].at[at(bits) if callable(at) else at], sems.at[1 + i, number]
                        )
                        for i, (which, at) in enumerate(goals)
                    ]
                )
            for load in loads:
                load.start()
            for load, group in zip(loads, stores):
                load.wait()
                for store in group:
                    store.start()
            for group in stores:
                for store in group:
                    store.wait()

        filled = self.order.launch(
            kernel,
            "move_blocks",
            [self.bits, *self.sources],
            [pl.BlockSpec(memory_space=pltpu.HBM)] * n_in,
            [pl.BlockSpec(memory_space=pltpu.HBM)] * n_out,
            [jax.ShapeDtypeStruct(shape, BF16) for shape in self.shapes],
            [pltpu.VMEM(shape, BF16) for _, _, shape, _ in moves]
            + [pltpu.SemaphoreType.DMA((1 + most, max(1, len(moves))))],
            None,
            self.aliases,
        )
        for step in self.then:
            step(filled)


def cast_shards(order, bits, groups):
    shapes = [(group[0].shape[0], sum(part.shape[1] for part in group)) for group in groups]
    parts = [part for group in groups for part in group]

    def kernel(bits_ref, *refs):
        number = 0
        for group, target in zip(groups, refs[len(parts) :]):
            start = 0
            for part in group:
                stop = start + part.shape[1]
                target[:, start:stop] = refs[number][...].astype(BF16)
                start, number = stop, number + 1

    return order.launch(
        kernel,
        "cast_shards",
        [bits, *parts],
        [pl.BlockSpec(memory_space=pltpu.VMEM)] * len(parts),
        [pl.BlockSpec(memory_space=pltpu.VMEM)] * len(shapes),
        [jax.ShapeDtypeStruct(shape, BF16) for shape in shapes],
        [],
        None,
        {},
    )


FIRST = (swap_next, swap_mem)
SECOND = (swap_mem, swap_next)


class Wave:
    def __init__(self, shard, windows, direct):
        self.windows = [(pl.ds(start, size), kind) for start, size, kind in windows]
        self.rows, self.columns = shard.shape
        self.outer = lax.axis_size("dp") // 4
        if direct:
            self.shards = [shard] + [swap_outer(shard, far) for far in range(1, self.outer)]
        else:
            self.stacked = outer_gather(shard)
        self.direct = direct

    def first(self, moves):
        def send(parts):
            self.pairs = [(part, FIRST[kind](part)) for part, (_, kind) in zip(parts, self.windows)]

        if not self.direct and len(self.windows) == 1:
            target = moves.passed(self.stacked)
            moves.then.append(lambda filled: send([filled[target]]))
            return
        targets = [moves.target((self.outer, self.rows, w.size)) for w, _ in self.windows]
        sources = [moves.source(part) for part in (self.shards if self.direct else [self.stacked])]
        for block in range(self.outer):
            for target, (window, _) in zip(targets, self.windows):
                shape = (self.rows, window.size)
                if self.direct:
                    goal = (target, lambda bits, block=block: (bits[3] ^ block,))
                    moves.move(sources[block], (slice(None), window), shape, goal)
                else:
                    goal = (target, (block,))
                    moves.move(sources[0], (block, slice(None), window), shape, goal)
        moves.then.append(lambda filled: send([filled[target] for target in targets]))

    def place(self, kind, second, first, block, window):
        near, mem = (first, second) if kind == 0 else (second, first)
        return lambda bits: (block, bits[0] ^ near, bits[2] ^ mem, slice(None), window)

    def second(self, moves):
        sources = [[moves.source(part) for part in pair] for pair in self.pairs]
        targets = [moves.target((2, *pair[0].shape)) for pair in self.pairs]
        own = moves.target((self.outer, 2, 2, self.rows, self.columns))
        for block in range(self.outer):
            for number, (window, kind) in enumerate(self.windows):
                for side in range(2):
                    goal = (targets[number], (side, block))
                    again = (own, self.place(kind, 0, side, block, window))
                    shape = (self.rows, window.size)
                    moves.move(sources[number][side], (block,), shape, goal, again)

        def send(filled):
            self.own = filled[own]
            self.far = [
                SECOND[kind](filled[target]) for target, (_, kind) in zip(targets, self.windows)
            ]

        moves.then.append(send)

    def third(self, moves):
        own = moves.target(self.own.shape, self.own)
        for number, (window, kind) in enumerate(self.windows):
            source = moves.source(self.far[number])
            for block in range(self.outer):
                for side in range(2):
                    goal = (own, self.place(kind, 1, side, block, window))
                    moves.move(source, (side, block), (self.rows, window.size), goal)

        def send(filled):
            shape = (2 * self.outer, 2 * self.rows, self.columns)
            self.own = filled[own].reshape(shape)
            self.other = swap_core(self.own)

        moves.then.append(send)


class Weight:
    def __init__(self, wave, start, width, whole=None):
        self.wave, self.start, self.width, self.whole = wave, start, width, whole
        if whole is not None:
            self.blocks, self.rows = whole.shape[0], whole.shape[2]
        else:
            self.blocks, self.rows = 2 * wave.outer, 2 * wave.rows
        self.features = self.blocks * 2 * self.rows

    def pieces(self):
        return [self.whole] if self.whole is not None else [self.wave.own, self.wave.other]

    def copies(self, kind, start, size, bits, find, target):
        if kind == "columns":
            blocks, columns = slice(None), pl.ds(self.start + start, size)
        else:
            blocks, columns = pl.ds(start, size), pl.ds(self.start, self.width)
        if self.whole is not None:
            return [(find(self.whole).at[blocks, :, :, columns], target)]
        return [
            (find(array).at[blocks, :, columns], target.at[:, bits[1] ^ core])
            for core, array in enumerate((self.wave.own, self.wave.other))
        ]


def weight_call(order, name, bits, weights, plan, inputs, outs, scratch, body, streams=None, sends=0):
    streams = streams or {}
    arrays = []
    for weight in weights:
        arrays += [a for a in weight.pieces() if not any(a is b for b in arrays)]
    kind, size = plan[0][1], plan[0][3]
    lead = weights[plan[0][0]]
    if kind == "columns":
        chunk = (lead.blocks, 2, lead.rows, size)
    else:
        chunk = (size, 2, lead.rows, lead.width)
    n_in, n_arrays, n_out = len(inputs), len(arrays), len(outs)
    depth = min(3, len(plan))
    streamed = sorted(streams)
    most = max([1] + [inputs[i].shape[1] // streams[i] for i in streamed])

    def kernel(bits_ref, *refs):
        ins, refs = list(refs[:n_in]), refs[n_in:]
        pieces, refs = refs[:n_arrays], refs[n_arrays:]
        out_refs, refs = refs[:n_out], refs[n_out:]
        held, sems, stream_sems, send_sems = refs[-4:]
        staged = refs[: n_out if sends else 0]
        stream_refs = refs[len(staged) : len(staged) + len(streamed)]
        rest = refs[len(staged) + len(streamed) : -4]
        bits_now = [bits_ref[i] for i in range(3)]

        def find(array):
            return next(ref for ref, known in zip(pieces, arrays) if known is array)

        def issue(number):
            which, kind, start, size = plan[number]
            slot = number % depth
            for source, target in weights[which].copies(
                kind, start, size, bits_now, find, held.at[slot]
            ):
                pltpu.make_async_copy(source, target, sems.at[slot]).start()

        taken, coming, sent = [0], {}, []

        def fetch():
            number = taken[0]
            taken[0] += 1
            if depth > 1 and number + depth - 1 < len(plan):
                issue(number + depth - 1)
            slot = number % depth
            pltpu.make_async_copy(held.at[slot], held.at[slot], sems.at[slot]).wait()
            return held[slot].reshape(-1, chunk[-1])

        def need(which, part=0):
            coming.pop((which, part)).wait()

        def send(which, columns=None):
            columns = slice(None) if columns is None else columns
            copy = pltpu.make_async_copy(
                staged[which].at[:, columns], out_refs[which].at[:, columns], send_sems.at[len(sent)]
            )
            copy.start()
            sent.append(copy)

        fetch.need, fetch.send, fetch.bits = need, send, bits_now
        for number in range(max(1, depth - 1)):
            issue(number)
        for number, which in enumerate(streamed):
            count = streams[which]
            for part in range(inputs[which].shape[1] // count):
                columns = pl.ds(part * count, count)
                copy = pltpu.make_async_copy(
                    ins[which].at[:, columns],
                    stream_refs[number].at[:, columns],
                    stream_sems.at[number, part],
                )
                copy.start()
                coming[which, part] = copy
            ins[which] = stream_refs[number]
        body(fetch, ins, staged if sends else out_refs, rest)
        for copy in sent + list(coming.values()):
            copy.wait()

    hbm, vmem = pl.BlockSpec(memory_space=pltpu.HBM), pl.BlockSpec(memory_space=pltpu.VMEM)
    return order.launch(
        kernel,
        name,
        [bits, *inputs, *arrays],
        [hbm if i in streams else vmem for i in range(n_in)] + [hbm] * n_arrays,
        [hbm if sends else vmem] * n_out,
        [jax.ShapeDtypeStruct(shape, kind) for shape, kind in outs],
        ([pltpu.VMEM(shape, kind) for shape, kind in outs] if sends else [])
        + [pltpu.VMEM(inputs[i].shape, inputs[i].dtype) for i in streamed]
        + [pltpu.VMEM(shape, kind) for shape, kind in scratch]
        + [
            pltpu.VMEM((depth, *chunk), BF16),
            pltpu.SemaphoreType.DMA((depth,)),
            pltpu.SemaphoreType.DMA((max(1, len(streamed)), most)),
            pltpu.SemaphoreType.DMA((max(1, sends),)),
        ],
        None,
        {},
    )


def columns_plan(which, width, size):
    return [(which, "columns", start, size) for start in range(0, width, size)]


def row_blocks(rows, size, step):
    def run(i, carry):
        step(pl.ds(pl.multiple_of(i * size, size), size))
        return carry

    lax.fori_loop(0, rows // size, run, 0)


def normed_parts(values):
    centred = values - jnp.mean(values, axis=-1, keepdims=True)
    spread = jnp.mean(centred * centred, axis=-1, keepdims=True)
    rate = lax.rsqrt(spread + EPSILON)
    return centred * rate, rate


def norm_gradient(normed, rate, gain, cotangent):
    inner = cotangent * gain
    mean_inner = jnp.mean(inner, axis=-1, keepdims=True)
    mean_both = jnp.mean(inner * normed, axis=-1, keepdims=True)
    return rate * (inner - mean_inner - normed * mean_both)


def add_stats(stats, normed, cotangent):
    fold = lambda values: jnp.sum(values.reshape(-1, 8, values.shape[-1]), axis=0)
    stats[:8, :] += fold(cotangent * normed)
    stats[8:, :] += fold(cotangent)


def norm_table(order, bits, weight):
    features = weight.features

    def body(fetch, ins, outs, scratch):
        outs[0][...] = fetch().astype(F32).T[:8]

    return weight_call(
        order, "norm_table", bits, [weight], [(0, "columns", 0, LANES)], [],
        [((8, features), F32)], [], body,
    )[0]


def project(order, name, bits, weight, sources, size, groups=None):
    groups = groups or [1] * len(sources)
    goals = []
    for number, count in enumerate(groups):
        row = 0
        for _ in range(count):
            goals.append((number, row))
            row += sources[len(goals) - 1].shape[0]
    rows = [
        sum(source.shape[0] for source, (which, _) in zip(sources, goals) if which == number)
        for number in range(len(groups))
    ]

    def body(fetch, ins, outs, scratch):
        for start in range(0, weight.width, size):
            chunk, columns = fetch(), slice(start, start + size)
            for number, (source, (which, row)) in enumerate(zip(ins, goals)):
                if start == 0:
                    fetch.need(number)
                block = slice(row, row + source.shape[0])
                outs[which][block, columns] = plain_dot(source[...], chunk).astype(BF16)
            for which in range(len(groups)):
                fetch.send(which, columns)

    return weight_call(
        order, name, bits, [weight], columns_plan(0, weight.width, size), sources,
        [((count, weight.width), BF16) for count in rows], [], body,
        {i: source.shape[1] for i, source in enumerate(sources)},
        weight.width // size * len(groups),
    )


def mix_norm(order, name, bits, weight, mixed, residual, table, index, query_weight=None):
    rows, width = mixed.shape
    size = min(1024, width)

    def body(fetch, ins, outs, scratch):
        mixed_ref, residual_ref, table_ref = ins
        summed, out, out_low = outs[:3]
        fetch.need(0)
        for start in range(0, width, size):
            part = plain_dot(mixed_ref[...], fetch())
            if start == 0:
                fetch.need(1)
            columns = slice(start, start + size)
            summed[:, columns] = ALPHA * residual_ref[:, columns].astype(F32) + part
        fetch.send(0)
        gain, shift = table_ref[index : index + 1, :], table_ref[3 + index : 4 + index, :]

        def step(block):
            normed, _ = normed_parts(summed[block, :])
            values = normed * gain + shift
            out[block, :] = values
            out_low[block, :] = values.astype(BF16)

        row_blocks(rows, 128, step)
        fetch.send(1)
        fetch.send(2)
        if query_weight is not None:
            for start in range(0, width, size):
                part = plain_dot(out_low[...], fetch())
                outs[3][:, start : start + size] = part.astype(BF16)
            fetch.send(3)

    weights = [weight] + ([query_weight] if query_weight is not None else [])
    plan = [entry for i in range(len(weights)) for entry in columns_plan(i, width, size)]
    outs = [((rows, width), F32), ((rows, width), F32), ((rows, width), BF16)]
    if query_weight is not None:
        outs.append(((rows, width), BF16))
    return weight_call(
        order, name, bits, weights, plan, [mixed, residual, table], outs, [], body,
        {0: width, 1: width}, len(outs),
    )


def feed_in(order, bits, weight, source, outer):
    rows, size = source.shape[0], 1024
    shard_rows = weight.width // (8 * outer) if outer else 0
    turning = shard_rows > 0 and LANES % shard_rows == 0

    def turn_chunk(bits_now, values, start, targets):
        for block in range(size // LANES):
            turned = values[:, block * LANES : (block + 1) * LANES].T
            for part in range(LANES // shard_rows):
                device = (start + block * LANES) // shard_rows + part
                mem, core, near = device & 1, (device >> 1) & 1, (device >> 2) & 1
                place = (mem ^ bits_now[2]) * 2 + (near ^ bits_now[0])
                place = (place * outer + (device >> 3)) * shard_rows
                block_rows = pl.ds(pl.multiple_of(place, shard_rows), shard_rows)
                piece = turned[part * shard_rows : (part + 1) * shard_rows]
                for side, target in enumerate(targets):

                    @pl.when((core ^ bits_now[1]) == side)
                    def _():
                        target[block_rows, :] = piece

    def body(fetch, ins, outs, scratch):
        held = scratch[0]
        fetch.need(0)
        for start in range(0, weight.width, size):
            held[...] = plain_dot(ins[0][...], fetch())

            def step(block):
                hidden = held[block, :]
                below = 0.5 + 0.5 * lax.erf(hidden * (0.5**0.5))
                density = jnp.exp(-0.5 * hidden * hidden) * (2.0 * jnp.pi) ** -0.5
                outs[0][block, start : start + size] = (hidden * below).astype(BF16)
                outs[1][block, start : start + size] = (below + hidden * density).astype(BF16)

            row_blocks(rows, 256, step)
            columns = slice(start, start + size)
            for which in range(2):
                fetch.send(which, columns)
            if turning:
                turn_chunk(fetch.bits, outs[0][:, columns], start, outs[2:])
        for which in range(2, len(outs)):
            fetch.send(which)

    out, turned = ((rows, weight.width), BF16), ((weight.width // 2, rows), BF16)
    outs = [out, out] + ([turned, turned] if turning else [])
    return weight_call(
        order, "feed_in", bits, [weight], columns_plan(0, weight.width, size), [source], outs,
        [((rows, size), F32)], body, {0: source.shape[1]}, 2 * weight.width // size + len(outs) - 2,
    )


def feed_out(order, bits, weight, activated, residual, table, cotangent):
    rows, width = residual.shape
    size = 512 if width % 512 == 0 else width

    def body(fetch, ins, outs, scratch):
        act_ref, residual_ref, table_ref, up_ref = ins
        layer_out, grad, grad_low, stats = outs
        summed = scratch[0]
        fetch.need(0)
        for start in range(0, width, size):
            columns = slice(start, start + size)
            part = plain_dot(act_ref[...], fetch())
            if start == 0:
                fetch.need(1)
            summed[:, columns] = ALPHA * residual_ref[:, columns] + part
        fetch.need(3)
        gain, shift = table_ref[2:3, :], table_ref[5:6, :]
        stats[...] = jnp.zeros_like(stats)

        def step(block):
            normed, rate = normed_parts(summed[block, :])
            layer_out[block, :] = (normed * gain + shift).astype(BF16)
            upstream = up_ref[block, :].astype(F32)
            values = norm_gradient(normed, rate, gain, upstream)
            grad[block, :] = values
            grad_low[block, :] = values.astype(BF16)
            add_stats(stats, normed, upstream)

        row_blocks(rows, 128, step)

    outs = [((rows, width), BF16), ((rows, width), F32), ((rows, width), BF16), ((16, width), F32)]
    return weight_call(
        order, "feed_out", bits, [weight], columns_plan(0, width, size),
        [activated, residual, table, cotangent], outs, [((rows, width), F32)], body,
        {0: activated.shape[1], 1: width, 3: width},
    )


def feed_back(order, bits, weight, cotangent, slope):
    rows, features = slope.shape
    size = 1024 if features % 1024 == 0 else features
    steps = features // size

    def body(fetch, ins, outs, scratch):
        fetch.need(0)
        for number in range(steps):
            part = back_dot(ins[0][...], fetch())
            fetch.need(1, number)
            columns = slice(number * size, (number + 1) * size)
            outs[0][:, columns] = (part * ins[1][:, columns].astype(F32)).astype(BF16)
            fetch.send(0, columns)

    blocks = weight.blocks // steps
    return weight_call(
        order, "feed_back", bits, [weight], [(0, "rows", i * blocks, blocks) for i in range(steps)],
        [cotangent, slope], [((rows, features), BF16)], [], body,
        {0: cotangent.shape[1], 1: size}, steps,
    )[0]


def norm_back(order, name, bits, weight, cotangent, carried, summed, table, index, mix_weight):
    rows, width = summed.shape
    size = min(1024, weight.width)

    def body(fetch, ins, outs, scratch):
        up_ref, carried_ref, summed_ref, table_ref = ins
        grad, grad_low, grad_mixed, stats = outs
        total = scratch[0]
        for number, start in enumerate(range(0, weight.width, size)):
            fetch.need(0, number)
            part = back_dot(up_ref[:, start : start + size], fetch())
            if start == 0:
                fetch.need(1)
            total[...] = part + (ALPHA * carried_ref[...] if start == 0 else total[...])
        fetch.need(2)
        gain = table_ref[index : index + 1, :]
        stats[...] = jnp.zeros_like(stats)

        def step(block):
            normed, rate = normed_parts(summed_ref[block, :])
            upstream = total[block, :]
            values = norm_gradient(normed, rate, gain, upstream)
            grad[block, :] = values
            grad_low[block, :] = values.astype(BF16)
            add_stats(stats, normed, upstream)

        row_blocks(rows, 128, step)
        for which in (0, 1, 3):
            fetch.send(which)
        grad_mixed[...] = back_dot(grad_low[...], fetch()).astype(BF16)
        fetch.send(2)

    outs = [((rows, width), F32), ((rows, width), BF16), ((rows, width), BF16), ((16, width), F32)]
    return weight_call(
        order, name, bits, [weight, mix_weight],
        columns_plan(0, weight.width, size) + columns_plan(1, width, size),
        [cotangent, carried, summed, table], outs, [((rows, width), F32)], body,
        {0: size, 1: width, 2: width}, len(outs),
    )


def input_back(order, name, bits, weight, cotangents, carried, spans):
    rows, features = cotangents[0].shape[0], weight.features
    step = 512 if rows % 512 == 0 else rows // 2
    count = len(cotangents)
    streams = {which: size for which, _, _, size in spans}
    if carried is not None:
        streams[count] = carried.shape[1]

    def body(fetch, ins, outs, scratch):
        for number, (which, first, _, size) in enumerate(spans):
            chunk = fetch()
            fetch.need(which, first // size)
            if number == 0 and carried is not None:
                fetch.need(count)
            for row in range(0, rows, step):
                block = slice(row, row + step)
                part = back_dot(ins[which][block, first : first + size], chunk)
                if number == 0 and carried is not None:
                    part += ALPHA * ins[count][block, :]
                elif number > 0:
                    part += scratch[0][block, :]
                if number == len(spans) - 1:
                    outs[0][block, :] = part.astype(BF16)
                else:
                    scratch[0][block, :] = part

    return weight_call(
        order, name, bits, [weight], [(0, "columns", start, size) for _, _, start, size in spans],
        [*cotangents] + ([carried] if carried is not None else []),
        [((rows, features), BF16)], [((rows, features), F32)], body, streams,
    )[0]


def turn_rows(order, bits, sources, outer):
    features = sources[0].shape[1]
    total_rows = sum(source.shape[0] for source in sources)
    shard_rows = features // (8 * outer)

    def kernel(bits_ref, *refs):
        targets, filled = refs[len(sources) :], 0
        for ref in refs[: len(sources)]:
            stop = filled + ref.shape[0]
            for block in range(features // LANES):
                turned_block = ref[:, block * LANES : (block + 1) * LANES].T
                for part in range(LANES // shard_rows):
                    device = block * (LANES // shard_rows) + part
                    mem, core, near = device & 1, (device >> 1) & 1, (device >> 2) & 1
                    place = (mem ^ bits_ref[2]) * 2 + (near ^ bits_ref[0])
                    place = place * outer + (device >> 3)
                    rows = pl.ds(pl.multiple_of(place * shard_rows, shard_rows), shard_rows)
                    values = turned_block[part * shard_rows : (part + 1) * shard_rows]
                    side = core ^ bits_ref[1]

                    @pl.when(side == 0)
                    def _():
                        targets[0][rows, filled:stop] = values

                    @pl.when(side == 1)
                    def _():
                        targets[1][rows, filled:stop] = values

            filled = stop

    return order.launch(
        kernel,
        "turn_rows",
        [bits, *sources],
        [pl.BlockSpec(memory_space=pltpu.VMEM)] * len(sources),
        [pl.BlockSpec(memory_space=pltpu.VMEM)] * 2,
        [jax.ShapeDtypeStruct((features // 2, total_rows), BF16)] * 2,
        [],
        None,
        {},
    )


def weight_grad(
    order, bits, turned, cotangents, outer, cut, extra=None, held=None, place=None
):
    half_features = turned[0][0].shape[0]
    each, width = cotangents[0].shape
    n_turned = len(turned)
    n_grads = len(cotangents)
    total_rows = n_grads // 2 * each
    shard_rows = half_features // (4 * outer)
    parts = [width] + ([cut, width - cut] if place is None else [place[1], place[2]])
    chunk = 1024 if all(part % 1024 == 0 for part in parts) else 512
    added = 0 if extra is None else LANES
    n_held = 2 if held is not None else 0
    if place is None:
        halves = [(0, 0, cut // chunk, cut), (1, 0, (width - cut) // chunk, width - cut)]
    else:
        halves = [(place[0], place[1] // chunk, width // chunk, place[2])]
    steps = [count for _, _, count, _ in halves]
    first_steps = [sum(steps[:i]) for i in range(len(steps))]

    def kernel(bits_ref, *refs):
        n_in = n_turned + n_grads
        targets = refs[n_in + n_held + (len(halves) if added else 0) :]
        step = pl.program_id(0)
        features = jnp.concatenate([ref[...] for ref in refs[:n_turned]], axis=1)
        grads = jnp.concatenate([ref[...] for ref in refs[n_turned:n_in]], axis=0)
        product = plain_dot(features, grads)
        blocks = product.astype(BF16).reshape(2, 2, outer, shard_rows, chunk)
        for number, (half, _, count, _) in enumerate(halves):

            @pl.when((step >= first_steps[number]) & (step < first_steps[number] + count))
            def _():
                for side in range(2):
                    target = targets[2 * number + side]
                    picked = blocks[1 - side] if half == 0 else blocks[:, 1 - side]
                    target[..., :chunk] = picked
                    if added:
                        beside = refs[n_in + number]
                        picked = beside[1 - side] if half == 0 else beside[:, 1 - side]
                        target[..., chunk:] = picked

    def out_spec(number):
        _, first, count, _ = halves[number]
        at = lambda i, _: (0, 0, 0, first + jnp.clip(i - first_steps[number], 0, count - 1))
        return pl.BlockSpec((2, outer, shard_rows, chunk + added), at)

    def turned_spec(start, size):
        return pl.BlockSpec((half_features, size), lambda i, _: (0, start // size))

    whole = (2, 2, outer, shard_rows, LANES)
    specs = [turned_spec(start, size) for _, start, size in turned]
    specs += [pl.BlockSpec((each, chunk), lambda i, _: (0, i))] * n_grads
    specs += [pl.BlockSpec(memory_space=pltpu.HBM)] * n_held
    specs += [whole_spec(whole)] * (len(halves) if added else 0)
    return order.launch(
        kernel,
        "weight_grad",
        [bits, *(part for part, _, _ in turned), *cotangents, *(held or ()), *(extra or ())],
        specs,
        [out_spec(number) for number in range(len(halves)) for _ in range(2)],
        [
            jax.ShapeDtypeStruct((2, outer, shard_rows, columns + added), BF16)
            for _, _, _, columns in halves
            for _ in range(2)
        ],
        [],
        (sum(steps),),
        {1 + n_turned + n_grads: 0, 2 + n_turned + n_grads: 1} if n_held else {},
    )


def relative_rows(bits, values, outer):
    rows = values.shape[0] // (8 * outer)
    blocks = values.reshape(outer, 2, 2, 2, rows, -1)
    for axis, bit in ((1, bits[0]), (2, bits[1]), (3, bits[2])):
        blocks = jnp.where(bit == 1, jnp.flip(blocks, axis), blocks)
    blocks = blocks.transpose(2, 3, 1, 0, 4, 5)
    return blocks[0], blocks[1]


def add_blocks(order, bits, sums, shapes, apart=False):
    if apart:
        shapes = [shapes[0][1:]] * shapes[0][0]
    arrays = []
    for group, _, _ in sums:
        arrays += [a for a, _ in group if not any(a is b for b in arrays)]
    blocks = [group[0][0].shape[-3:] for group, _, _ in sums]
    find = lambda array: next(i for i, known in enumerate(arrays) if known is array)
    chunks = [(number, place) for place in range(blocks[0][0]) for number in range(len(sums))]

    def kernel(bits_ref, *refs):
        sources, refs = refs[: len(arrays)], refs[len(arrays) :]
        targets, refs = refs[: len(shapes)], refs[len(shapes) :]
        held, summed, (load_sems, store_sems) = refs[: len(sums)], refs[len(sums) : -2], refs[-2:]
        loads, stores = [], []
        for index, (number, place) in enumerate(chunks):
            loads.append([])
            block = place ^ bits_ref[3] if apart else place
            for term, (array, at) in enumerate(sums[number][0]):
                load = pltpu.make_async_copy(
                    sources[find(array)].at[(*at, block)],
                    held[number].at[term, place],
                    load_sems.at[index, term],
                )
                load.start()
                loads[-1].append(load)
        for index, (number, place) in enumerate(chunks):
            group, which, column = sums[number]
            for load in loads[index]:
                load.wait()
            values = [held[number][term, place].astype(F32) for term in range(len(group))]
            summed[number][place] = sum(values[1:], values[0]).astype(BF16)
            columns = pl.ds(column, blocks[number][2])
            goal = targets[place].at[:, columns] if apart else targets[which].at[place, :, columns]
            store = pltpu.make_async_copy(summed[number].at[place], goal, store_sems.at[index])
            store.start()
            stores.append(store)
        for store in stores:
            store.wait()

    most = max(len(group) for group, _, _ in sums)
    return order.launch(
        kernel,
        "add_blocks",
        [bits, *arrays],
        [pl.BlockSpec(memory_space=pltpu.HBM)] * len(arrays),
        [pl.BlockSpec(memory_space=pltpu.HBM)] * len(shapes),
        [jax.ShapeDtypeStruct(shape, BF16) for shape in shapes],
        [pltpu.VMEM((len(group), *block), BF16) for (group, _, _), block in zip(sums, blocks)]
        + [pltpu.VMEM(block, BF16) for block in blocks]
        + [
            pltpu.SemaphoreType.DMA((len(chunks), most)),
            pltpu.SemaphoreType.DMA((len(chunks),)),
        ],
        None,
        {},
    )


class Spread:
    def __init__(self, parts, kinds):
        self.kinds, self.kept = kinds, parts[1::2]
        self.once = [FIRST_BACK[kind](part) for part, kind in zip(parts[0::2], kinds)]

    def second(self):
        return [[(kept, (1,)), (once, (1,))] for kept, once in zip(self.kept, self.once)]

    def send(self, sent):
        self.twice = [SECOND_BACK[kind](part) for part, kind in zip(sent, self.kinds)]

    def third(self):
        return [
            [(kept, (0,)), (once, (0,)), (twice, ())]
            for kept, once, twice in zip(self.kept, self.once, self.twice)
        ]


def block_shape(group):
    return group[0][0].shape[-3:]


def spread_steps(order, bits, seconds, thirds, together=False):
    sums, shapes = [], []
    for wave in seconds:
        for group in wave.second():
            sums.append((group, len(shapes), 0))
            shapes.append(block_shape(group))
    joined = len(shapes)
    for number, wave in enumerate(thirds):
        if number == 0 or not together:
            shapes.append((*block_shape(wave.third()[0])[:2], 0))
        for group in wave.third():
            outer, rows, columns = shapes[-1]
            sums.append((group, len(shapes) - 1, columns))
            shapes[-1] = (outer, rows, columns + block_shape(group)[2])
    filled = add_blocks(order, bits, sums, shapes, together)
    start = 0
    for wave in seconds:
        wave.send(filled[start : start + len(wave.kinds)])
        start += len(wave.kinds)
    return filled[joined:]


def outer_sum(joined):
    joined = joined.reshape(-1, joined.shape[-1])
    return lax.psum_scatter(
        joined, "dp", axis_index_groups=outer_groups(), scatter_dimension=0, tiled=True
    )


def last_shards(order, bits, parts, summed, spans):
    rows, columns = parts[0].shape
    widths = [sum(size for _, _, size in span) for span in spans]

    def kernel(bits_ref, *refs):
        refs, summed_ref, targets = refs[: len(parts)], refs[len(parts)], refs[len(parts) + 1 :]
        total = refs[0][...].astype(F32)
        for ref in refs[1:]:
            total += ref[...].astype(F32)
        for target, span in zip(targets, spans):
            at = 0
            for wave, start, size in span:
                if wave == 0:
                    values = total[:, start : start + size]
                else:
                    values = summed_ref[:, start : start + size].astype(F32)
                target[:, at : at + size] = values
                at += size

    return order.launch(
        kernel,
        "last_shards",
        [bits, *parts, summed],
        [pl.BlockSpec(memory_space=pltpu.VMEM)] * (len(parts) + 1),
        [pl.BlockSpec(memory_space=pltpu.VMEM)] * len(spans),
        [jax.ShapeDtypeStruct((rows, width), F32) for width in widths],
        [],
        None,
        {},
    )


FIRST_BACK = (swap_mem, swap_next)
SECOND_BACK = (swap_next, swap_mem)


def per_device(
    target_in,
    memory_in,
    bucket_ids,
    target_lengths,
    memory_mask,
    self_qkv,
    self_out,
    cross_q,
    cross_kv,
    cross_out,
    ffn_in,
    ffn_out,
    norm_gains,
    norm_biases,
    grad_out,
):
    both = ("dp", "mem")
    row_count, model_width = target_in.shape
    shard_rows = self_qkv.shape[0]
    outer = lax.axis_size("dp") // 4
    staged = shard_rows % 16 == 0 and shard_rows <= LANES and model_width % LANES == 0
    bits = place_bits()
    order = Order()
    own_index, pieces = lax.axis_index("mem"), lax.axis_size("mem")
    slot_count, mem_piece = memory_in.shape[3], memory_in.shape[4]

    norm_shard = jnp.concatenate((norm_gains, norm_biases), axis=1)
    norm_columns = norm_shard.shape[1]
    norm_shard = jnp.pad(norm_shard, ((0, 0), (0, LANES - norm_columns)))

    groups = [
        (self_qkv,),
        (cross_q, cross_out, norm_shard, cross_kv, self_out),
        (ffn_in,),
        (ffn_out,),
    ]
    if staged:
        shards = list(cast_shards(order, bits, groups))
    else:
        shards = [jnp.concatenate([part.astype(BF16) for part in group], axis=1) for group in groups]

    def gather(index, windows, direct=False):
        shard = shards[index]
        widths = [part.shape[1] for part in groups[index]]
        starts = [sum(widths[:i]) for i in range(len(widths))]
        if staged:
            wave = Wave(shard, windows, direct)
            return [Weight(wave, at, size) for at, size in zip(starts, widths)]
        full = lax.all_gather(shard, both, axis=0, tiled=True)
        rows = full.shape[0] // 16
        return [
            Weight(None, 0, size, full[:, at : at + size].reshape(8, 2, rows, size))
            for at, size in zip(starts, widths)
        ]

    def whole_sum(gradient):
        return lax.psum_scatter(gradient, both, scatter_dimension=0, tiled=True).astype(F32)

    class Turned:
        def __init__(self, *sources, turned=()):
            self.sources = sources
            own, other = turned or (turn_rows(order, bits, sources, outer) if staged else (None, None))
            self.both = (own, swap_core(other)) if staged else ()

        def due(self):
            order.before(*self.both[1:])

    class Grad:
        def __init__(self, *places):
            self.sources = [source for _, *sources in places for source in sources]
            self.turned = []
            for side in range(2 if staged else 0):
                for turned, *sources in places:
                    start = 0
                    for other in turned.sources:
                        if other is sources[0]:
                            break
                        start += other.shape[0]
                    stop = start + sum(source.shape[0] for source in sources)
                    size = math.gcd(start, stop)
                    for at in range(start, stop, size):
                        self.turned.append((turned.both[side], at, size))

        def take(self, *cotangents):
            self.cotangents = cotangents
            if staged:
                self.cotangents += tuple(swap_core(part) for part in cotangents)

        def make(self, cut=None, **options):
            if staged:
                return weight_grad(
                    order, bits, self.turned, self.cotangents, outer, cut, **options
                )
            rows = [jnp.concatenate(part, axis=0) for part in (self.sources, self.cotangents)]
            return lead_dot(*rows).astype(BF16)

    def at_mem(values, index):
        return lax.dynamic_index_in_dim(values, index, 0, False)

    mem_rows = memory_in[0, :, 0]
    mem_live = memory_mask[0, :, 0]
    near_live = at_mem(mem_live, own_index)
    far_live = swap_mem(at_mem(mem_live, 1 - own_index))
    piece_shape = (mem_piece, model_width)
    if staged:
        moves = Moves(order, bits)
        source, near = moves.source(mem_rows), moves.target((slot_count, *piece_shape))
        sent = [moves.target(piece_shape) for _ in range(slot_count)]
        for slot in range(slot_count):
            at_far = lambda bits, slot=slot: (1 - bits[2], slot)
            at_near = lambda bits, slot=slot: (bits[2], slot)
            moves.move(source, at_far, piece_shape, (sent[slot], (slice(None),)))
            moves.move(source, at_near, piece_shape, (near, (slot,)))
        given = {}
        moves.then.append(lambda filled: given.update(near=filled[near], sent=[filled[t] for t in sent]))
        moves.run()
        near_rows, sent_rows = given["near"], given["sent"]
    else:
        near_rows = at_mem(mem_rows, own_index)
        sent_rows = [at_mem(mem_rows[:, slot], 1 - own_index) for slot in range(slot_count)]

    qkv_half = 3 * model_width // 2
    (w_qkv,) = gather(0, [(0, qkv_half, 0), (qkv_half, qkv_half, 1)], True)
    far_parts = [swap_mem(sent_rows[0])]
    if staged:
        order.before(far_parts[0], far_live)
        moves = Moves(order, bits)
        w_qkv.wave.first(moves)
        places = [moves.passed(shard) for shard in shards[1:]]
        moves.then.append(lambda filled: shards.__setitem__(slice(1, None), [filled[i] for i in places]))
        moves.run()
    lead = 2 * model_width + LANES
    w_cq, w_co, w_norm, w_ckv, w_so = gather(
        1, [(0, lead, 0), (lead, 5 * model_width + LANES - lead, 1)]
    )
    (w_in,) = gather(2, [(0, ffn_in.shape[1], 0)])
    (w_out,) = gather(3, [(0, model_width, 1)])

    bucket = pick_entry(bucket_ids[0], own_index)
    lengths = target_lengths[0, 0]
    self_meta = jnp.stack([jnp.right_shift(jnp.int32(row_count), bucket), lengths[0], lengths[1]])
    cross_meta = bucket[None]
    live = jnp.concatenate((near_live, far_live), axis=1)
    key_bias = jnp.where(live == 1, 0.0, NEG_LARGE).astype(F32)
    key_columns = jnp.broadcast_to(key_bias[:, :, None], (*key_bias.shape, LANES))
    near_flat = near_rows.reshape(-1, model_width)
    slotted = (slot_count, mem_piece, 2 * model_width)

    def steps(*wanted):
        if staged:
            moves = Moves(order, bits)
            for weight, name in wanted:
                getattr(weight.wave, name)(moves)
            moves.run()

    steps((w_qkv, "second"))
    order.part()
    first_turned = Turned(target_in, near_flat)
    steps((w_ckv, "first"))
    order.part()
    steps((w_qkv, "third"))
    first_turned.due()
    order.part()
    steps((w_ckv, "second"))
    (united,) = project(order, "self_project", bits, w_qkv, [target_in], 1024)
    far_parts += [swap_mem(part) for part in gate(order, bits, sent_rows[1:])]
    steps((w_in, "first"))
    order.before(key_columns)
    self_mixed, self_log = self_forward(order, self_meta, united)
    order.part()
    steps((w_ckv, "third"))
    order.before(*far_parts[1:])
    order.part()
    steps((w_out, "first"))
    middle = Turned(self_mixed, *far_parts)
    table = norm_table(order, bits, w_norm)
    near_kv, far_kv = project(
        order, "cross_project", bits, w_ckv, [near_flat, *far_parts], 1024, [1, len(far_parts)]
    )
    near_kv, far_kv = near_kv.reshape(slotted), far_kv.reshape(slotted)
    order.part()
    steps((w_in, "second"))
    order.part()
    steps((w_out, "second"))
    middle.due()
    sum_one, first_out, first_low, cross_query = mix_norm(
        order, "self_mix", bits, w_so, self_mixed, target_in, table, 0, w_cq
    )
    cross_mixed, cross_log = cross_forward(
        order, cross_meta, cross_query, near_kv, far_kv, key_bias[:, None, :]
    )
    sum_two, second_out, second_low = mix_norm(
        order, "cross_mix", bits, w_co, cross_mixed, first_out, table, 1
    )
    later = Turned(first_low, cross_mixed, second_low)
    order.part()
    steps((w_in, "third"))
    steps((w_out, "third"))
    activated, slope, *turned = feed_in(order, bits, w_in, second_low, outer if staged else 0)
    later.due()
    hidden = Turned(activated, turned=turned)
    layer_out, grad_three, grad_ffn, stats_three = feed_out(
        order, bits, w_out, activated, second_out, table, grad_out
    )
    qkv_grad = Grad((first_turned, target_in))
    so_grad = Grad((middle, self_mixed))
    ckv_grad = Grad((first_turned, near_flat), (middle, *far_parts))
    cq_grad = Grad((later, first_low))
    co_grad = Grad((later, cross_mixed))
    in_grad = Grad((later, second_low))
    out_grad = Grad((hidden, activated))

    shards = {}

    def spread(name, parts, kinds):
        if staged:
            return Spread(parts, kinds)
        shards[name] = whole_sum(parts)
        return None

    def advance(seconds=(), thirds=()):
        if staged:
            waves = [wave for _, wave in thirds]
            joined = spread_steps(order, bits, seconds, waves)
            for (name, _), part in zip(thirds, joined):
                shards[name] = outer_sum(part)

    out_grad.take(grad_ffn)
    out_wave = spread("out", out_grad.make(model_width // 2), (0, 1))
    grad_hidden = feed_back(order, bits, w_out, grad_ffn, slope)
    in_grad.take(grad_hidden)
    grad_two, grad_cross_out, grad_cross_mixed, stats_two = norm_back(
        order, "cross_back", bits, w_in, grad_hidden, grad_three, sum_two, table, 1, w_co
    )
    co_grad.take(grad_cross_out)
    order.part()
    advance([out_wave])
    in_wave = spread("in", in_grad.make(2 * model_width), (0, 1))
    pair_width = 2 * model_width
    near_parts = co_grad.make(place=(0, 0, pair_width))
    grad_query_low, grad_near_kv, grad_far_kv = cross_backward(
        order,
        cross_meta,
        cross_query,
        near_kv,
        far_kv,
        key_columns,
        cross_mixed,
        grad_cross_mixed,
        cross_log,
    )
    cq_grad.take(grad_query_low)
    ckv_grad.take(grad_near_kv, grad_far_kv)
    order.part()
    advance([in_wave], [("out", out_wave)])

    def memory_back(cotangent):
        spans = [(0, start, start, model_width) for start in (0, model_width)]
        return input_back(order, "memory_back", bits, w_ckv, [cotangent], None, spans)

    grad_one, grad_self_out, grad_self_mixed, stats_one = norm_back(
        order, "self_back", bits, w_cq, grad_query_low, grad_two, sum_one, table, 0, w_so
    )
    so_grad.take(grad_self_out)
    stats = [jnp.sum(s.reshape(2, 8, model_width), axis=1) for s in (stats_one, stats_two, stats_three)]
    norm_grads = [
        jnp.pad(jnp.stack([s[i] for s in stats], axis=1), ((0, 0), (0, LANES - len(stats))))
        for i in range(2)
    ]
    norm_grads = jnp.concatenate(norm_grads, axis=1).astype(BF16)
    if staged:
        own, other = relative_rows(bits, norm_grads, outer)
        own = (own.astype(F32) + swap_core(other).astype(F32)).astype(BF16)
        norm_grads = (own[..., :LANES], own[..., LANES:])
        far_parts = ckv_grad.make(place=(1, 0, pair_width))
        near_parts = cq_grad.make(place=(0, model_width, pair_width), held=near_parts)
        mid_parts = [*near_parts, *far_parts]
    else:
        mid_parts = jnp.concatenate([near_parts, cq_grad.make(), ckv_grad.make()], axis=1)
    mid_wave = spread("mid", mid_parts, (0, 1))
    order.part()
    advance([], [("in", in_wave)])
    grad_united = self_backward(
        order,
        self_meta,
        united,
        self_mixed,
        grad_self_mixed,
        self_log,
    )
    qkv_grad.take(grad_united)
    half_width = model_width // 2
    if staged:
        so_wave = spread("so", so_grad.make(half_width, extra=norm_grads), (0, 1))
    else:
        part = so_grad.make()
        columns = [part[:, :half_width], norm_grads[:, :LANES], part[:, half_width:], norm_grads[:, LANES:]]
        so_wave = spread("so", jnp.concatenate(columns, axis=1), (0, 1))
    order.part()
    advance([mid_wave])
    qkv_wave = spread("qkv", qkv_grad.make(qkv_half), (0, 1))
    if staged:
        order.before(shards["out"], shards["in"])
        order.part()
        advance([], [("mid", mid_wave)])
    split = half_width + LANES
    grad_far = memory_back(grad_far_kv)
    if staged:
        order.part()
        advance([qkv_wave, so_wave])
        (grad_far,) = gate(order, bits, [grad_far])
    grad_far = swap_mem(grad_far)
    if staged:
        order.before(shards["mid"])
        order.part()
        blocks = spread_steps(order, bits, [], [so_wave, qkv_wave], True)
        blocks = [blocks[0]] + [swap_outer(blocks[far], far) for far in range(1, outer)]
    grad_near = memory_back(grad_near_kv)
    target_grad = input_back(
        order,
        "target_back",
        bits,
        w_qkv,
        [grad_united],
        grad_one,
        [(0, start, start, model_width) for start in range(0, w_qkv.width, model_width)],
    )
    so_spans = [(0, 0, half_width), (0, split, half_width)]
    norm_spans = [[(0, half_width, 3)], [(0, split + half_width, 3)]]
    mid_spans = [[(1, i * model_width, model_width)] for i in range(2)]
    mid_spans.append([(1, 2 * model_width, 2 * model_width)])
    spans = [[(0, 2 * split, 2 * qkv_half)], so_spans, *norm_spans, *mid_spans]
    if staged:
        last = last_shards(order, bits, blocks, shards["mid"], spans)
        moves = Moves(order, bits)
        target = moves.target((2, *near_flat.shape))
        for number, part in enumerate((grad_near, grad_far)):
            place = lambda bits, number=number: (bits[2] ^ number,)
            moves.move(moves.source(part), (slice(None),), near_flat.shape, (target, place))
        moves.then.append(lambda filled: shards.update(memory=filled[target]))
        moves.run()
        grad_pair = shards["memory"]
    else:
        grad_pair = jnp.stack((grad_near, grad_far))
        grad_pair = jnp.where(own_index == 0, grad_pair, grad_pair[::-1])
        sources = (jnp.concatenate((shards["so"], shards["qkv"]), axis=1), shards["mid"])
        last = [
            jnp.concatenate([sources[w][:, at : at + size] for w, at, size in span], axis=1)
            for span in spans
        ]
    qkv_shard, so_shard, gains, biases, co_shard, cq_shard, ckv_shard = last

    return (
        layer_out,
        target_grad,
        grad_pair.reshape(1, pieces, 1, *near_rows.shape),
        qkv_shard,
        so_shard,
        cq_shard,
        ckv_shard,
        co_shard,
        shards["in"].astype(F32),
        shards["out"].astype(F32),
        gains,
        biases,
    )


def solution(mesh):
    rows = P(("dp", "mem"), None)
    memory = P("dp", None, "mem", None, None, None)
    return jax.shard_map(
        per_device,
        mesh=mesh,
        in_specs=(
            rows,
            memory,
            P("dp", None),
            P("dp", "mem", None),
            P("dp", None, "mem", None, None),
        )
        + (rows,) * 10,
        out_specs=(rows, rows, memory) + (rows,) * 9,
        check_vma=False,
    )
```
